32 devices in a mesh: row: 4 (over z), dp: 4 (over y, x), mp: 2 (over core).
Axes of the slice: x: 2, y: 2, z: 4, core: 2. Of those that a mesh axis runs over, the one named last changes fastest.
Arguments:
- tokens: bfloat16 [16384, 640], P(('row', 'dp')), may hold values from -6 to 6
- encoder: bfloat16 [4, 16384, 640], P('row', 'dp'), may hold values from -6 to 6
- layer_pick: int32 [4, 4], replicated, may hold values from 0 to 1, as said below
- piece_heads: int32 [4], replicated, may hold values from 2 to 8, as said below
- piece_ffn: int32 [4], replicated, may hold values from 1024 to 3072, as said below
- tgt_len: int32 [64], P(('row', 'dp')), may hold values from 128 to 256, as said below
- src_len: int32 [64], P(('row', 'dp')), may hold values from 128 to 256, as said below
- norm_gain: float32 [3, 640], replicated, may hold values from 0.1 to 1.9
- norm_shift: float32 [3, 640], replicated, may hold values from -4 to 4
- out_bias: float32 [3, 640], replicated, may hold values from -4 to 4
- w_self: bfloat16 [3, 640, 640], P(None, None, 'mp'), may hold values from -0.3125 to 0.3125
- o_self: bfloat16 [640, 640], P('mp'), may hold values from -0.625 to 0.625
- b_self: float32 [2, 640], P(None, 'mp'), may hold values from -6 to 6
- w_cross: bfloat16 [3, 640, 640], P(None, None, 'mp'), may hold values from -0.3125 to 0.3125
- o_cross: bfloat16 [640, 640], P('mp'), may hold values from -0.625 to 0.625
- b_cross: float32 [2, 640], P(None, 'mp'), may hold values from -6 to 6
- w_up: bfloat16 [640, 3072], P(None, 'mp'), may hold values from -0.25 to 0.25
- b_up: float32 [3072], P('mp'), may hold values from -6 to 6
- w_down: bfloat16 [3072, 640], P('mp'), may hold values from -0.15625 to 0.15625
- cotangent: bfloat16 [16384, 640], P(('row', 'dp')), may hold values from -6 to 6
Outputs:
- block_out: float32 [16384, 640], P(('row', 'dp'))
- grad_tokens: float32 [16384, 640], P(('row', 'dp'))
- grad_encoder: float32 [4, 16384, 640], P('row', 'dp')
- grad_norm_gain: float32 [3, 640], P(None, ('row', 'dp'))
- grad_norm_shift: float32 [3, 640], P(None, ('row', 'dp'))
- grad_out_bias: float32 [3, 640], P(None, ('row', 'dp'))
- grad_w_self: float32 [3, 640, 640], P(None, ('row', 'dp'), 'mp')
- grad_o_self: float32 [640, 640], P('mp', ('row', 'dp'))
- grad_b_self: float32 [2, 640], P(None, 'mp')
- grad_w_cross: float32 [3, 640, 640], P(None, ('row', 'dp'), 'mp')
- grad_o_cross: float32 [640, 640], P('mp', ('row', 'dp'))
- grad_b_cross: float32 [2, 640], P(None, 'mp')
- grad_w_up: float32 [640, 3072], P(('row', 'dp'), 'mp')
- grad_b_up: float32 [3072], P('mp')
- grad_w_down: float32 [3072, 640], P('mp', ('row', 'dp'))
The draws below stay inside these ranges and needn't reach their ends.
Inputs may be any that keep to these rules, and one draw needn't show every extreme that they name: `layer_pick`: each piece chooses 1 to 3 of the 4 layers (1 marks a chosen one); some piece chooses 3 and another 1. `piece_heads`: a piece uses heads 0 to this count - 1 in both attentions; some piece uses all 8. `piece_ffn`: a multiple of 1024; a piece uses units 0 to this - 1; some piece uses all 3072. `tgt_len`: among each aligned block of 4 sentences one has 256. `src_len`: among each aligned block of 4 sentences one has 256.
All inputs are finite; a program needn't handle non-finite values.
Results may differ from the reference program's by a relative error of at most 0.028.
The reference program's roundings to bfloat16 on the way count: a program that leaves them out, or rounds other values in their place, can miss the bound.
Values may be sent and summed in bfloat16 or wider, within the bound.
A program may use at most 192 MiB of HBM per device.

```python
import jax
import jax.numpy as jnp
from jax import lax

D = 640
HEADS = 8
HD = 80
FF = 3072
SEQ_DEV = 4
TGT_LEN = 256
SRC_LEN = 256
ENC_LAYERS = 4
PIECES = 4
SEQS = 64
TOKENS = 16384
SOURCES = 16384
N_ROW = 4
N_DP = 4


def draw_layer_pick(key, part):
    key = jax.random.fold_in(key, 11)
    key_count, key_full, key_single, key_order = jax.random.split(key, 4)
    counts = jax.random.randint(key_count, (PIECES,), 1, 4)
    full_piece = jax.random.randint(key_full, (), 0, PIECES)
    single_piece = (full_piece + 1 + jax.random.randint(key_single, (), 0, PIECES - 1)) % PIECES
    piece_ids = jnp.arange(PIECES)
    counts = jnp.where(piece_ids == full_piece, 3, jnp.where(piece_ids == single_piece, 1, counts))
    layer_rank = jax.vmap(lambda sub_key: jax.random.permutation(sub_key, ENC_LAYERS))(jax.random.split(key_order, PIECES))
    return (layer_rank < counts[:, None]).astype(jnp.int32)


def draw_piece_heads(key, part):
    key = jax.random.fold_in(key, 12)
    key_draw, key_full = jax.random.split(key)
    counts = jax.random.randint(key_draw, (PIECES,), 2, HEADS + 1)
    full_piece = jax.random.randint(key_full, (), 0, PIECES)
    return jnp.where(jnp.arange(PIECES) == full_piece, HEADS, counts).astype(jnp.int32)


def draw_piece_ffn(key, part):
    key = jax.random.fold_in(key, 13)
    key_draw, key_full = jax.random.split(key)
    levels = jax.random.randint(key_draw, (PIECES,), 1, 4)
    full_piece = jax.random.randint(key_full, (), 0, PIECES)
    levels = jnp.where(jnp.arange(PIECES) == full_piece, 3, levels)
    return (levels * (FF // 3)).astype(jnp.int32)


def ragged_lengths(key, longest):
    key_draw, key_full = jax.random.split(key)
    lengths = jax.random.randint(key_draw, (SEQS,), longest // 2, longest + 1)
    full_slot = jax.random.randint(key_full, (SEQS // SEQ_DEV, 1), 0, SEQ_DEV)
    is_full = jnp.arange(SEQ_DEV)[None, :] == full_slot
    return jnp.where(is_full, longest, lengths.reshape(SEQS // SEQ_DEV, SEQ_DEV)).reshape(SEQS).astype(jnp.int32)


def draw_tgt_len(key, part):
    key = jax.random.fold_in(key, 14)
    return ragged_lengths(key, TGT_LEN)


def draw_src_len(key, part):
    key = jax.random.fold_in(key, 15)
    return ragged_lengths(key, SRC_LEN)


def steps_of(own_key, shape, cuts, smallest, largest):
    loudness = 1.0
    for dim, shards_of in cuts:
        heights = jax.random.uniform(jax.random.fold_in(jax.random.fold_in(own_key, 6), dim), (shards_of,), jnp.float32, smallest / len(cuts), largest / len(cuts))
        loudness = loudness * jnp.repeat(jnp.exp(heights), shape[dim] // shards_of).reshape((-1,) + (1,) * (len(shape) - 1 - dim))
    return loudness


def scatter_about(rng, shape, width, reach, cuts=(), dtype=jnp.bfloat16):
    drawn = jax.random.normal(rng, shape, jnp.float32) * width
    if len(cuts) > 0:
        drawn = steps_of(rng, shape, cuts, -0.22, 0.18) * drawn
    return jnp.clip(drawn, min=-reach, max=reach).astype(dtype)


def setup_inputs(seed: int = 0) -> dict:
    seeds = jax.random.split(jax.random.key(seed), 21)
    return {
        "tokens": scatter_about(seeds[0], (TOKENS, D), 1.0, 6.0, ((0, 16),)),
        "encoder": scatter_about(seeds[1], (ENC_LAYERS, SOURCES, D), 1.0, 6.0, ((0, 4), (1, 4))),
        "layer_pick": draw_layer_pick(jax.random.fold_in(seeds[20], 71), 0),
        "piece_heads": draw_piece_heads(jax.random.fold_in(seeds[20], 71), 0),
        "piece_ffn": draw_piece_ffn(jax.random.fold_in(seeds[20], 71), 0),
        "tgt_len": draw_tgt_len(jax.random.fold_in(seeds[20], 71), 0),
        "src_len": draw_src_len(jax.random.fold_in(seeds[20], 71), 0),
        "norm_gain": jnp.clip(1.0 + 0.18 * jax.random.normal(seeds[7], (3, D), jnp.float32), 0.1, 1.9),
        "norm_shift": scatter_about(seeds[8], (3, D), 0.3, 4.0, (), jnp.float32),
        "out_bias": scatter_about(seeds[9], (3, D), 0.3, 4.0, (), jnp.float32),
        "w_self": scatter_about(seeds[10], (3, D, D), (D // 2) ** -0.5, 0.3125, ((2, 2),)),
        "o_self": scatter_about(seeds[11], (D, D), (D // 8) ** -0.5, 0.625, ((0, 2),)),
        "b_self": scatter_about(seeds[12], (2, D), 0.5, 6.0, ((1, 2),), jnp.float32),
        "w_cross": scatter_about(seeds[13], (3, D, D), (D // 2) ** -0.5, 0.3125, ((2, 2),)),
        "o_cross": scatter_about(seeds[14], (D, D), (D // 8) ** -0.5, 0.625, ((0, 2),)),
        "b_cross": scatter_about(seeds[15], (2, D), 0.5, 6.0, ((1, 2),), jnp.float32),
        "w_up": scatter_about(seeds[16], (D, FF), D ** -0.5, 0.25, ((1, 2),)),
        "b_up": scatter_about(seeds[17], (FF,), 0.5, 6.0, ((0, 2),), jnp.float32),
        "w_down": scatter_about(seeds[18], (FF, D), (FF // 2) ** -0.5, 0.15625, ((0, 2),)),
        "cotangent": scatter_about(seeds[19], (TOKENS, D), 1.0, 6.0, ((0, 16),)),
    }


EPSILON = 1e-05
MASKED = -1e+30
HIGHEST = lax.Precision.HIGHEST

@jax.custom_vjp
def low(v):
    return lax.optimization_barrier(v.astype(jnp.bfloat16)).astype(jnp.float32)

@jax.custom_vjp
def low_back(v):
    return v

def low_keep(v):
    return (low(v), None)

def low_pass(kept, grad):
    return (grad,)

def back_keep(v):
    return (v, None)

def back_low(kept, grad):
    return (low(grad),)
low.defvjp(low_keep, low_pass)
low_back.defvjp(back_keep, back_low)

def matmul(left, right):
    return jnp.dot(left, right, precision=HIGHEST, preferred_element_type=jnp.float32)

def layer_norm(stream, gain, shift):
    centre = stream - lax.optimization_barrier(jnp.mean(stream, axis=-1, keepdims=True))
    spread = lax.optimization_barrier(jnp.mean(centre * centre, axis=-1, keepdims=True))
    return centre * lax.rsqrt(spread + EPSILON) * gain + shift

def attend(queries, keys_in, values, key_mask, head_mask):
    query_shape = queries.shape
    query_low = low(queries).reshape(query_shape[0], query_shape[1], HEADS, HD)
    key_low = low(keys_in).reshape(keys_in.shape[0], keys_in.shape[1], HEADS, HD)
    value_low = low(values).reshape(values.shape[0], values.shape[1], HEADS, HD)
    raw_scores = low_back(jnp.einsum('gqhd,gkhd->ghqk', query_low, key_low, precision=HIGHEST))
    scores = jnp.where(key_mask[:, None], raw_scores * HD ** (-0.5), MASKED)
    soft_probs = jax.nn.softmax(scores, axis=-1)
    mixed_heads = low_back(jnp.einsum('ghqk,gkhd->gqhd', low(soft_probs), value_low, precision=HIGHEST))
    mixed_heads = mixed_heads * head_mask[:, None, :, None]
    return low(mixed_heads.reshape(query_shape))

def decoder_layer(stream_in, enc_layers, seq_pick, head_mask, unit_mask, target_len, source_len, params):
    norm_gain, norm_shift, out_bias, w_self, o_self, b_self, w_cross, o_cross, b_cross, w_up, b_up, w_down = params
    positions = jnp.arange(TGT_LEN)
    self_mask = (positions[None, :, None] >= positions[None, None, :]) & (positions[None, None, :] < target_len[:, None, None])
    source_ok = jnp.arange(SRC_LEN)[None, None, :] < source_len[:, None, None]
    cross_mask = jnp.broadcast_to(source_ok, (stream_in.shape[0], TGT_LEN, SRC_LEN))
    normed_one = low(layer_norm(stream_in, norm_gain[0], norm_shift[0]))
    query_one = low_back(matmul(normed_one, w_self[0]) + b_self[0])
    key_one = low_back(matmul(normed_one, w_self[1]))
    value_one = low_back(matmul(normed_one, w_self[2]) + b_self[1])
    attn_one = attend(query_one, key_one, value_one, self_mask, head_mask)
    stream_mid = stream_in + low_back(matmul(attn_one, o_self) + out_bias[0])
    normed_two = low(layer_norm(stream_mid, norm_gain[1], norm_shift[1]))
    memory = low(jnp.einsum('gl,lgsd->gsd', seq_pick, enc_layers, precision=HIGHEST))
    query_two = low_back(matmul(normed_two, w_cross[0]) + b_cross[0])
    key_two = low_back(matmul(memory, w_cross[1]))
    value_two = low_back(matmul(memory, w_cross[2]) + b_cross[1])
    attn_two = attend(query_two, key_two, value_two, cross_mask, head_mask)
    stream_late = stream_mid + low_back(matmul(attn_two, o_cross) + out_bias[1])
    normed_three = low(layer_norm(stream_late, norm_gain[2], norm_shift[2]))
    hidden = low_back(matmul(normed_three, w_up) + b_up)
    active = low(jax.nn.gelu(hidden) * unit_mask[:, None, :])
    return stream_late + low_back(matmul(active, w_down) + out_bias[2])

def reference(tokens, encoder, layer_pick, piece_heads, piece_ffn, tgt_len, src_len, norm_gain, norm_shift, out_bias, w_self, o_self, b_self, w_cross, o_cross, b_cross, w_up, b_up, w_down, cotangent):
    chosen = layer_pick.astype(jnp.float32)
    layer_weight = chosen / lax.optimization_barrier(jnp.sum(chosen, axis=1, keepdims=True))
    piece_of = (jnp.arange(SEQS) // (SEQS // PIECES)).astype(jnp.int32)
    group_count = SEQS // SEQ_DEV
    seq_pick = layer_weight[piece_of].reshape(group_count, SEQ_DEV, ENC_LAYERS)
    head_mask = (jnp.arange(HEADS)[None, :] < piece_heads[piece_of][:, None]).astype(jnp.float32)
    unit_mask = (jnp.arange(FF)[None, :] < piece_ffn[piece_of][:, None]).astype(jnp.float32)
    head_mask = head_mask.reshape(group_count, SEQ_DEV, HEADS)
    unit_mask = unit_mask.reshape(group_count, SEQ_DEV, FF)
    stream_groups = tokens.reshape(group_count, SEQ_DEV, TGT_LEN, D)
    cot_groups = cotangent.reshape(group_count, SEQ_DEV, TGT_LEN, D)
    enc_groups = encoder.reshape(ENC_LAYERS, N_DP, N_ROW, SEQ_DEV, SRC_LEN, D)
    enc_groups = enc_groups.transpose(0, 2, 1, 3, 4, 5).reshape(ENC_LAYERS, group_count, SEQ_DEV, SRC_LEN, D)
    enc_groups = jnp.moveaxis(enc_groups, 1, 0)
    target_groups = tgt_len.reshape(group_count, SEQ_DEV)
    source_groups = src_len.reshape(group_count, SEQ_DEV)
    params = tuple((value.astype(jnp.float32) for value in (norm_gain, norm_shift, out_bias, w_self, o_self, b_self, w_cross, o_cross, b_cross, w_up, b_up, w_down)))

    def group_step(running, item):
        stream_part, enc_part, pick_part, head_part, unit_part, target_part, source_part, cot_part = item

        def forward(stream_in, enc_layers, weights_in):
            return decoder_layer(stream_in, enc_layers, pick_part, head_part, unit_part, target_part, source_part, weights_in)
        result, pullback = jax.vjp(forward, stream_part.astype(jnp.float32), enc_part.astype(jnp.float32), params)
        grad_stream, grad_enc, grad_params = pullback(cot_part.astype(jnp.float32))
        running = jax.tree.map(jnp.add, running, grad_params)
        return (running, (result, grad_stream, grad_enc))
    start = jax.tree.map(jnp.zeros_like, params)
    totals, outputs = lax.scan(group_step, start, (stream_groups, enc_groups, seq_pick, head_mask, unit_mask, target_groups, source_groups, cot_groups))
    block_out = outputs[0].reshape(TOKENS, D)
    grad_tokens = outputs[1].reshape(TOKENS, D)
    grad_encoder = jnp.moveaxis(outputs[2], 0, 1).reshape(ENC_LAYERS, N_ROW, N_DP, SEQ_DEV, SRC_LEN, D)
    grad_encoder = grad_encoder.transpose(0, 2, 1, 3, 4, 5).reshape(ENC_LAYERS, SOURCES, D)
    return (block_out, grad_tokens, grad_encoder, totals[0], totals[1], totals[2], totals[3], totals[4], totals[5], totals[6], totals[7], totals[8], totals[9], totals[10], totals[11])
```

```python
import functools
import jax
import jax.numpy as jnp
from jax import lax
from jax.experimental import pallas as pl
from jax.experimental.pallas import tpu as pltpu
from jax.sharding import PartitionSpec as P

HD = 80
EPSILON = 1e-05
MASKED = -1e30
F32, BF16 = jnp.float32, jnp.bfloat16
MESH = pl.DeviceIdType.MESH
ANY = pl.BlockSpec(memory_space=pl.ANY)
VMEM = pl.BlockSpec(memory_space=pltpu.VMEM)


def nn(a, b):
    return lax.dot_general(a, b, (((1,), (0,)), ((), ())), preferred_element_type=F32)


def nt(a, b):
    return lax.dot_general(a, b, (((1,), (1,)), ((), ())), preferred_element_type=F32)


def tn(a, b):
    return lax.dot_general(a, b, (((0,), (0,)), ((), ())), preferred_element_type=F32)


def lanes(i, n):
    return pl.ds(pl.multiple_of(i * n, n), n)


def layer_norm(v_ref, x_ref, gain, shift):
    @pl.loop(0, v_ref.shape[1] // 128)
    def _(i):
        v = v_ref[:, lanes(i, 128)].astype(F32)
        c = v - jnp.mean(v, axis=0, keepdims=True)
        r = lax.rsqrt(jnp.mean(c * c, axis=0, keepdims=True) + EPSILON)
        x_ref[:, lanes(i, 128)] = (c * r * gain + shift).astype(BF16)


def norm_back(v_ref, gain, up_ref, base_ref, out_ref, low_ref, gain_sum, shift_sum, bias_sum):
    for ref in (gain_sum, shift_sum, bias_sum):
        if ref is not None:
            ref[...] = jnp.zeros_like(ref)

    @pl.loop(0, v_ref.shape[1] // 128)
    def _(i):
        at = lanes(i, 128)
        v = v_ref[:, at].astype(F32)
        c = v - jnp.mean(v, axis=0, keepdims=True)
        r = lax.rsqrt(jnp.mean(c * c, axis=0, keepdims=True) + EPSILON)
        xhat = c * r
        e = up_ref[:, at]
        gain_sum[...] += e * xhat
        shift_sum[...] += e
        eg = e * gain
        m1 = jnp.mean(eg, axis=0, keepdims=True)
        m2 = jnp.mean(eg * xhat, axis=0, keepdims=True)
        out = base_ref[:, at].astype(F32) + r * (eg - m1 - xhat * m2)
        out_ref[:, at] = out
        if low_ref is not None:
            low = out.astype(BF16)
            low_ref[:, at] = low
            bias_sum[...] += low.astype(F32)


def attend(q_ref, k_ref, v_ref, out_ref, out_row, prob_ref, masks, head_on, hd, heads):
    groups, slots = len(out_row), masks[0].shape[1]
    per = heads // groups
    for g in range(groups):

        @pl.loop(0, per)
        def _(h, g=g):
            rows = pl.ds(pl.multiple_of((g * per + h) * hd, 16), hd)
            to = pl.ds(pl.multiple_of(out_row[g] + h * hd, 16), hd)
            for s, mask in enumerate(masks):
                at = slice(s * slots, (s + 1) * slots)
                scores = tn(k_ref[rows, at], q_ref[rows, at]) * hd ** (-0.5)
                scores = jnp.where(mask, scores, MASKED)
                e = jnp.exp(scores - jnp.max(scores, axis=0, keepdims=True))
                total = jnp.sum(e, axis=0, keepdims=True)
                p = (e / total).astype(BF16)
                prob_ref[(g * per + h) * len(masks) + s] = p
                mixed = nn(v_ref[rows, at], p) * head_on[g * per + h]
                out_ref[g, to, at] = mixed.astype(BF16)


def attend_back(q_ref, k_ref, v_ref, e_ref, prob_ref, d_ref, at_rows, hd, heads, sents):
    groups = d_ref.shape[0]
    per, slots = heads // groups, q_ref.shape[1] // sents
    for g in range(groups):

        @pl.loop(0, per)
        def _(h, g=g):
            rows = pl.ds(pl.multiple_of((g * per + h) * hd, 16), hd)
            dq_at, dk_at, dv_at = [
                pl.ds(pl.multiple_of(first + h * hd, 16), hd) for first in at_rows
            ]
            for s in range(sents):
                at = slice(s * slots, (s + 1) * slots)
                e, p = e_ref[rows, at], prob_ref[(g * per + h) * sents + s]
                d_ref[g, dv_at, at] = nt(e, p).astype(BF16)
                dp = tn(v_ref[rows, at], e)
                pf = p.astype(F32)
                delta = jnp.sum(pf * dp, axis=0, keepdims=True)
                ds = (pf * (dp - delta) * hd ** (-0.5)).astype(BF16)
                d_ref[g, dq_at, at] = nn(k_ref[rows, at], ds).astype(BF16)
                d_ref[g, dk_at, at] = nt(q_ref[rows, at], ds).astype(BF16)


def lane_sum(values):
    return jnp.sum(values.astype(F32), axis=1, keepdims=True)


def compute_kernel(
    hd, lw, head_on, ints, tok, cot, enc, ws, os_, wc, oc, wu, wd, cols, bcols, bup,
    block, gtok, gmem, gs, gx, gu, gd, small,
    tok_t, mid_t, late_t, acc_a, acc_b, x1, x2, x3, ct, mem_t, e_low,
    q1, k1, v1, q2, k2, v2, attn1, attn2, prob1, prob2, grads, eh, sum_a, sum_b, sum_c, vec, bvec, ubias,
    wu_buf, wd_buf, gu_buf, gd_buf, in_sem, out_sem,
):
    width, tokens = tok_t.shape
    groups, hw = ws.shape[0], ws.shape[3]
    heads, units = groups * hw // hd, wu.shape[2]
    sents = ints.shape[0] - 1 >> 1
    slots = tokens // sents
    pad = -(-3 * hw // 128) * 128
    lead = 3 * hw // 128 * 128
    first = 3 * hw - lead
    gain = [cols[:, i : i + 1] for i in range(3)]
    shift = [cols[:, 3 + i : 4 + i] for i in range(3)]
    obias = [cols[:, 6 + i : 7 + i] for i in range(3)]
    key_at = lax.broadcasted_iota(jnp.int32, (slots, slots), 0)
    query_at = lax.broadcasted_iota(jnp.int32, (slots, slots), 1)
    for ref in (attn1, attn2):
        ref[:, :first, :] = jnp.zeros((groups, first, tokens), BF16)
    grads[:, 3 * hw :, :] = jnp.zeros((groups, pad - 3 * hw, tokens), BF16)

    vec[...] = jnp.zeros_like(vec)
    bvec[...] = jnp.zeros_like(bvec)

    tok_t[...] = tok[...].astype(F32).T.astype(BF16)
    layer_norm(tok_t, x1, gain[0], shift[0])
    for g in range(groups):
        rows = slice(g * hw, (g + 1) * hw)
        q1[rows] = (tn(ws[g, 0], x1[...]) + bcols[g, :, 0:1]).astype(BF16)
        k1[rows] = tn(ws[g, 1], x1[...]).astype(BF16)
        v1[rows] = (tn(ws[g, 2], x1[...]) + bcols[g, :, 1:2]).astype(BF16)
    masks = [(key_at <= query_at) & (key_at < ints[1 + s]) for s in range(sents)]
    attend(q1, k1, v1, attn1, [first] * groups, prob1, masks, head_on, hd, heads)
    acc_a[...] = tn(os_[0], attn1[0, first:])
    for g in range(1, groups):
        acc_a[...] += tn(os_[g], attn1[g, first:])
    mid_t[...] = tok_t[...].astype(F32) + acc_a[...] + obias[0]

    memory = lw[0] * enc[0].astype(F32)
    for i in range(1, enc.shape[0]):
        memory += lw[i] * enc[i].astype(F32)
    mem_t[...] = memory.T.astype(BF16)
    layer_norm(mid_t, x2, gain[1], shift[1])
    for g in range(groups):
        rows = slice(g * hw, (g + 1) * hw)
        q2[rows] = (tn(wc[g, 0], x2[...]) + bcols[g, :, 2:3]).astype(BF16)
        k2[rows] = tn(wc[g, 1], mem_t[...]).astype(BF16)
        v2[rows] = (tn(wc[g, 2], mem_t[...]) + bcols[g, :, 3:4]).astype(BF16)
    masks = [key_at < ints[1 + sents + s] for s in range(sents)]
    attend(q2, k2, v2, attn2, [first] * groups, prob2, masks, head_on, hd, heads)
    acc_a[...] = tn(oc[0], attn2[0, first:])
    for g in range(1, groups):
        acc_a[...] += tn(oc[g], attn2[g, first:])
    late_t[...] = mid_t[...] + acc_a[...] + obias[1]

    layer_norm(late_t, x3, gain[2], shift[2])
    ct[...] = cot[...].astype(F32).T.astype(BF16)
    acc_a[...] = jnp.zeros_like(acc_a)
    acc_b[...] = jnp.zeros_like(acc_b)
    ubias[...] = jnp.zeros_like(ubias)
    ublk = bup.shape[1]
    blocks = units // ublk

    def fetches(i):
        slot, g, at = lax.rem(i, 2), i // blocks, lanes(lax.rem(i, blocks), ublk)
        return [
            pltpu.make_async_copy(wu.at[g, :, at], wu_buf.at[slot], in_sem.at[0, slot]),
            pltpu.make_async_copy(wd.at[g, at, :], wd_buf.at[slot], in_sem.at[1, slot]),
        ]

    def writes(i):
        slot, g, at = lax.rem(i, 2), i // blocks, lanes(lax.rem(i, blocks), ublk)
        return [
            pltpu.make_async_copy(gu_buf.at[slot], gu.at[g, :, at], out_sem.at[0, slot]),
            pltpu.make_async_copy(gd_buf.at[slot], gd.at[g, :, at], out_sem.at[1, slot]),
        ]

    for copy in fetches(0):
        copy.start()

    @pl.loop(0, groups * blocks)
    def _(i):
        slot, g = lax.rem(i, 2), i // blocks
        outs = writes(i)

        @pl.when(i + 1 < groups * blocks)
        def _():
            for copy in fetches(i + 1):
                copy.start()

        for copy in fetches(i):
            copy.wait()
        up, down = wu_buf.at[slot], wd_buf.at[slot]
        mine = lax.broadcasted_iota(jnp.int32, (ublk, 128), 1) == lax.rem(i, blocks)
        h = tn(up[...], x3[...]) + lane_sum(jnp.where(mine, bup[g], 0.0))
        unit = i * ublk + lax.broadcasted_iota(jnp.int32, (ublk, 1), 0)
        on = jnp.where(unit < ints[0], 1.0, 0.0)
        inner = 0.7978845608028654 * (h + 0.044715 * (h * h * h))
        t = jnp.tanh(inner)
        cdf = 0.5 * (1.0 + t)
        slope = cdf + 0.5 * h * (1.0 - t * t) * (
            0.7978845608028654 * (1.0 + 3 * 0.044715 * h * h)
        )
        act = (h * cdf * on).astype(BF16)
        acc_a[...] += tn(down[...], act)
        dh = (nn(down[...], ct[...]) * slope * on).astype(BF16)
        ubias[g] += jnp.where(mine, lane_sum(dh), 0.0)
        acc_b[...] += nn(up[...], dh)

        @pl.when(i >= 2)
        def _():
            for copy in writes(i - 2):
                copy.wait()

        gu_buf[slot] = nt(x3[...], dh).astype(BF16)
        gd_buf[slot] = nt(ct[...], act).astype(BF16)
        for copy in outs:
            copy.start()

    for i in (groups * blocks - 2, groups * blocks - 1):
        for copy in writes(i):
            copy.wait()
    block[...] = (late_t[...] + acc_a[...] + obias[2]).T
    vec[:, 8:9] = lane_sum(ct[...])
    norm_back(late_t, gain[2], acc_b, ct, acc_a, e_low, sum_a, sum_b, sum_c)
    vec[:, 2:3] = lane_sum(sum_a[...])
    vec[:, 5:6] = lane_sum(sum_b[...])
    vec[:, 7:8] = lane_sum(sum_c[...])

    for g in range(groups):
        for h in range(hw // hd):
            rows = slice(h * hd, (h + 1) * hd)
            eh[g * hw + h * hd : g * hw + (h + 1) * hd] = (
                nn(oc[g, rows], e_low[...]) * head_on[g * (hw // hd) + h]
            ).astype(BF16)
    attend_back(q2, k2, v2, eh, prob2, grads, (2 * hw, 0, hw), hd, heads, sents)
    for g in range(groups):
        bvec[g, :, 2:3] = lane_sum(grads[g, 2 * hw : 3 * hw])
        bvec[g, :, 3:4] = lane_sum(grads[g, hw : 2 * hw])

        @pl.loop(0, 2 * hw // 128)
        def _(i, g=g):
            gx[g, :, lanes(i, 128)] = nt(mem_t[...], grads[g, lanes(i, 128)]).astype(BF16)

        @pl.loop(2 * hw // 128, lead // 128)
        def _(i, g=g):
            gx[g, :, lanes(i, 128)] = nt(x2[...], grads[g, lanes(i, 128)]).astype(BF16)

        tail = nt(e_low[...], attn2[g])
        gx[g, :, lead:pad] = (tail[:, :128] + nt(x2[...], grads[g, lead:pad])).astype(BF16)
        gx[g, :, pad:] = tail[:, 128:].astype(BF16)
        part = nn(wc[g, 0], grads[g, 2 * hw : 3 * hw])
        mpart = nn(wc[g, 1], grads[g, :hw]) + nn(wc[g, 2], grads[g, hw : 2 * hw])
        if g == 0:
            acc_b[...] = part
            tok_m = mpart
        else:
            acc_b[...] += part
            tok_m += mpart
    gmem[...] = tok_m.T.astype(BF16)
    norm_back(mid_t, gain[1], acc_b, acc_a, acc_a, e_low, sum_a, sum_b, sum_c)
    vec[:, 1:2] = lane_sum(sum_a[...])
    vec[:, 4:5] = lane_sum(sum_b[...])
    vec[:, 6:7] = lane_sum(sum_c[...])

    for g in range(groups):
        for h in range(hw // hd):
            rows = slice(h * hd, (h + 1) * hd)
            eh[g * hw + h * hd : g * hw + (h + 1) * hd] = (
                nn(os_[g, rows], e_low[...]) * head_on[g * (hw // hd) + h]
            ).astype(BF16)
    attend_back(q1, k1, v1, eh, prob1, grads, (0, hw, 2 * hw), hd, heads, sents)
    for g in range(groups):
        bvec[g, :, 0:1] = lane_sum(grads[g, :hw])
        bvec[g, :, 1:2] = lane_sum(grads[g, 2 * hw : 3 * hw])

        @pl.loop(0, lead // 128)
        def _(i, g=g):
            gs[g, :, lanes(i, 128)] = nt(x1[...], grads[g, lanes(i, 128)]).astype(BF16)

        tail = nt(e_low[...], attn1[g])
        gs[g, :, lead:pad] = (tail[:, :128] + nt(x1[...], grads[g, lead:pad])).astype(BF16)
        gs[g, :, pad:] = tail[:, 128:].astype(BF16)
        for j in range(3):
            part = nn(ws[g, j], grads[g, j * hw : (j + 1) * hw])
            if g == 0 and j == 0:
                acc_b[...] = part
            else:
                acc_b[...] += part
    norm_back(tok_t, gain[0], acc_b, acc_a, acc_a, None, sum_a, sum_b, None)
    vec[:, 0:1] = lane_sum(sum_a[...])
    vec[:, 3:4] = lane_sum(sum_b[...])
    gtok[...] = acc_a[...].T
    small[...] = jnp.zeros_like(small)
    small[0:16, :] = vec[...].T[0:16]
    for g in range(groups):
        small[16 + 8 * g : 24 + 8 * g, :hw] = bvec[g].T[0:8]
        small[32 + 8 * g : 40 + 8 * g, :ublk] = ubias[g].T[0:8]


def compute(hd, lw, head_on, ints, tok, cot, enc, ws, os_, wc, oc, wu, wd, cols, bcols, bup):
    tokens, width = tok.shape
    groups, _, _, hw = ws.shape
    units = wu.shape[2]
    sents = (ints.shape[0] - 1) // 2
    slots = tokens // sents
    heads = groups * hw // hd
    pad = -(-3 * hw // 128) * 128
    first = 3 * hw % 128
    shape = jax.ShapeDtypeStruct
    tall = pltpu.VMEM((width, tokens), F32)
    low = pltpu.VMEM((width, tokens), BF16)
    feat = pltpu.VMEM((groups * hw, tokens), BF16)
    attn = pltpu.VMEM((groups, first + hw, tokens), BF16)
    prob = pltpu.VMEM((heads * sents, slots, slots), BF16)
    sums = pltpu.VMEM((width, 128), F32)
    vm, sm = pl.BlockSpec(memory_space=pltpu.VMEM), pl.BlockSpec(memory_space=pltpu.SMEM)
    return pl.pallas_call(
        functools.partial(compute_kernel, hd),
        out_shape=(
            shape((tokens, width), F32),
            shape((tokens, width), F32),
            shape((tokens, width), BF16),
            shape((groups, width, 4 * hw), BF16),
            shape((groups, width, 4 * hw), BF16),
            shape((groups, width, units), BF16),
            shape((groups, width, units), BF16),
            shape((48, width), F32),
        ),
        in_specs=[sm] * 3 + [vm] * 7 + [ANY] * 2 + [vm] * 3,
        out_specs=(vm,) * 5 + (ANY,) * 2 + (vm,),
        scratch_shapes=[low] + [tall] * 4 + [low] * 6 + [feat] * 6 + [attn] * 2 + [prob] * 2
        + [pltpu.VMEM((groups, pad, tokens), BF16), feat] + [sums] * 4
        + [pltpu.VMEM((groups, hw, 128), F32), pltpu.VMEM((groups, bup.shape[1], 128), F32)]
        + [pltpu.VMEM((2, width, bup.shape[1]), BF16), pltpu.VMEM((2, bup.shape[1], width), BF16)]
        + [pltpu.VMEM((2, width, bup.shape[1]), BF16)] * 2
        + [pltpu.SemaphoreType.DMA((2, 2))] * 2,
        compiler_params=pltpu.CompilerParams(vmem_limit_bytes=63 << 20),
    )(lw, head_on, ints, tok, cot, enc, ws, os_, wc, oc, wu, wd, cols, bcols, bup)


def place():
    return tuple(lax.axis_index(name) for name in ("row", "dp", "mp"))


def send(src, dst, send_sem, recv_sem, peer):
    copy = pltpu.make_async_remote_copy(
        src_ref=src, dst_ref=dst, send_sem=send_sem, recv_sem=recv_sem,
        device_id=peer, device_id_type=MESH,
    )
    copy.start()
    return copy


def greet(peers):
    barrier = pltpu.get_barrier_semaphore()
    for peer in peers:
        pl.semaphore_signal(barrier, inc=1, device_id=peer, device_id_type=MESH)
    pl.semaphore_wait(barrier, len(peers))


def gather_kernel(n_row, n_in, *refs):
    encoder, halves = refs[0], refs[1 : 1 + n_in]
    land, wholes = refs[1 + n_in], refs[2 + n_in : 2 + 2 * n_in]
    send_sem, recv_sem, local_sem = refs[2 + 2 * n_in :]
    r, d, c = place()
    rows = land.shape[1]
    partner = (r, d, 1 - c)
    others = [(lax.rem(r + i, n_row), d, c) for i in range(1, n_row)]
    greet([partner] + others)
    copies = []
    for i, peer in enumerate(others):
        start = pl.multiple_of(peer[0] * (2 * rows) + c * rows, rows)
        copies.append(
            send(encoder.at[pl.ds(start, rows)], land.at[r], send_sem.at[i], recv_sem.at[i], peer)
        )
    for i, (half, whole) in enumerate(zip(halves, wholes)):
        j = n_row - 1 + i
        copies.append(send(half, whole.at[c], send_sem.at[j], recv_sem.at[j], partner))
        own = pltpu.make_async_copy(half, whole.at[c], local_sem.at[i])
        own.start()
        copies.append(own)
    start = pl.multiple_of(r * (2 * rows) + c * rows, rows)
    own = pltpu.make_async_copy(encoder.at[pl.ds(start, rows)], land.at[r], local_sem.at[n_in])
    own.start()
    copies.append(own)
    for copy in copies:
        copy.wait()


def gather(n_row, rows, encoder, halves):
    shape = jax.ShapeDtypeStruct
    out = [shape((n_row, rows, encoder.shape[1]), encoder.dtype)]
    out += [shape((2,) + half.shape, half.dtype) for half in halves]
    sems = n_row - 1 + len(halves)
    return pl.pallas_call(
        functools.partial(gather_kernel, n_row, len(halves)),
        out_shape=tuple(out),
        in_specs=[ANY] * (1 + len(halves)),
        out_specs=(VMEM,) * len(out),
        scratch_shapes=[
            pltpu.SemaphoreType.DMA((sems,)),
            pltpu.SemaphoreType.DMA((sems,)),
            pltpu.SemaphoreType.DMA((len(halves) + 1,)),
        ],
        compiler_params=pltpu.CompilerParams(
            collective_id=0, has_side_effects=True, vmem_limit_bytes=40 << 20
        ),
    )(encoder, *halves)


def window(rows, share):
    wide = max(
        -(-(i + 1) * share // 16) * 16 - i * share // 16 * 16 for i in range(rows // share)
    )
    return wide, lambda i: pl.multiple_of(
        jnp.minimum(i * share // 16 * 16, rows - wide), 16
    )


def scatter_kernel(n_row, n_dp, n_part, *refs):
    grads, (small, gmem, block, gtok) = refs[:n_part], refs[n_part : n_part + 4]
    refs = refs[n_part + 4 :]
    shards, (small_out, land, block_in, gtok_in) = refs[:n_part], refs[n_part : n_part + 4]
    refs = refs[n_part + 4 :]
    held, came, came_dp, low, came_row = [refs[i * n_part : (i + 1) * n_part] for i in range(5)]
    refs = refs[5 * n_part :]
    small_mp, small_dp, small_row, s_one, r_one, s_grad, r_grad, s_small, r_small, s_mem, r_mem, local_sem = refs
    r, d, c = place()
    rows = held[0].shape[1]
    wide, start_of = window(rows, rows // n_dp)
    partner = (r, d, 1 - c)
    rings = [(r, lax.rem(d + i, n_dp), c) for i in range(1, n_dp)]
    lines = [(lax.rem(r + i, n_row), d, c) for i in range(1, n_row)]
    greet([partner] + rings + lines)
    late = []

    first = []
    for i in range(n_part):
        first.append(send(grads[i].at[1 - c], came[i], s_one.at[i], r_one.at[i], partner))
        own = pltpu.make_async_copy(grads[i].at[c], held[i], local_sem.at[i])
        own.start()
        first.append(own)
    small_copy = send(small, small_mp, s_small.at[0], r_small.at[0], partner)
    mem = []
    for i, peer in enumerate(lines):
        mem.append(send(gmem, land.at[r, c], s_mem.at[i], r_mem.at[i], peer))
    own = pltpu.make_async_copy(gmem, land.at[r, c], local_sem.at[n_part])
    own.start()
    late.append(own)
    k = n_row - 1
    late.append(send(gmem, land.at[r, c], s_mem.at[k], r_mem.at[k], partner))
    late.append(send(block, block_in, s_one.at[n_part], r_one.at[n_part], partner))
    late.append(send(gtok, gtok_in, s_one.at[n_part + 1], r_one.at[n_part + 1], partner))

    over_dp = []
    for i in range(n_part):
        first[2 * i].wait()
        first[2 * i + 1].wait()

        @pl.loop(0, n_row)
        def _(z, i=i):
            @pl.loop(0, rows // 16)
            def _(j):
                at = lanes(j, 16)
                held[i][z, at] = (
                    held[i][z, at].astype(F32) + came[i][z, at].astype(F32)
                ).astype(BF16)

        over_dp.append([
            send(
                held[i].at[:, pl.ds(start_of(peer[1]), wide)], came_dp[i].at[j],
                s_grad.at[i, j], r_grad.at[i, j], peer,
            )
            for j, peer in enumerate(rings)
        ])
    small_copy.wait()
    small_dp[d] = small[...] + small_mp[...]
    small_over = [
        send(small_dp.at[d], small_dp.at[d], s_small.at[1 + j], r_small.at[1 + j], peer)
        for j, peer in enumerate(rings)
    ]

    over_row = []
    for i in range(n_part):
        for copy in over_dp[i]:
            copy.wait()

        @pl.loop(0, n_row)
        def _(z, i=i):
            total = held[i][z, pl.ds(start_of(d), wide)].astype(F32)
            for j in range(n_dp - 1):
                total += came_dp[i][j, z].astype(F32)
            low[i][z] = total.astype(BF16)

            @pl.when(z == r)
            def _():
                shards[i][...] = total

        over_row.append([
            send(
                low[i].at[peer[0]], came_row[i].at[j],
                s_grad.at[i, n_dp - 1 + j], r_grad.at[i, n_dp - 1 + j], peer,
            )
            for j, peer in enumerate(lines)
        ])
    for copy in small_over:
        copy.wait()
    total = small_dp[0]
    for j in range(1, n_dp):
        total += small_dp[j]
    small_row[r] = total
    small_over = [
        send(small_row.at[r], small_row.at[r], s_small.at[n_dp + j], r_small.at[n_dp + j], peer)
        for j, peer in enumerate(lines)
    ]

    for i in range(n_row - 1):
        mem[i].wait()
        origin = lax.rem(r + n_row - 1 - i, n_row)
        late.append(
            send(
                land.at[origin, c], land.at[origin, c], s_mem.at[n_row + i], r_mem.at[n_row + i], partner
            )
        )
    for i in range(n_part):
        for copy in over_row[i]:
            copy.wait()
        for j in range(n_row - 1):
            shards[i][...] += came_row[i][j].astype(F32)
    for copy in small_over:
        copy.wait()
    total = small_row[0]
    for j in range(1, n_row):
        total += small_row[j]
    small_out[...] = total
    for copy in late:
        copy.wait()


def scatter(n_row, n_dp, grads, small, gmem, block, gtok):
    shape = jax.ShapeDtypeStruct
    n = len(grads)
    tokens, width = gmem.shape
    rows = width // n_row
    wide, _ = window(rows, rows // n_dp)
    grads = [g.reshape(2, n_row, rows, g.shape[2]) for g in grads]
    full = [pltpu.VMEM(g.shape[1:], BF16) for g in grads]
    rings = [pltpu.VMEM((n_dp - 1, n_row, wide, g.shape[3]), BF16) for g in grads]
    lows = [pltpu.VMEM((n_row, wide, g.shape[3]), BF16) for g in grads]
    lines = [pltpu.VMEM((n_row - 1, wide, g.shape[3]), BF16) for g in grads]
    dma = pltpu.SemaphoreType.DMA
    return pl.pallas_call(
        functools.partial(scatter_kernel, n_row, n_dp, n),
        out_shape=tuple(shape((wide, g.shape[3]), F32) for g in grads)
        + (
            shape(small.shape, F32),
            shape((n_row, 2, tokens, width), BF16),
            shape(block.shape, F32),
            shape(gtok.shape, F32),
        ),
        in_specs=[ANY] * n + [VMEM] * 2 + [ANY] * 2,
        out_specs=(VMEM,) * (n + 1) + (ANY,) * 3,
        scratch_shapes=full + full + rings + lows + lines
        + [
            pltpu.VMEM(small.shape, F32),
            pltpu.VMEM((n_dp,) + small.shape, F32),
            pltpu.VMEM((n_row,) + small.shape, F32),
            dma((n + 2,)), dma((n + 2,)),
            dma((n, n_dp + n_row - 2)), dma((n, n_dp + n_row - 2)),
            dma((n_dp + n_row - 1,)), dma((n_dp + n_row - 1,)),
            dma((2 * n_row - 1,)), dma((2 * n_row - 1,)),
            dma((n + 1,)),
        ],
        compiler_params=pltpu.CompilerParams(
            collective_id=1, has_side_effects=True, vmem_limit_bytes=60 << 20
        ),
    )(*grads, small, gmem, block, gtok)


def per_device(
    tokens, encoder, layer_pick, piece_heads, piece_ffn, tgt_len, src_len, norm_gain, norm_shift,
    out_bias, w_self, o_self, b_self, w_cross, o_cross, b_cross, w_up, b_up, w_down, cotangent,
):
    n_row, n_dp = lax.axis_size("row"), lax.axis_size("dp")
    r, d, c = place()
    width = tokens.shape[1]
    half = tokens.shape[0] // 2
    sents = tgt_len.shape[0] // 2
    units, hw = w_up.shape[1], w_self.shape[2]
    chosen = lax.dynamic_index_in_dim(layer_pick, r, 0, keepdims=False).astype(F32)
    layer_weight = chosen / jnp.sum(chosen)
    head_limit = lax.dynamic_index_in_dim(piece_heads, r, 0, keepdims=False)
    unit_limit = lax.dynamic_index_in_dim(piece_ffn, r, 0, keepdims=True)
    head_on = (jnp.arange(2 * hw // HD) < head_limit).astype(F32)
    lengths = [lax.dynamic_slice_in_dim(v, c * sents, sents) for v in (tgt_len, src_len)]
    ints = jnp.concatenate([unit_limit] + lengths)
    cols = jnp.concatenate([norm_gain, norm_shift, out_bias]).T
    bcols = jnp.concatenate([b_self, b_cross]).T
    ublk = 256
    bup = jnp.pad(b_up.reshape(-1, ublk).T, ((0, 0), (0, 128 - units // ublk)))
    own = lambda v: lax.dynamic_slice_in_dim(v, c * half, half)
    encoder = encoder.reshape(-1, width)

    land, ws, os_, wc, oc, wu, wd, bcols, bup = gather(
        n_row, half, encoder, (w_self, o_self, w_cross, o_cross, w_up, w_down, bcols, bup)
    )
    block, gtok, gmem, *grads, small = compute(
        HD, layer_weight, head_on, ints, own(tokens), own(cotangent), land,
        ws, os_, wc, oc, wu, wd, cols, bcols, bup,
    )
    rows = width // n_row
    share = rows // n_dp

    def both(mine, other):
        return jnp.where(
            c == 0, jnp.concatenate([mine, other]), jnp.concatenate([other, mine])
        )

    if n_dp <= 8:
        *shards, small, glad, block_in, gtok_in = scatter(
            n_row, n_dp, grads, small, gmem, block, gtok
        )
        _, start_of = window(rows, share)
        shards = [
            lax.dynamic_slice_in_dim(v, share * d - start_of(d), share) for v in shards
        ]
        block, gtok = both(block, block_in), both(gtok, gtok_in)
    else:
        shards = [
            lax.psum_scatter(
                lax.dynamic_index_in_dim(lax.psum(v.astype(F32), "mp"), c, 0, keepdims=False),
                ("row", "dp"), scatter_dimension=0, tiled=True,
            )
            for v in grads
        ]
        small = lax.psum(small, ("row", "dp", "mp"))
        glad = lax.all_gather(gmem, ("row", "mp")).reshape(n_row, 2, half, width)
        block, gtok = [lax.all_gather(v, "mp", tiled=True) for v in (block, gtok)]

    mine = lax.dynamic_index_in_dim(layer_pick, r, 1, keepdims=False).astype(F32)
    totals = jnp.sum(layer_pick.astype(F32), axis=1)
    grad_encoder = (mine / totals)[:, None, None, None] * glad.astype(F32)
    at = (r * n_dp + d) * share
    norms = lax.dynamic_slice_in_dim(small[:9], at, share, axis=1)
    heads = lax.dynamic_slice_in_dim(small, 16 + 8 * c, 8)[:4, :hw]
    ups = lax.dynamic_slice_in_dim(small, 32 + 8 * c, 8)[: units // ublk, :ublk]
    cut = lambda v, i: v[:, i * hw : (i + 1) * hw]
    w_s, w_x, w_u, w_d = shards
    return (
        block,
        gtok,
        grad_encoder.reshape(1, -1, width),
        norms[0:3],
        norms[3:6],
        norms[6:9],
        jnp.stack([cut(w_s, 0), cut(w_s, 1), cut(w_s, 2)]),
        cut(w_s, 3).T,
        heads[0:2],
        jnp.stack([cut(w_x, 2), cut(w_x, 0), cut(w_x, 1)]),
        cut(w_x, 3).T,
        heads[2:4],
        w_u,
        ups.reshape(units),
        w_d.T,
    )


def solution(mesh):
    return jax.shard_map(
        per_device,
        mesh=mesh,
        in_specs=(
            P(("row", "dp"), None),
            P("row", "dp", None),
            P(),
            P(),
            P(),
            P(("row", "dp")),
            P(("row", "dp")),
            P(),
            P(),
            P(),
            P(None, None, "mp"),
            P("mp", None),
            P(None, "mp"),
            P(None, None, "mp"),
            P("mp", None),
            P(None, "mp"),
            P(None, "mp"),
            P("mp"),
            P("mp", None),
            P(("row", "dp"), None),
        ),
        out_specs=(
            P(("row", "dp"), None),
            P(("row", "dp"), None),
            P("row", "dp", None),
            P(None, ("row", "dp")),
            P(None, ("row", "dp")),
            P(None, ("row", "dp")),
            P(None, ("row", "dp"), "mp"),
            P("mp", ("row", "dp")),
            P(None, "mp"),
            P(None, ("row", "dp"), "mp"),
            P("mp", ("row", "dp")),
            P(None, "mp"),
            P(("row", "dp"), "mp"),
            P("mp"),
            P("mp", ("row", "dp")),
        ),
        check_vma=False,
    )
```

```python
import functools
import types
import jax
import jax.numpy as jnp
from jax import lax
from jax.experimental import pallas as pl
from jax.experimental.pallas import tpu as pltpu
from jax.sharding import PartitionSpec as P

HD = 80
EPSILON = 1e-05
MASKED = -1e30
F32, BF16 = jnp.float32, jnp.bfloat16
MESH = pl.DeviceIdType.MESH
ANY = pl.BlockSpec(memory_space=pl.ANY)
VMEM = pl.BlockSpec(memory_space=pltpu.VMEM)


def nn(a, b):
    return lax.dot_general(a, b, (((1,), (0,)), ((), ())), preferred_element_type=F32)


def nt(a, b):
    return lax.dot_general(a, b, (((1,), (1,)), ((), ())), preferred_element_type=F32)


def tn(a, b):
    return lax.dot_general(a, b, (((0,), (0,)), ((), ())), preferred_element_type=F32)


def lanes(i, n):
    return pl.ds(pl.multiple_of(i * n, n), n)


def layer_norm(v_ref, x_ref, gain, shift, begin, end):
    @pl.loop(begin // 128, end // 128)
    def _(i):
        v = v_ref[:, lanes(i, 128)].astype(F32)
        c = v - jnp.mean(v, axis=0, keepdims=True)
        r = lax.rsqrt(jnp.mean(c * c, axis=0, keepdims=True) + EPSILON)
        x_ref[:, lanes(i, 128)] = (c * r * gain + shift).astype(BF16)


def norm_back(v_ref, gain, up_ref, base_ref, out_ref, low_ref, sums, begin, end):
    gain_sum, shift_sum, bias_sum = sums
    if begin == 0:
        for ref in sums:
            ref[...] = jnp.zeros_like(ref)

    @pl.loop(begin // 128, end // 128)
    def _(i):
        at = lanes(i, 128)
        v = v_ref[:, at].astype(F32)
        c = v - jnp.mean(v, axis=0, keepdims=True)
        r = lax.rsqrt(jnp.mean(c * c, axis=0, keepdims=True) + EPSILON)
        xhat = c * r
        e = up_ref[:, at]
        gain_sum[...] += e * xhat
        shift_sum[...] += e
        eg = e * gain
        m1 = jnp.mean(eg, axis=0, keepdims=True)
        m2 = jnp.mean(eg * xhat, axis=0, keepdims=True)
        out = base_ref[:, at].astype(F32) + r * (eg - m1 - xhat * m2)
        out_ref[:, at] = out
        low = out.astype(BF16)
        low_ref[:, at] = low
        bias_sum[...] += low.astype(F32)


def attend(q_ref, k_ref, v_ref, out_ref, prob_ref, masks, head_on, hd, per, sents):
    groups, slots = out_ref.shape[0], q_ref.shape[1] // sents
    first = out_ref.shape[1] - per * hd
    for g in range(groups):

        @pl.loop(0, per)
        def _(h, g=g):
            rows = pl.ds(pl.multiple_of((g * per + h) * hd, 16), hd)
            to = pl.ds(pl.multiple_of(first + h * hd, 16), hd)
            for s, mask in masks.items():
                at = slice(s * slots, (s + 1) * slots)
                scores = tn(k_ref[rows, at], q_ref[rows, at]) * hd ** (-0.5)
                scores = jnp.where(mask, scores, MASKED)
                e = jnp.exp(scores - jnp.max(scores, axis=0, keepdims=True))
                total = jnp.sum(e, axis=0, keepdims=True)
                p = (e * (1.0 / total)).astype(BF16)
                prob_ref[(g * per + h) * sents + s] = p
                mixed = nn(v_ref[rows, at], p) * head_on(g, h)
                out_ref[g, to, at] = mixed.astype(BF16)


def attend_back(q_ref, k_ref, v_ref, e_ref, prob_ref, d_ref, at_rows, hd, per, sents, some):
    groups, slots = d_ref.shape[0], q_ref.shape[1] // sents
    for g in range(groups):

        @pl.loop(0, per)
        def _(h, g=g):
            rows = pl.ds(pl.multiple_of((g * per + h) * hd, 16), hd)
            dq_at, dk_at, dv_at = [
                pl.ds(pl.multiple_of(first + h * hd, 16), hd) for first in at_rows
            ]
            for s in some:
                at = slice(s * slots, (s + 1) * slots)
                e, p = e_ref[rows, at], prob_ref[(g * per + h) * sents + s]
                d_ref[g, dv_at, at] = nt(e, p).astype(BF16)
                dp = tn(v_ref[rows, at], e)
                pf = p.astype(F32)
                delta = jnp.sum(pf * dp, axis=0, keepdims=True)
                ds = (pf * (dp - delta) * hd ** (-0.5)).astype(BF16)
                d_ref[g, dq_at, at] = nn(k_ref[rows, at], ds).astype(BF16)
                d_ref[g, dk_at, at] = nt(q_ref[rows, at], ds).astype(BF16)


def lane_sum(values):
    return jnp.sum(values.astype(F32), axis=1, keepdims=True)


def place():
    return tuple(lax.axis_index(name) for name in ("row", "dp", "mp"))


def window(rows, share):
    wide = max(
        -(-(i + 1) * share // 16) * 16 - i * share // 16 * 16 for i in range(rows // share)
    )
    return wide, lambda i: pl.multiple_of(
        jnp.minimum(i * share // 16 * 16, rows - wide), 16
    )


def remote(src, dst, send_sem, recv_sem, peer):
    return pltpu.make_async_remote_copy(
        src_ref=src, dst_ref=dst, send_sem=send_sem, recv_sem=recv_sem,
        device_id=peer, device_id_type=MESH,
    )


def started(copy):
    copy.start()
    return copy


def layer_kernel(n_row, n_dp, names, *args):
    refs = dict(zip(names, args))
    ref = types.SimpleNamespace(**refs)
    layer_pick, piece_heads, piece_ffn, tgt_len, src_len = (ref.layer_pick, ref.piece_heads, ref.piece_ffn, ref.tgt_len, ref.src_len)
    tokens, cotangent, encoder = (ref.tokens, ref.cotangent, ref.encoder)
    ws, wc, os_, oc, wu_buf, wd_buf = (ref.ws, ref.wc, ref.os, ref.oc, ref.wu_buf, ref.wd_buf)
    tok_in, cot_in, enc, tout, tok_t, mid_t, late_t, acc_a, acc_b = (ref.tok_in, ref.cot_in, ref.enc, ref.tout, ref.tok_t, ref.mid_t, ref.late_t, ref.acc_a, ref.acc_b)
    x1, x2, x3, ct, mem_t, e_low, eh = (ref.x1, ref.x2, ref.x3, ref.ct, ref.mem_t, ref.e_low, ref.eh)
    q1, k1, v1, q2, k2, v2 = (ref.q1, ref.k1, ref.v1, ref.q2, ref.k2, ref.v2)
    attn1, attn2, prob1, prob2, grads = (ref.attn1, ref.attn2, ref.prob1, ref.prob2, ref.grads)
    sum_a, sum_b, sum_c, vec, bvec, ubias, colm, cols, bm, bcols, bups = (ref.sum_a, ref.sum_b, ref.sum_c, ref.vec, ref.bvec, ref.ubias, ref.colm, ref.cols, ref.bm, ref.bcols, ref.bups)
    out_s, out_x, out_u, out_d, abuf = (ref.out_s, ref.out_x, ref.out_u, ref.out_d, ref.abuf)
    local_sem, send_sem, recv_sem, fetch_sem, push_sem, land_sem = (ref.local_sem, ref.send_sem, ref.recv_sem, ref.fetch_sem, ref.push_sem, ref.land_sem)
    held, came = (ref.held_s, ref.held_x, ref.held_u, ref.held_d), (ref.came_s, ref.came_x, ref.came_u, ref.came_d)
    small, glad = (ref.small, ref.glad)
    spread = n_dp == 4

    width, tokens_here = tok_t.shape
    groups, _, hw, _ = ws.shape
    units, ublk, hd = ref.w_up.shape[1], bups.shape[1], HD
    blocks, per = units // ublk, hw // HD
    rows = width // n_row
    sents = tgt_len.shape[0] // 2
    slots = tokens_here // sents
    pad = -(-3 * hw // 128) * 128
    lead = 3 * hw // 128 * 128
    first = 3 * hw - lead
    r, d, c = place()
    partner = (r, d, 1 - c)
    rings = [(r, lax.rem(d + i, n_dp), c) for i in range(1, n_dp)] if spread else []
    lines = [(lax.rem(r + i, n_row), d, c) for i in range(1, n_row)]
    counts = {"local": 0, "link": 0}

    def fetch(src, dst):
        i = counts["local"]
        counts["local"] += 1
        return started(pltpu.make_async_copy(src, dst, local_sem.at[i]))

    def push(src, dst, peer):
        i = counts["link"]
        counts["link"] += 1
        return started(remote(src, dst, send_sem.at[i], recv_sem.at[i], peer))

    mine = pl.ds(pl.multiple_of(c * tokens_here, tokens_here), tokens_here)
    tok_copy = fetch(tokens.at[mine], tok_in)
    ws_copies = [fetch(ref.w_self, ws.at[0]), fetch(ref.o_self, os_.at[0])]
    bm[...] = jnp.zeros_like(bm)
    bm[0, 0:2, :hw] = ref.b_self[...]
    bm[0, 2:4, :hw] = ref.b_cross[...]
    bm[0, 8 : 8 + blocks, :ublk] = ref.b_up[...]
    colm[...] = jnp.zeros_like(colm)
    colm[0:3] = ref.norm_gain[...]
    colm[3:6] = ref.norm_shift[...]
    colm[6:9] = ref.out_bias[...]
    barrier = pltpu.get_barrier_semaphore()
    peers = [partner] + rings + lines
    for peer in peers:
        pl.semaphore_signal(barrier, inc=1, device_id=peer, device_id_type=MESH)
    pl.semaphore_wait(barrier, len(peers))
    ws_copies += [
        push(ref.w_self, ws.at[1], partner),
        push(bm.at[0], bm.at[1], partner),
        push(ref.o_self, os_.at[1], partner),
    ]
    def sentence(piece, i):
        start = (piece * 2 + c) * tokens_here + i * slots
        return encoder.at[pl.ds(pl.multiple_of(start, slots), slots)]

    columns = [slice(i * slots, (i + 1) * slots) for i in range(sents)]

    def send_sentence(i):
        at = columns[i]
        copies = [push(sentence(peer[0], i), enc.at[r, at], peer) for peer in lines]
        return copies + [fetch(sentence(r, i), enc.at[r, at])]

    enc_copies = [send_sentence(0)]
    wc_copies = [
        fetch(ref.w_cross, wc.at[0]),
        fetch(ref.o_cross, oc.at[0]),
        push(ref.w_cross, wc.at[1], partner),
        push(ref.o_cross, oc.at[1], partner),
    ]
    cot_copy = fetch(cotangent.at[mine], cot_in)
    ffn_copies = [
        push(ref.w_up, ref.up_in, partner),
        push(ref.w_down, ref.down_in, partner),
    ]

    cols[...] = colm[...].T
    gain, shift, obias = [[cols[:, j : j + 1] for j in range(3 * i, 3 * i + 3)] for i in range(3)]
    key_at = lax.broadcasted_iota(jnp.int32, (slots, slots), 0)
    query_at = lax.broadcasted_iota(jnp.int32, (slots, slots), 1)
    for zeroed in (attn1, attn2):
        zeroed[:, :first, :] = jnp.zeros((groups, first, tokens_here), BF16)
    grads[:, 3 * hw :, :] = jnp.zeros((groups, pad - 3 * hw, tokens_here), BF16)
    vec[...] = jnp.zeros_like(vec)
    bvec[...] = jnp.zeros_like(bvec)
    ubias[...] = jnp.zeros_like(ubias)
    heads_here, units_here = piece_heads[r], piece_ffn[r]
    group_at = [c, 1 - c]

    def head_on(g, h):
        return jnp.where(group_at[g] * per + h < heads_here, 1.0, 0.0)

    tok_copy.wait()
    tok_t[...] = tok_in[...].astype(F32).T.astype(BF16)
    layer_norm(tok_t, x1, gain[0], shift[0], 0, tokens_here)
    for copy in ws_copies:
        copy.wait()
    for g in range(groups):
        bcols[g] = bm[g, 0:8].T
        bups[g] = bm[g, 8:16, :ublk].T
    for g in range(groups):
        at = slice(g * hw, (g + 1) * hw)
        q1[at] = (nn(ws[g, 0], x1[...]) + bcols[g, :hw, 0:1]).astype(BF16)
        k1[at] = nn(ws[g, 1], x1[...]).astype(BF16)
        v1[at] = (nn(ws[g, 2], x1[...]) + bcols[g, :hw, 1:2]).astype(BF16)
    masks = {
        i: (key_at <= query_at) & (key_at < tgt_len[c * sents + i]) for i in range(sents)
    }
    attend(q1, k1, v1, attn1, prob1, masks, head_on, hd, per, sents)
    acc_a[...] = tn(os_[0], attn1[0, first:])
    for g in range(1, groups):
        acc_a[...] += tn(os_[g], attn1[g, first:])
    mid_t[...] = tok_t[...].astype(F32) + acc_a[...] + obias[0]
    layer_norm(mid_t, x2, gain[1], shift[1], 0, tokens_here)
    for copy in wc_copies:
        copy.wait()
    for g in range(groups):
        at = slice(g * hw, (g + 1) * hw)
        q2[at] = (nn(wc[g, 0], x2[...]) + bcols[g, :hw, 2:3]).astype(BF16)
    cot_copy.wait()
    ct[...] = cot_in[...].astype(F32).T.astype(BF16)

    picks = [
        jnp.full((1, width), layer_pick[r, i].astype(F32), F32) for i in range(layer_pick.shape[1])
    ]
    total = functools.reduce(jnp.add, picks)
    weights = [pick / total for pick in picks]
    def cross(i):
        at = columns[i]
        for copy in enc_copies[i]:
            copy.wait()
        if i + 1 < sents:
            enc_copies.append(send_sentence(i + 1))
        memory = weights[0] * enc[0, at].astype(F32)
        for j in range(1, n_row):
            memory += weights[j] * enc[j, at].astype(F32)
        mem_t[:, at] = memory.T.astype(BF16)
        for g in range(groups):
            to = slice(g * hw, (g + 1) * hw)
            k2[to, at] = nn(wc[g, 1], mem_t[:, at]).astype(BF16)
            v2[to, at] = (nn(wc[g, 2], mem_t[:, at]) + bcols[g, :hw, 3:4]).astype(BF16)
        masks = {i: key_at < src_len[c * sents + i]}
        attend(q2, k2, v2, attn2, prob2, masks, head_on, hd, per, sents)
        branch = tn(oc[0], attn2[0, first:, at])
        for g in range(1, groups):
            branch += tn(oc[g], attn2[g, first:, at])
        late_t[:, at] = mid_t[:, at] + branch + obias[1]
        layer_norm(late_t, x3, gain[2], shift[2], at.start, at.stop)

    def fetches(phase, i):
        slot, at = lax.rem(phase * blocks + i, 2), lanes(i, ublk)
        up, down = (ref.w_up, ref.w_down) if phase else (ref.up_in, ref.down_in)
        return [
            pltpu.make_async_copy(up.at[:, at], wu_buf.at[slot], fetch_sem.at[0, slot]),
            pltpu.make_async_copy(down.at[at, :], wd_buf.at[slot], fetch_sem.at[1, slot]),
        ]

    def pushes(i, k):
        at = lanes(i, ublk)
        return remote(
            (out_u, out_d)[k].at[:, :, at], came[2 + k].at[:, :, at],
            push_sem.at[k, i], land_sem.at[k, i], partner,
        )

    def feed_forward(n, ready):
        cols_at = columns[n]
        if n == 0:
            for copy in ready:
                copy.wait()
            for copy in fetches(0, 0):
                copy.start()
        acc_a[:, cols_at] = jnp.zeros((width, slots), F32)
        acc_b[:, cols_at] = jnp.zeros((width, slots), F32)
        for phase in range(2):
            g = 1 - phase
            sink_u, sink_d = (held[2], held[3]) if phase else (out_u, out_d)

            @pl.loop(0, blocks)
            def _(i, phase=phase, g=g, sink_u=sink_u, sink_d=sink_d):
                slot, at = lax.rem(phase * blocks + i, 2), lanes(i, ublk)

                @pl.when(i + 1 < blocks)
                def _():
                    for copy in fetches(phase, i + 1):
                        copy.start()

                if phase == 0 or n + 1 < sents:

                    @pl.when(i + 1 == blocks)
                    def _():
                        for copy in fetches(1 - phase, 0):
                            copy.start()

                for copy in fetches(phase, i):
                    copy.wait()
                up, down = wu_buf.at[slot], wd_buf.at[slot]
                here = lax.broadcasted_iota(jnp.int32, bups.shape[1:], 1) == i
                h = nn(up[...].T, x3[:, cols_at]) + lane_sum(jnp.where(here, bups[g], 0.0))
                unit = group_at[g] * units + i * ublk
                unit = unit + lax.broadcasted_iota(jnp.int32, (ublk, 1), 0)
                on = jnp.where(unit < units_here, 1.0, 0.0)
                inner = 0.7978845608028654 * (h + 0.044715 * (h * h * h))
                t = jnp.tanh(inner)
                cdf = 0.5 * (1.0 + t)
                slope = cdf + 0.5 * h * (1.0 - t * t) * (
                    0.7978845608028654 * (1.0 + 3 * 0.044715 * h * h)
                )
                act = (h * cdf * on).astype(BF16)
                acc_a[:, cols_at] += tn(down[...], act)
                dh = (nn(down[...], ct[:, cols_at]) * slope * on).astype(BF16)
                in_sums = lax.broadcasted_iota(jnp.int32, ubias.shape[1:], 1) == i
                ubias[g] += jnp.where(in_sums, lane_sum(dh), 0.0)
                acc_b[:, cols_at] += nn(up[...], dh)
                shape = (n_row, rows, ublk)
                grad_u = nt(x3[:, cols_at], dh).reshape(shape)
                grad_d = nt(ct[:, cols_at], act).reshape(shape)
                if n > 0:
                    grad_u += sink_u[:, :, at].astype(F32)
                    grad_d += sink_d[:, :, at].astype(F32)
                sink_u[:, :, at] = grad_u.astype(BF16)
                sink_d[:, :, at] = grad_d.astype(BF16)
                if phase == 0 and n + 1 == sents:
                    for k in range(2):
                        pushes(i, k).start()

        tout[cols_at] = (late_t[:, cols_at] + acc_a[:, cols_at] + obias[2]).T
        norm_back(
            late_t, gain[2], acc_b, ct, acc_a, e_low, (sum_a, sum_b, sum_c),
            cols_at.start, cols_at.stop,
        )

    late = []
    half = rows // 2
    wide, start_of = window(half, half // 2)
    up, across = lax.div(d, 2), lax.rem(d, 2)
    ours = half * up + start_of(across)
    pieces = {
        "u": (2, 0, units, True),
        "d": (3, 0, units, False),
        "x_a": (1, 0, 2 * hw, True),
        "x_b": (1, 2 * hw, 4 * hw, False),
        "s_a": (0, 0, 2 * hw, True),
        "s_b": (0, 2 * hw, 4 * hw, False),
    }

    def add_in(part, begin, end, landing, places, shard=None):
        size = landing.shape[1]
        at = pl.ds(begin, end - begin)
        loads = [
            pltpu.make_async_copy(
                landing.at[z], abuf.at[z % 2, pl.ds(0, size), pl.ds(0, end - begin)],
                fetch_sem.at[0, z % 2],
            )
            for z in range(n_row)
        ]
        loads[0].start()
        for z in range(n_row):
            if z + 1 < n_row:
                loads[z + 1].start()
            loads[z].wait()
            for to, source, count in places:

                @pl.loop(0, count // 16)
                def _(j, z=z, to=to, source=source):
                    held_at = pl.ds(pl.multiple_of(to + 16 * j, 16), 16)
                    from_at = pl.ds(pl.multiple_of(source + 16 * j, 16), 16)
                    total = held[part][z, held_at, at].astype(F32)
                    total += abuf[z % 2, from_at, pl.ds(0, end - begin)].astype(F32)
                    held[part][z, held_at, at] = total.astype(BF16)
                    if shard is not None:

                        @pl.when(r == z)
                        def _():
                            shard[from_at, at] = total

    def take(part, arrived):
        for copy in arrived:
            copy()
        add_in(part, 0, held[part].shape[2], came[part], [(0, 0, rows)])

    def first_ring(name):
        if not spread:
            return []
        part, begin, end, tall_first = pieces[name]
        landing, at = refs["ring_" + name], pl.ds(begin, end - begin)
        if tall_first:
            peer = (r, lax.rem(d + 2, 4), c)
            return [push(held[part].at[:, pl.ds(half * (1 - up), half), at], landing, peer)]
        peer = (r, d + 1 - 2 * across, c)
        return [
            push(
                held[part].at[:, pl.ds(half * i + start_of(1 - across), wide), at],
                landing.at[:, pl.ds(wide * i, wide)], peer,
            )
            for i in range(2)
        ]

    def second_ring(name, copies):
        if not spread:
            return []
        part, begin, end, tall_first = pieces[name]
        landing, at = refs["ring_" + name], pl.ds(begin, end - begin)
        for copy in copies:
            copy.wait()
        if tall_first:
            add_in(part, begin, end, landing, [(half * up, 0, half)])
            peer, gone = (r, d + 1 - 2 * across, c), half * up + start_of(1 - across)
        else:
            places = [(half * i + start_of(across), wide * i, wide) for i in range(2)]
            add_in(part, begin, end, landing, places)
            peer, gone = (r, lax.rem(d + 2, 4), c), half * (1 - up) + start_of(across)
        gone = pl.multiple_of(gone, 16)
        return [push(held[part].at[:, pl.ds(gone, wide), at], refs["turn_" + name], peer)]

    def to_lines(name, copies):
        if not spread:
            return []
        part, begin, end, _ = pieces[name]
        for copy in copies:
            copy.wait()
        shard, line = refs["shard_" + "sxud"[part]], refs["line_" + "sxud"[part]]
        at, here = pl.ds(begin, end - begin), pl.multiple_of(ours, 16)
        add_in(part, begin, end, refs["turn_" + name], [(here, 0, wide)], shard)
        return [
            push(held[part].at[peer[0], pl.ds(here, wide), at], line.at[j, :, at], peer)
            for j, peer in enumerate(lines)
        ]

    def sum_lines(part, copies):
        if spread:
            shard, line = refs["shard_" + "sxud"[part]], refs["line_" + "sxud"[part]]
            for copy in copies:
                copy.wait()
            for j in range(n_row - 1):
                shard[...] += line[j].astype(F32)

    def heads_back(weight, at):
        for g in range(groups):
            for h in range(per):
                to = slice(h * hd, (h + 1) * hd)
                eh[g * hw + h * hd : g * hw + (h + 1) * hd, at] = (
                    nn(weight[g, to], e_low[:, at]) * head_on(g, h)
                ).astype(BF16)

    def cross_back(i):
        at = columns[i]
        heads_back(oc, at)
        attend_back(q2, k2, v2, eh, prob2, grads, (2 * hw, 0, hw), hd, per, sents, [i])
        total = jnp.zeros((width, slots), F32)
        for g in range(groups):
            total += tn(wc[g, 1], grads[g, :hw, at]) + tn(wc[g, 2], grads[g, hw : 2 * hw, at])
        tok_in[at] = total.T.astype(BF16)
        late.append(fetch(tok_in.at[at], glad.at[r, c, at]))
        late.append(push(tok_in.at[at], glad.at[r, c, at], partner))
        return [push(tok_in.at[at], glad.at[r, c, at], peer) for peer in lines]

    mem_copies = []
    for i in range(sents):
        cross(i)
        feed_forward(i, ffn_copies)
        if i + 1 == sents:
            block_copies = [fetch(tout, ref.block), push(tout, ref.block_in, partner)]
            take(2, [pushes(j, 0).wait for j in range(blocks)])
            ring_u = first_ring("u")
            take(3, [pushes(j, 1).wait for j in range(blocks)])
            ring_d = first_ring("d")
        mem_copies.append(cross_back(i))
    vec[:, 8:9] = lane_sum(ct[...])
    vec[:, 2:3] = lane_sum(sum_a[...])
    vec[:, 5:6] = lane_sum(sum_b[...])
    vec[:, 7:8] = lane_sum(sum_c[...])

    def put(g, begin, value):
        sink = (held_now, out_now)[g]
        at = pl.ds(begin, value.shape[1])
        sink[:, :, at] = value.astype(BF16).reshape(n_row, rows, -1)

    def weight_grads(g, sources, attn):
        tail = nt(e_low[...], attn[g])
        begin = 0
        for source, end in sources:
            while begin < end:
                step = min(256, end - begin)
                value = nt(source[...], grads[g, begin : begin + step])
                if begin + step == pad:
                    keep = lead - begin
                    if keep:
                        put(g, begin, value[:, :keep])
                    put(g, lead, value[:, keep:] + tail[:, : pad - lead])
                else:
                    put(g, begin, value)
                begin += step
        put(g, pad, tail[:, pad - lead :])

    held_now, out_now = held[1], out_x
    for g in (1, 0):
        bvec[g, :hw, 2:3] = lane_sum(grads[g, 2 * hw : 3 * hw])
        bvec[g, :hw, 3:4] = lane_sum(grads[g, hw : 2 * hw])
        weight_grads(g, [(mem_t, 2 * hw), (x2, pad)], attn2)
        if g == 1:
            came_x = push(out_x, came[1], partner)
            acc_b[...] = tn(wc[g, 0], grads[g, 2 * hw : 3 * hw])
        else:
            acc_b[...] += tn(wc[g, 0], grads[g, 2 * hw : 3 * hw])
    norm_back(
        mid_t, gain[1], acc_b, acc_a, acc_a, e_low, (sum_a, sum_b, sum_c), 0, tokens_here
    )
    vec[:, 1:2] = lane_sum(sum_a[...])
    vec[:, 4:5] = lane_sum(sum_b[...])
    vec[:, 6:7] = lane_sum(sum_c[...])
    take(1, [came_x.wait])
    ring_x = [first_ring("x_a"), first_ring("x_b")]

    heads_back(os_, slice(0, tokens_here))
    attend_back(q1, k1, v1, eh, prob1, grads, (0, hw, 2 * hw), hd, per, sents, range(sents))
    ring_u = second_ring("u", ring_u)
    ring_d = second_ring("d", ring_d)
    held_now, out_now = held[0], out_s
    for g in (1, 0):
        bvec[g, :hw, 0:1] = lane_sum(grads[g, :hw])
        bvec[g, :hw, 1:2] = lane_sum(grads[g, 2 * hw : 3 * hw])
        weight_grads(g, [(x1, pad)], attn1)
        if g == 1:
            came_s = push(out_s, came[0], partner)
    for g in range(groups):
        for j in range(3):
            part = tn(ws[g, j], grads[g, j * hw : (j + 1) * hw])
            if g == 0 and j == 0:
                acc_b[...] = part
            else:
                acc_b[...] += part
    take(0, [came_s.wait])
    ring_s = [first_ring("s_a"), first_ring("s_b")]
    ring_x = [second_ring("x_a", ring_x[0]), second_ring("x_b", ring_x[1])]
    norm_back(
        tok_t, gain[0], acc_b, acc_a, acc_a, e_low, (sum_a, sum_b, sum_c), 0, tokens_here
    )
    vec[:, 0:1] = lane_sum(sum_a[...])
    vec[:, 3:4] = lane_sum(sum_b[...])
    for copy in block_copies:
        copy.wait()
    tout[...] = acc_a[...].T
    late += [fetch(tout, ref.gtok), push(tout, ref.gtok_in, partner)]

    small[...] = jnp.zeros_like(small)
    small[0:16, :] = vec[...].T[0:16]
    for g in range(groups):
        at = pl.multiple_of(16 + 8 * group_at[g], 8)
        small[pl.ds(at, 8), :hw] = bvec[g].T[0:8, :hw]
        small[pl.ds(at + 16, 8), :ublk] = ubias[g].T[0:8]
    if spread:
        small_mp, small_dp, small_row = (ref.small_mp, ref.small_dp, ref.small_row)
        push(small, small_mp, partner).wait()
        small_dp[d] = small[...] + small_mp[...]
        small_copies = [push(small_dp.at[d], small_dp.at[d], peer) for peer in rings]
        line_u = to_lines("u", ring_u)
        line_d = to_lines("d", ring_d)
        ring_s = [second_ring("s_a", ring_s[0]), second_ring("s_b", ring_s[1])]
        for copy in small_copies:
            copy.wait()
        total = small_dp[0]
        for j in range(1, n_dp):
            total += small_dp[j]
        small_row[r] = total
        small_copies = [push(small_row.at[r], small_row.at[r], peer) for peer in lines]
        line_x = to_lines("x_a", ring_x[0]) + to_lines("x_b", ring_x[1])
    for at, copies in zip(columns, mem_copies):
        for i, copy in enumerate(copies):
            copy.wait()
            came_at = glad.at[lax.rem(r + n_row - 1 - i, n_row), c, at]
            late.append(push(came_at, came_at, partner))
    if spread:
        line_s = to_lines("s_a", ring_s[0]) + to_lines("s_b", ring_s[1])
        sum_lines(2, line_u)
        sum_lines(3, line_d)
        sum_lines(1, line_x)
        for copy in small_copies:
            copy.wait()
        total = small_row[0]
        for j in range(1, n_row):
            total += small_row[j]
        small[...] = total
        sum_lines(0, line_s)
    for copy in late:
        copy.wait()


def layer(n_row, n_dp, scalars, vectors, arrays):
    shape = jax.ShapeDtypeStruct
    encoder, w_self, w_up = arrays["encoder"], arrays["w_self"], arrays["w_up"]
    width, tokens = encoder.shape[1], arrays["tokens"].shape[0] // 2
    hw, units = w_self.shape[1], w_up.shape[1]
    blocks, ublk = vectors["b_up"].shape
    sents = scalars["tgt_len"].shape[0] // 2
    slots, heads = tokens // sents, 2 * hw // HD
    pad, first = -(-3 * hw // 128) * 128, 3 * hw % 128
    rows = width // n_row
    spread = n_dp == 4
    wide, _ = window(rows // 2, rows // 4)
    sizes = {"s": 4 * hw, "x": 4 * hw, "u": units, "d": units}
    outs = {
        "block": ((tokens, width), F32, ANY),
        "block_in": ((tokens, width), F32, ANY),
        "gtok": ((tokens, width), F32, ANY),
        "gtok_in": ((tokens, width), F32, ANY),
        "glad": ((n_row, 2, tokens, width), BF16, ANY),
        "small": ((48, width), F32, VMEM),
        "up_in": (w_up.shape, BF16, ANY),
        "down_in": (arrays["w_down"].shape, BF16, ANY),
    }
    scratch = {}
    for name, size in sizes.items():
        outs["came_" + name] = ((n_row, rows, size), BF16, ANY)
        if spread:
            for piece in (name,) if name in "ud" else (name + "_a", name + "_b"):
                tall_first = piece == "u" or piece[-1] == "a"
                cols_of = size if name in "ud" else size // 2
                landing = rows // 2 if tall_first else 2 * wide
                outs["ring_" + piece] = ((n_row, landing, cols_of), BF16, ANY)
                outs["turn_" + piece] = ((n_row, wide, cols_of), BF16, ANY)
            outs["shard_" + name] = ((wide, size), F32, VMEM)
            scratch["held_" + name] = pltpu.VMEM((n_row, rows, size), BF16)
            scratch["line_" + name] = pltpu.VMEM((n_row - 1, wide, size), BF16)
        else:
            outs["held_" + name] = ((n_row, rows, size), BF16, VMEM)
    tall, low = pltpu.VMEM((width, tokens), F32), pltpu.VMEM((width, tokens), BF16)
    flat = pltpu.VMEM((tokens, width), BF16)
    scratch["ws"] = scratch["wc"] = pltpu.VMEM((2,) + w_self.shape, BF16)
    scratch["os"] = scratch["oc"] = pltpu.VMEM((2, hw, width), BF16)
    scratch["wu_buf"] = pltpu.VMEM((2, width, ublk), BF16)
    scratch["wd_buf"] = pltpu.VMEM((2, ublk, width), BF16)
    scratch["out_u"] = scratch["out_d"] = pltpu.VMEM((n_row, rows, units), BF16)
    scratch["out_s"] = scratch["out_x"] = pltpu.VMEM((n_row, rows, 4 * hw), BF16)
    scratch["abuf"] = pltpu.VMEM((2, rows, max(sizes.values())), BF16)
    scratch["tok_in"] = scratch["cot_in"] = flat
    scratch["enc"] = pltpu.VMEM((n_row, tokens, width), BF16)
    scratch["tout"] = pltpu.VMEM((tokens, width), F32)
    for name in ("mid_t", "late_t", "acc_a", "acc_b"):
        scratch[name] = tall
    for name in ("tok_t", "x1", "x2", "x3", "ct", "mem_t", "e_low"):
        scratch[name] = low
    for name in ("q1", "k1", "v1", "q2", "k2", "v2", "eh"):
        scratch[name] = pltpu.VMEM((2 * hw, tokens), BF16)
    for name in ("attn1", "attn2"):
        scratch[name] = pltpu.VMEM((2, first + hw, tokens), BF16)
    for name in ("prob1", "prob2"):
        scratch[name] = pltpu.VMEM((heads * sents, slots, slots), BF16)
    scratch["grads"] = pltpu.VMEM((2, pad, tokens), BF16)
    for name in ("sum_a", "sum_b", "sum_c", "vec", "cols"):
        scratch[name] = pltpu.VMEM((width, 128), F32)
    scratch["colm"] = pltpu.VMEM((128, width), F32)
    scratch["bm"] = pltpu.VMEM((2, 16, width), F32)
    scratch["bvec"] = pltpu.VMEM((2, -(-hw // 128) * 128, 128), F32)
    scratch["bcols"] = pltpu.VMEM((2, width, 8), F32)
    scratch["ubias"] = pltpu.VMEM((2, ublk, 128), F32)
    scratch["bups"] = pltpu.VMEM((2, ublk, 8), F32)
    if spread:
        scratch["small_mp"] = pltpu.VMEM((48, width), F32)
        scratch["small_dp"] = pltpu.VMEM((n_dp, 48, width), F32)
        scratch["small_row"] = pltpu.VMEM((n_row, 48, width), F32)
    dma = pltpu.SemaphoreType.DMA
    scratch["local_sem"] = dma((16,))
    scratch["send_sem"] = scratch["recv_sem"] = dma((80,))
    scratch["fetch_sem"] = dma((2, 2))
    scratch["push_sem"] = scratch["land_sem"] = dma((2, blocks))
    names = list(scalars) + list(vectors) + list(arrays) + list(outs) + list(scratch)
    smem = pl.BlockSpec(memory_space=pltpu.SMEM)
    results = pl.pallas_call(
        functools.partial(layer_kernel, n_row, n_dp, names),
        out_shape=tuple(shape(s, t) for s, t, _ in outs.values()),
        in_specs=[smem] * len(scalars) + [VMEM] * len(vectors) + [ANY] * len(arrays),
        out_specs=tuple(spec for _, _, spec in outs.values()),
        scratch_shapes=list(scratch.values()),
        compiler_params=pltpu.CompilerParams(
            collective_id=0, has_side_effects=True, vmem_limit_bytes=63 << 20
        ),
    )(*scalars.values(), *vectors.values(), *arrays.values())
    return dict(zip(outs, results))


def per_device(
    tokens, encoder, layer_pick, piece_heads, piece_ffn, tgt_len, src_len, norm_gain, norm_shift,
    out_bias, w_self, o_self, b_self, w_cross, o_cross, b_cross, w_up, b_up, w_down, cotangent,
):
    n_row, n_dp = lax.axis_size("row"), lax.axis_size("dp")
    r, d, c = place()
    width = tokens.shape[1]
    units, hw = w_up.shape[1], w_self.shape[2]
    ublk = 256
    out = layer(
        n_row, n_dp,
        dict(
            layer_pick=layer_pick, piece_heads=piece_heads, piece_ffn=piece_ffn,
            tgt_len=tgt_len, src_len=src_len,
        ),
        dict(
            norm_gain=norm_gain, norm_shift=norm_shift, out_bias=out_bias,
            b_self=b_self, b_cross=b_cross, b_up=b_up.reshape(-1, ublk),
        ),
        dict(
            tokens=tokens, cotangent=cotangent, encoder=encoder.reshape(-1, width),
            w_self=jnp.swapaxes(w_self, 1, 2), o_self=o_self,
            w_cross=jnp.swapaxes(w_cross, 1, 2), o_cross=o_cross, w_up=w_up, w_down=w_down,
        ),
    )
    share = width // n_row // n_dp
    small = out["small"]
    if n_dp == 4:
        _, start_of = window(2 * share, share)
        across = lax.rem(d, 2)
        shards = [
            lax.dynamic_slice_in_dim(
                out["shard_" + name], share * across - start_of(across), share
            )
            for name in "sxud"
        ]
    else:
        shards = [
            lax.psum_scatter(
                out["held_" + name].astype(F32).reshape(width, -1),
                ("row", "dp"), scatter_dimension=0, tiled=True,
            )
            for name in "sxud"
        ]
        small = lax.psum(small, ("row", "dp", "mp"))

    def both(mine, other):
        return jnp.where(
            c == 0, jnp.concatenate([mine, other]), jnp.concatenate([other, mine])
        )

    mine = lax.dynamic_index_in_dim(layer_pick, r, 1, keepdims=False).astype(F32)
    totals = jnp.sum(layer_pick.astype(F32), axis=1)
    grad_encoder = (mine / totals)[:, None, None, None] * out["glad"].astype(F32)
    at = (r * n_dp + d) * share
    norms = lax.dynamic_slice_in_dim(small[:9], at, share, axis=1)
    heads = lax.dynamic_slice_in_dim(small, 16 + 8 * c, 8)[:4, :hw]
    ups = lax.dynamic_slice_in_dim(small, 32 + 8 * c, 8)[: units // ublk, :ublk]
    cut = lambda v, i: v[:, i * hw : (i + 1) * hw]
    w_s, w_x, w_u, w_d = shards
    return (
        both(out["block"], out["block_in"]),
        both(out["gtok"], out["gtok_in"]),
        grad_encoder.reshape(1, -1, width),
        norms[0:3],
        norms[3:6],
        norms[6:9],
        jnp.stack([cut(w_s, 0), cut(w_s, 1), cut(w_s, 2)]),
        cut(w_s, 3).T,
        heads[0:2],
        jnp.stack([cut(w_x, 2), cut(w_x, 0), cut(w_x, 1)]),
        cut(w_x, 3).T,
        heads[2:4],
        w_u,
        ups.reshape(units),
        w_d.T,
    )


def solution(mesh):
    return jax.shard_map(
        per_device,
        mesh=mesh,
        in_specs=(
            P(("row", "dp"), None),
            P("row", "dp", None),
            P(),
            P(),
            P(),
            P(("row", "dp")),
            P(("row", "dp")),
            P(),
            P(),
            P(),
            P(None, None, "mp"),
            P("mp", None),
            P(None, "mp"),
            P(None, None, "mp"),
            P("mp", None),
            P(None, "mp"),
            P(None, "mp"),
            P("mp"),
            P("mp", None),
            P(("row", "dp"), None),
        ),
        out_specs=(
            P(("row", "dp"), None),
            P(("row", "dp"), None),
            P("row", "dp", None),
            P(None, ("row", "dp")),
            P(None, ("row", "dp")),
            P(None, ("row", "dp")),
            P(None, ("row", "dp"), "mp"),
            P("mp", ("row", "dp")),
            P(None, "mp"),
            P(None, ("row", "dp"), "mp"),
            P("mp", ("row", "dp")),
            P(None, "mp"),
            P(("row", "dp"), "mp"),
            P("mp"),
            P("mp", ("row", "dp")),
        ),
        check_vma=False,
    )
```

```python
import functools
import types
import jax
import jax.numpy as jnp
from jax import lax
from jax.experimental import pallas as pl
from jax.experimental.pallas import tpu as pltpu
from jax.sharding import PartitionSpec as P

HD = 80
EPSILON = 1e-05
MASKED = -1e30
F32, BF16 = jnp.float32, jnp.bfloat16
MESH = pl.DeviceIdType.MESH
ANY = pl.BlockSpec(memory_space=pl.ANY)
VMEM = pl.BlockSpec(memory_space=pltpu.VMEM)


def nn(a, b):
    return lax.dot_general(a, b, (((1,), (0,)), ((), ())), preferred_element_type=F32)


def nt(a, b):
    return lax.dot_general(a, b, (((1,), (1,)), ((), ())), preferred_element_type=F32)


def tn(a, b):
    return lax.dot_general(a, b, (((0,), (0,)), ((), ())), preferred_element_type=F32)


def lanes(i, n):
    return pl.ds(pl.multiple_of(i * n, n), n)


def layer_norm(v_ref, x_ref, gain, shift, begin, end):
    @pl.loop(begin // 128, end // 128)
    def _(i):
        v = v_ref[:, lanes(i, 128)].astype(F32)
        c = v - jnp.mean(v, axis=0, keepdims=True)
        r = lax.rsqrt(jnp.mean(c * c, axis=0, keepdims=True) + EPSILON)
        x_ref[:, lanes(i, 128)] = (c * r * gain + shift).astype(BF16)


def norm_back(v_ref, gain, up_ref, base_ref, out_ref, low_ref, sums, begin, end):
    gain_sum, shift_sum, bias_sum = sums
    if begin == 0:
        for ref in sums:
            ref[...] = jnp.zeros_like(ref)

    @pl.loop(begin // 128, end // 128)
    def _(i):
        at = lanes(i, 128)
        v = v_ref[:, at].astype(F32)
        c = v - jnp.mean(v, axis=0, keepdims=True)
        r = lax.rsqrt(jnp.mean(c * c, axis=0, keepdims=True) + EPSILON)
        xhat = c * r
        e = up_ref[:, at]
        gain_sum[...] += e * xhat
        shift_sum[...] += e
        eg = e * gain
        m1 = jnp.mean(eg, axis=0, keepdims=True)
        m2 = jnp.mean(eg * xhat, axis=0, keepdims=True)
        out = base_ref[:, at].astype(F32) + r * (eg - m1 - xhat * m2)
        out_ref[:, at] = out
        low = out.astype(BF16)
        low_ref[:, at] = low
        bias_sum[...] += low.astype(F32)


def attend(q_ref, k_ref, v_ref, out_ref, prob_ref, masks, head_on, hd, per, sents):
    groups, slots = out_ref.shape[0], q_ref.shape[1] // sents
    first = out_ref.shape[1] - per * hd
    for g in range(groups):

        @pl.loop(0, per, unroll=2)
        def _(h, g=g):
            rows = pl.ds(pl.multiple_of((g * per + h) * hd, 16), hd)
            to = pl.ds(pl.multiple_of(first + h * hd, 16), hd)
            for s, mask in masks.items():
                at = slice(s * slots, (s + 1) * slots)
                scores = tn(k_ref[rows, at], q_ref[rows, at]) * hd ** (-0.5)
                scores = jnp.where(mask, scores, MASKED)
                e = jnp.exp(scores - jnp.max(scores, axis=0, keepdims=True))
                total = jnp.sum(e, axis=0, keepdims=True)
                p = (e * (1.0 / total)).astype(BF16)
                prob_ref[(g * per + h) * sents + s] = p
                mixed = nn(v_ref[rows, at], p) * head_on(g, h)
                out_ref[g, to, at] = mixed.astype(BF16)


def attend_back(q_ref, k_ref, v_ref, e_ref, prob_ref, d_ref, at_rows, hd, per, sents, some):
    groups, slots = d_ref.shape[0], q_ref.shape[1] // sents
    for g in range(groups):

        @pl.loop(0, per, unroll=2)
        def _(h, g=g):
            rows = pl.ds(pl.multiple_of((g * per + h) * hd, 16), hd)
            dq_at, dk_at, dv_at = [
                pl.ds(pl.multiple_of(first + h * hd, 16), hd) for first in at_rows
            ]
            for s in some:
                at = slice(s * slots, (s + 1) * slots)
                e, p = e_ref[rows, at], prob_ref[(g * per + h) * sents + s]
                d_ref[g, dv_at, at] = nt(e, p).astype(BF16)
                dp = tn(v_ref[rows, at], e)
                pf = p.astype(F32)
                delta = jnp.sum(pf * dp, axis=0, keepdims=True)
                ds = (pf * (dp - delta) * hd ** (-0.5)).astype(BF16)
                d_ref[g, dq_at, at] = nn(k_ref[rows, at], ds).astype(BF16)
                d_ref[g, dk_at, at] = nt(q_ref[rows, at], ds).astype(BF16)


def lane_sum(values):
    return jnp.sum(values.astype(F32), axis=1, keepdims=True)


def place():
    return tuple(lax.axis_index(name) for name in ("row", "dp", "mp"))


def window(rows, share):
    wide = max(
        -(-(i + 1) * share // 16) * 16 - i * share // 16 * 16 for i in range(rows // share)
    )
    return wide, lambda i: pl.multiple_of(
        jnp.minimum(i * share // 16 * 16, rows - wide), 16
    )


def remote(src, dst, send_sem, recv_sem, peer):
    return pltpu.make_async_remote_copy(
        src_ref=src, dst_ref=dst, send_sem=send_sem, recv_sem=recv_sem,
        device_id=peer, device_id_type=MESH,
    )


def started(copy):
    copy.start()
    return copy


def layer_kernel(n_row, n_dp, names, *args):
    refs = dict(zip(names, args))
    ref = types.SimpleNamespace(**refs)
    layer_pick, piece_heads, piece_ffn, tgt_len, src_len = (ref.layer_pick, ref.piece_heads, ref.piece_ffn, ref.tgt_len, ref.src_len)
    tokens, cotangent, encoder = (ref.tokens, ref.cotangent, ref.encoder)
    ws, wc, os_, oc, wu_buf, wd_buf = (ref.ws, ref.wc, ref.os, ref.oc, ref.wu_buf, ref.wd_buf)
    act_buf, dh_buf = ref.act_buf, ref.dh_buf
    via, near, near_sem = ref.via, ref.near, ref.near_sem
    enc_s, enc_r, via_s, via_r = ref.enc_s, ref.enc_r, ref.via_s, ref.via_r
    mem_s, mem_r, link_s, link_r = ref.mem_s, ref.mem_r, ref.link_s, ref.link_r
    tok_in, cot_in, enc, tout, tok_t, mid_t, late_t, acc_a, acc_b = (ref.tok_in, ref.cot_in, ref.enc, ref.tout, ref.tok_t, ref.mid_t, ref.late_t, ref.acc_a, ref.acc_b)
    x1, x2, x3, ct, mem_t, e_low, eh = (ref.x1, ref.x2, ref.x3, ref.ct, ref.mem_t, ref.e_low, ref.eh)
    q1, k1, v1, q2, k2, v2 = (ref.q1, ref.k1, ref.v1, ref.q2, ref.k2, ref.v2)
    attn1, attn2, prob1, prob2, grads = (ref.attn1, ref.attn2, ref.prob1, ref.prob2, ref.grads)
    sum_a, sum_b, sum_c, vec, bvec, ubias, colm, cols, bm, bcols, bups = (ref.sum_a, ref.sum_b, ref.sum_c, ref.vec, ref.bvec, ref.ubias, ref.colm, ref.cols, ref.bm, ref.bcols, ref.bups)
    out_s, out_x, out_u, out_d, abuf = (ref.out_s, ref.out_x, ref.out_u, ref.out_d, ref.abuf)
    local_sem, send_sem, recv_sem, fetch_sem, push_sem, land_sem = (ref.local_sem, ref.send_sem, ref.recv_sem, ref.fetch_sem, ref.push_sem, ref.land_sem)
    held, came = (ref.held_s, ref.held_x, ref.held_u, ref.held_d), (ref.came_s, ref.came_x, ref.came_u, ref.came_d)
    small, glad = (ref.small, ref.glad)
    spread = n_dp == 4

    width, tokens_here = tok_t.shape
    groups, _, hw, _ = ws.shape
    units, ublk, hd = ref.w_up.shape[1], bups.shape[1], HD
    blocks, per = units // ublk, hw // HD
    rows = width // n_row
    sents = tgt_len.shape[0] // 2
    slots = tokens_here // sents
    pad = -(-3 * hw // 128) * 128
    lead = 3 * hw // 128 * 128
    first = 3 * hw - lead
    r, d, c = place()
    partner = (r, d, 1 - c)
    rings = [(r, lax.rem(d + i, n_dp), c) for i in range(1, n_dp)] if spread else []
    lines = [(lax.rem(r + i, n_row), d, c) for i in range(1, n_row)]
    counts = {"local": 0, "link": 0}

    def fetch(src, dst):
        i = counts["local"]
        counts["local"] += 1
        return started(pltpu.make_async_copy(src, dst, local_sem.at[i]))

    def push(src, dst, peer):
        i = counts["link"]
        counts["link"] += 1
        return started(remote(src, dst, send_sem.at[i], recv_sem.at[i], peer))

    mine = pl.ds(pl.multiple_of(c * tokens_here, tokens_here), tokens_here)
    tok_copy = fetch(tokens.at[mine], tok_in)
    ws_copies = [fetch(ref.w_self, ws.at[0]), fetch(ref.o_self, os_.at[0])]
    bm[...] = jnp.zeros_like(bm)
    bm[0, 0:2, :hw] = ref.b_self[...]
    bm[0, 2:4, :hw] = ref.b_cross[...]
    bm[0, 8 : 8 + blocks, :ublk] = ref.b_up[...]
    colm[...] = jnp.zeros_like(colm)
    colm[0:3] = ref.norm_gain[...]
    colm[3:6] = ref.norm_shift[...]
    colm[6:9] = ref.out_bias[...]
    barrier = pltpu.get_barrier_semaphore()
    peers = [partner] + rings + lines
    for peer in peers:
        pl.semaphore_signal(barrier, inc=1, device_id=peer, device_id_type=MESH)
    pl.semaphore_wait(barrier, len(peers))
    ws_copies += [
        push(ref.w_self, ws.at[1], partner),
        push(bm.at[0], bm.at[1], partner),
        push(ref.o_self, os_.at[1], partner),
    ]
    def sentence(piece, i):
        start = (piece * 2 + c) * tokens_here + i * slots
        return encoder.at[pl.ds(pl.multiple_of(start, slots), slots)]

    columns = [slice(i * slots, (i + 1) * slots) for i in range(sents)]

    middle = (r == 1) | (r == 2)
    target, far = lax.rem(r + 2, 4), lax.rem(r + 1 + 2 * (2 - r), 4)
    merged = n_row == 4

    def block_to(i, k):
        peer = lines[k - 1]
        return remote(
            sentence(peer[0], i), enc.at[r, columns[i]], enc_s.at[i, k - 1], enc_r.at[i, k - 1], peer
        )

    def block_via(i):
        peer = (jnp.where(r == 0, 1, 2), d, c)
        return remote(sentence(3 - r, i), via.at[i], via_s.at[i], via_r.at[i], peer)

    def block_sum(i):
        return remote(
            via.at[i], enc.at[r, columns[i]], enc_s.at[i, 1], enc_r.at[i, 1], (target, d, c)
        )

    def block_near(i):
        return pltpu.make_async_copy(sentence(target, i), near, near_sem)

    own_blocks = []

    def send_far(i):
        own_blocks.append(fetch(sentence(r, i), enc.at[r, columns[i]]))
        if merged:

            @pl.when(middle)
            def _():
                block_near(i).start()

            @pl.when(jnp.logical_not(middle))
            def _():
                block_via(i).start()

    def send_blocks(i):
        if not merged:
            for k in range(1, n_row):
                block_to(i, k).start()
            return

        @pl.when(r != 3)
        def _():
            block_to(i, 1).start()

        @pl.when(r != 0)
        def _():
            block_to(i, 3).start()

        @pl.when(jnp.logical_not(middle))
        def _():
            block_to(i, 2).start()

    def send_sum(i):
        if merged:

            @pl.when(middle)
            def _():
                picks = [
                    jnp.full((1, width), layer_pick[target, j].astype(F32), F32)
                    for j in range(n_row)
                ]
                total = functools.reduce(jnp.add, picks)
                far_pick = jnp.full((1, width), layer_pick[target, far].astype(F32), F32)
                near_pick = jnp.full((1, width), layer_pick[target, r].astype(F32), F32)
                block_near(i).wait()
                block_via(i).wait_recv()
                via[i] = (
                    far_pick / total * via[i].astype(F32) + near_pick / total * near[...].astype(F32)
                ).astype(BF16)
                block_sum(i).start()

    def wait_blocks(i):
        own_blocks[i].wait()
        if not merged:
            for k in range(1, n_row):
                block_to(i, k).wait()
            return

        @pl.when(r != 3)
        def _():
            block_to(i, 1).wait_send()
            block_to(i, 3).wait_recv()

        @pl.when(r != 0)
        def _():
            block_to(i, 3).wait_send()
            block_to(i, 1).wait_recv()

        @pl.when(middle)
        def _():
            block_sum(i).wait_send()

        @pl.when(jnp.logical_not(middle))
        def _():
            block_to(i, 2).wait_send()
            block_via(i).wait_send()

        block_to(i, 2).wait_recv()

    send_far(0)
    if merged:

        @pl.when(r == 0)
        def _():
            enc[3] = jnp.zeros(enc.shape[1:], BF16)

        @pl.when(r == 3)
        def _():
            enc[0] = jnp.zeros(enc.shape[1:], BF16)

    wc_copies = [
        fetch(ref.w_cross, wc.at[0]),
        fetch(ref.o_cross, oc.at[0]),
        push(ref.w_cross, wc.at[1], partner),
        push(ref.o_cross, oc.at[1], partner),
    ]
    cot_copy = fetch(cotangent.at[mine], cot_in)
    ffn_copies = [
        push(ref.w_up, ref.up_in, partner),
        push(ref.w_down, ref.down_in, partner),
    ]

    cols[...] = colm[...].T
    gain, shift, obias = [[cols[:, j : j + 1] for j in range(3 * i, 3 * i + 3)] for i in range(3)]
    key_at = lax.broadcasted_iota(jnp.int32, (slots, slots), 0)
    query_at = lax.broadcasted_iota(jnp.int32, (slots, slots), 1)
    for zeroed in (attn1, attn2):
        zeroed[:, :first, :] = jnp.zeros((groups, first, tokens_here), BF16)
    grads[:, 3 * hw :, :] = jnp.zeros((groups, pad - 3 * hw, tokens_here), BF16)
    vec[...] = jnp.zeros_like(vec)
    bvec[...] = jnp.zeros_like(bvec)
    ubias[...] = jnp.zeros_like(ubias)
    heads_here, units_here = piece_heads[r], piece_ffn[r]
    group_at = [c, 1 - c]

    def head_on(g, h):
        return jnp.where(group_at[g] * per + h < heads_here, 1.0, 0.0)

    tok_copy.wait()
    tok_t[...] = tok_in[...].astype(F32).T.astype(BF16)
    layer_norm(tok_t, x1, gain[0], shift[0], 0, tokens_here)
    for copy in ws_copies:
        copy.wait()
    for g in range(groups):
        bcols[g] = bm[g, 0:8, : bcols.shape[1]].T
        bups[g] = bm[g, 8:16, :ublk].T
    for g in range(groups):
        at = slice(g * hw, (g + 1) * hw)
        q1[at] = (nn(ws[g, 0], x1[...]) + bcols[g, :hw, 0:1]).astype(BF16)
        k1[at] = nn(ws[g, 1], x1[...]).astype(BF16)
        v1[at] = (nn(ws[g, 2], x1[...]) + bcols[g, :hw, 1:2]).astype(BF16)
    send_blocks(0)
    masks = {
        i: (key_at <= query_at) & (key_at < tgt_len[c * sents + i]) for i in range(sents)
    }
    attend(q1, k1, v1, attn1, prob1, masks, head_on, hd, per, sents)
    send_sum(0)
    acc_a[...] = tn(os_[0], attn1[0, first:])
    for g in range(1, groups):
        acc_a[...] += tn(os_[g], attn1[g, first:])
    mid_t[...] = tok_t[...].astype(F32) + acc_a[...] + obias[0]
    layer_norm(mid_t, x2, gain[1], shift[1], 0, tokens_here)
    for copy in wc_copies:
        copy.wait()
    for g in range(groups):
        at = slice(g * hw, (g + 1) * hw)
        q2[at] = (nn(wc[g, 0], x2[...]) + bcols[g, :hw, 2:3]).astype(BF16)
    cot_copy.wait()
    ct[...] = cot_in[...].astype(F32).T.astype(BF16)

    picks = [
        jnp.full((1, width), layer_pick[r, i].astype(F32), F32) for i in range(layer_pick.shape[1])
    ]
    total = functools.reduce(jnp.add, picks)
    weights = [pick / total for pick in picks]
    if merged:
        summed = [False, r == 3, r == 0, False]
        absent = [r == 3, False, False, r == 0]
        weights = [
            jnp.where(one, 1.0, jnp.where(none, 0.0, weight))
            for one, none, weight in zip(summed, absent, weights)
        ]
    def cross(i):
        at = columns[i]
        wait_blocks(i)
        if i + 1 < sents:
            send_far(i + 1)
        if i > 0:
            send_memory(i - 1)
        memory = weights[0] * enc[0, at].astype(F32)
        for j in range(1, n_row):
            memory += weights[j] * enc[j, at].astype(F32)
        mem_t[:, at] = memory.T.astype(BF16)
        for g in range(groups):
            to = slice(g * hw, (g + 1) * hw)
            k2[to, at] = nn(wc[g, 1], mem_t[:, at]).astype(BF16)
            v2[to, at] = (nn(wc[g, 2], mem_t[:, at]) + bcols[g, :hw, 3:4]).astype(BF16)
        masks = {i: key_at < src_len[c * sents + i]}
        attend(q2, k2, v2, attn2, prob2, masks, head_on, hd, per, sents)
        branch = tn(oc[0], attn2[0, first:, at])
        for g in range(1, groups):
            branch += tn(oc[g], attn2[g, first:, at])
        late_t[:, at] = mid_t[:, at] + branch + obias[1]
        layer_norm(late_t, x3, gain[2], shift[2], at.start, at.stop)
        if i + 1 < sents:
            send_blocks(i + 1)

    def slot_of(phase, i):
        return lax.rem(phase * blocks + i, 3)

    def fetches(phase, i):
        slot, at = slot_of(phase, i), lanes(i, ublk)
        up, down = (ref.w_up, ref.w_down) if phase else (ref.up_in, ref.down_in)
        return [
            pltpu.make_async_copy(up.at[:, at], wu_buf.at[slot], fetch_sem.at[0, slot]),
            pltpu.make_async_copy(down.at[at, :], wd_buf.at[slot], fetch_sem.at[1, slot]),
        ]

    def pushes(i, k):
        at = lanes(i, ublk)
        return remote(
            (out_u, out_d)[k].at[:, :, at], came[2 + k].at[:, :, at],
            push_sem.at[k, i], land_sem.at[k, i], partner,
        )

    def feed_forward(n, ready):
        cols_at = columns[n]
        if n == 0:
            for copy in ready:
                copy.wait()
            for copy in fetches(0, 0):
                copy.start()
        acc_a[:, cols_at] = jnp.zeros((width, slots), F32)
        acc_b[:, cols_at] = jnp.zeros((width, slots), F32)

        def hidden(phase, i):
            g, slot, at = 1 - phase, slot_of(phase, i), lax.rem(i, 2)
            up, down = wu_buf.at[slot], wd_buf.at[slot]
            here = lax.broadcasted_iota(jnp.int32, bups.shape[1:], 1) == i
            h = nn(up[...].T, x3[:, cols_at]) + lane_sum(jnp.where(here, bups[g], 0.0))
            unit = group_at[g] * units + i * ublk
            unit = unit + lax.broadcasted_iota(jnp.int32, (ublk, 1), 0)
            on = jnp.where(unit < units_here, 1.0, 0.0)
            squared = h * h
            t = jnp.tanh(h * (0.7978845608028654 + 0.0356774081363001 * squared))
            cdf = 0.5 + 0.5 * t
            slope = cdf + h * (0.5 - 0.5 * t * t) * (
                0.7978845608028654 + 0.1070322244089003 * squared
            )
            act_buf[at] = (h * cdf * on).astype(BF16)
            dh = (nn(down[...], ct[:, cols_at]) * (slope * on)).astype(BF16)
            dh_buf[at] = dh
            in_sums = lax.broadcasted_iota(jnp.int32, ubias.shape[1:], 1) == i
            ubias[g] += jnp.where(in_sums, lane_sum(dh), 0.0)

        def spread_block(phase, i):
            slot, at = slot_of(phase, i), lax.rem(i, 2)
            sink_u, sink_d = (held[2], held[3]) if phase else (out_u, out_d)
            act, dh = act_buf[at], dh_buf[at]
            acc_a[:, cols_at] += tn(wd_buf[slot], act)
            acc_b[:, cols_at] += nn(wu_buf[slot], dh)
            shape, to = (n_row, rows, ublk), lanes(i, ublk)
            grad_u = nt(x3[:, cols_at], dh).reshape(shape)
            grad_d = nt(ct[:, cols_at], act).reshape(shape)
            if n > 0:
                grad_u += sink_u[:, :, to].astype(F32)
                grad_d += sink_d[:, :, to].astype(F32)
            sink_u[:, :, to] = grad_u.astype(BF16)
            sink_d[:, :, to] = grad_d.astype(BF16)

        def finished(i):
            if n + 1 == sents:
                for k in range(2):
                    pushes(i, k).start()

        for phase in range(2):
            more = phase == 0 or n + 1 < sents
            for copy in fetches(phase, 0):
                copy.wait()
            for copy in fetches(phase, 1):
                copy.start()
            hidden(phase, 0)
            if phase == 1:
                if n + 1 < sents:
                    send_sum(n + 1)
                spread_block(0, blocks - 1)
                finished(blocks - 1)

            @pl.loop(1, blocks)
            def _(i, phase=phase, more=more):
                for copy in fetches(phase, i):
                    copy.wait()

                @pl.when(i + 1 < blocks)
                def _():
                    for copy in fetches(phase, i + 1):
                        copy.start()

                if more:

                    @pl.when(i + 1 == blocks)
                    def _():
                        for copy in fetches(1 - phase, 0):
                            copy.start()

                hidden(phase, i)
                spread_block(phase, i - 1)
                if phase == 0:
                    finished(i - 1)

        spread_block(1, blocks - 1)
        tout[cols_at] = (late_t[:, cols_at] + acc_a[:, cols_at] + obias[2]).T
        norm_back(
            late_t, gain[2], acc_b, ct, acc_a, e_low, (sum_a, sum_b, sum_c),
            cols_at.start, cols_at.stop,
        )

    late = []
    half = rows // 2
    wide, start_of = window(half, half // 2)
    up, across = lax.div(d, 2), lax.rem(d, 2)
    ours = half * up + start_of(across)
    pieces = {
        "u": (2, 0, units, True),
        "d": (3, 0, units, False),
        "x_a": (1, 0, 2 * hw, True),
        "x_b": (1, 2 * hw, 4 * hw, False),
        "s_a": (0, 0, 2 * hw, True),
        "s_b": (0, 2 * hw, 4 * hw, False),
    }

    def add_in(part, begin, end, landing, places, shard=None):
        size = landing.shape[1]
        at = pl.ds(begin, end - begin)
        loads = [
            pltpu.make_async_copy(
                landing.at[z], abuf.at[z % 2, pl.ds(0, size), pl.ds(0, end - begin)],
                fetch_sem.at[0, z % 2],
            )
            for z in range(n_row)
        ]
        loads[0].start()
        for z in range(n_row):
            if z + 1 < n_row:
                loads[z + 1].start()
            loads[z].wait()
            for to, source, count in places:

                step = 80 if count % 80 == 0 else 48 if count % 48 == 0 else 16

                @pl.loop(0, count // step)
                def _(j, z=z, to=to, source=source, step=step):
                    held_at = pl.ds(pl.multiple_of(to + step * j, 16), step)
                    from_at = pl.ds(pl.multiple_of(source + step * j, 16), step)
                    total = held[part][z, held_at, at].astype(F32)
                    total += abuf[z % 2, from_at, pl.ds(0, end - begin)].astype(F32)
                    held[part][z, held_at, at] = total.astype(BF16)
                    if shard is not None:

                        @pl.when(r == z)
                        def _():
                            shard[from_at, at] = total

    def take(part, arrived):
        for copy in arrived:
            copy()
        add_in(part, 0, held[part].shape[2], came[part], [(0, 0, rows)])

    def first_ring(name):
        if not spread:
            return []
        part, begin, end, tall_first = pieces[name]
        landing, at = refs["ring_" + name], pl.ds(begin, end - begin)
        if tall_first:
            peer = (r, lax.rem(d + 2, 4), c)
            return [push(held[part].at[:, pl.ds(half * (1 - up), half), at], landing, peer)]
        peer = (r, d + 1 - 2 * across, c)
        return [
            push(
                held[part].at[:, pl.ds(half * i + start_of(1 - across), wide), at],
                landing.at[:, pl.ds(wide * i, wide)], peer,
            )
            for i in range(2)
        ]

    def second_ring(name, copies):
        if not spread:
            return []
        part, begin, end, tall_first = pieces[name]
        landing, at = refs["ring_" + name], pl.ds(begin, end - begin)
        for copy in copies:
            copy.wait()
        if tall_first:
            add_in(part, begin, end, landing, [(half * up, 0, half)])
            peer, gone = (r, d + 1 - 2 * across, c), half * up + start_of(1 - across)
        else:
            places = [(half * i + start_of(across), wide * i, wide) for i in range(2)]
            add_in(part, begin, end, landing, places)
            peer, gone = (r, lax.rem(d + 2, 4), c), half * (1 - up) + start_of(across)
        gone = pl.multiple_of(gone, 16)
        return [push(held[part].at[:, pl.ds(gone, wide), at], refs["turn_" + name], peer)]

    def to_lines(name, copies):
        if not spread:
            return []
        part, begin, end, _ = pieces[name]
        for copy in copies:
            copy.wait()
        shard = refs["shard_" + "sxud"[part]]
        add_in(part, begin, end, refs["turn_" + name], [(pl.multiple_of(ours, 16), 0, wide)], shard)
        if not merged:
            for k in range(1, n_row):
                line_to(name, k).start()
            return [name]

        @pl.when(jnp.logical_not(middle))
        def _():
            line_via(name).start()
            line_to(name, 2).start()

        @pl.when(r != 3)
        def _():
            line_to(name, 1).start()

        @pl.when(r != 0)
        def _():
            line_to(name, 3).start()

        return [name]

    def line_part(name):
        part, begin, end, _ = pieces[name]
        return part, pl.ds(pl.multiple_of(ours, 16), wide), pl.ds(begin, end - begin)

    def line_to(name, k):
        part, here, at = line_part(name)
        p = list(pieces).index(name)
        peer = lines[k - 1]
        return remote(
            held[part].at[peer[0], here, at], refs["line_" + "sxud"[part]].at[k - 1, :, at],
            link_s.at[p, k - 1], link_r.at[p, k - 1], peer,
        )

    def line_via(name):
        part, here, at = line_part(name)
        p = list(pieces).index(name)
        peer = (jnp.where(r == 0, 1, 2), d, c)
        return remote(
            held[part].at[3 - r, here, at], refs["far_" + "sxud"[part]].at[:, at],
            link_s.at[p, n_row - 1], link_r.at[p, n_row - 1], peer,
        )

    def line_sum(name):
        if spread and merged:

            @pl.when(middle)
            def _():
                part, here, at = line_part(name)
                line_via(name).wait_recv()
                total = held[part][target, here, at].astype(F32)
                total += refs["far_" + "sxud"[part]][:, at].astype(F32)
                held[part][target, here, at] = total.astype(BF16)
                line_to(name, 2).start()

    def sum_lines(part, names):
        if not spread:
            return
        shard, line = refs["shard_" + "sxud"[part]], refs["line_" + "sxud"[part]]

        def arrived(k):
            for name in names:
                line_to(name, k).wait_recv()
            shard[...] += line[k - 1].astype(F32)

        if not merged:
            for k in range(1, n_row):
                for name in names:
                    line_to(name, k).wait_send()
                arrived(k)
            return

        @pl.when(r != 0)
        def _():
            for name in names:
                line_to(name, 3).wait_send()
            arrived(1)

        @pl.when(r != 3)
        def _():
            for name in names:
                line_to(name, 1).wait_send()
            arrived(3)

        @pl.when(jnp.logical_not(middle))
        def _():
            for name in names:
                line_via(name).wait_send()

        for name in names:
            line_to(name, 2).wait_send()
        arrived(2)

    def heads_back(weight, at):
        for g in range(groups):
            for h in range(per):
                to = slice(h * hd, (h + 1) * hd)
                eh[g * hw + h * hd : g * hw + (h + 1) * hd, at] = (
                    nn(weight[g, to], e_low[:, at]) * head_on(g, h)
                ).astype(BF16)

    def cross_back(i):
        at = columns[i]
        heads_back(oc, at)
        attend_back(q2, k2, v2, eh, prob2, grads, (2 * hw, 0, hw), hd, per, sents, [i])
        total = jnp.zeros((width, slots), F32)
        for g in range(groups):
            total += tn(wc[g, 1], grads[g, :hw, at]) + tn(wc[g, 2], grads[g, hw : 2 * hw, at])
        tok_in[at] = total.T.astype(BF16)
        late.append(fetch(tok_in.at[at], glad.at[r, c, at]))
        late.append(push(tok_in.at[at], glad.at[r, c, at], partner))

    def memory_to(i, k):
        at = columns[i]
        return remote(
            tok_in.at[at], glad.at[r, c, at], mem_s.at[i, k - 1], mem_r.at[i, k - 1], lines[k - 1]
        )

    def memory_on(i):
        came_at = glad.at[lax.rem(r + 2, 4), c, columns[i]]
        peer, k = (jnp.where(r == 2, 3, 0), d, c), jnp.where(r == 2, 2, 0)
        return remote(came_at, came_at, mem_s.at[i, n_row - 1], mem_r.at[i, k], peer)

    def share_memory(i, k):
        came_at = glad.at[lax.rem(r + n_row - k, n_row), c, columns[i]]
        late.append(push(came_at, came_at, partner))

    def send_memory(i):
        if merged:

            @pl.when(r != 3)
            def _():
                memory_to(i, 1).start()

            @pl.when(r != 0)
            def _():
                memory_to(i, 3).start()

            memory_to(i, 2).start()
        else:
            for k in range(1, n_row):
                memory_to(i, k).start()

    def pass_memory(i):
        if merged:
            memory_to(i, 2).wait()

            @pl.when(middle)
            def _():
                memory_on(i).start()

            share_memory(i, 2)

    def wait_memory(i):
        if not merged:
            for k in range(1, n_row):
                memory_to(i, k).wait()
                share_memory(i, k)
            return

        @pl.when(r != 3)
        def _():
            memory_to(i, 1).wait_send()

        @pl.when(r != 0)
        def _():
            memory_to(i, 3).wait_send()

        @pl.when(middle)
        def _():
            memory_on(i).wait_send()

        for k in (1, 3):
            memory_to(i, k).wait_recv()
            share_memory(i, k)

    for i in range(sents):
        cross(i)
        feed_forward(i, ffn_copies)
        if i + 1 == sents:
            block_copies = [fetch(tout, ref.block), push(tout, ref.block_in, partner)]
            take(2, [pushes(j, 0).wait for j in range(blocks)])
            ring_u = first_ring("u")
            take(3, [pushes(j, 1).wait for j in range(blocks)])
            ring_d = first_ring("d")
        cross_back(i)
    for i in range(sents - 1):
        pass_memory(i)
    send_memory(sents - 1)
    vec[:, 8:9] = lane_sum(ct[...])
    vec[:, 2:3] = lane_sum(sum_a[...])
    vec[:, 5:6] = lane_sum(sum_b[...])
    vec[:, 7:8] = lane_sum(sum_c[...])

    def put(g, begin, value):
        sink = (held_now, out_now)[g]
        at = pl.ds(begin, value.shape[1])
        sink[:, :, at] = value.astype(BF16).reshape(n_row, rows, -1)

    def weight_grads(g, sources, attn):
        tail = nt(e_low[...], attn[g])
        begin = 0
        for source, end in sources:
            while begin < end:
                step = min(256, end - begin)
                value = nt(source[...], grads[g, begin : begin + step])
                if begin + step == pad:
                    keep = lead - begin
                    if keep:
                        put(g, begin, value[:, :keep])
                    put(g, lead, value[:, keep:] + tail[:, : pad - lead])
                else:
                    put(g, begin, value)
                begin += step
        put(g, pad, tail[:, pad - lead :])

    held_now, out_now = held[1], out_x
    for g in (1, 0):
        bvec[g, :hw, 2:3] = lane_sum(grads[g, 2 * hw : 3 * hw])
        bvec[g, :hw, 3:4] = lane_sum(grads[g, hw : 2 * hw])
        weight_grads(g, [(mem_t, 2 * hw), (x2, pad)], attn2)
        if g == 1:
            came_x = push(out_x, came[1], partner)
            acc_b[...] = tn(wc[g, 0], grads[g, 2 * hw : 3 * hw])
        else:
            acc_b[...] += tn(wc[g, 0], grads[g, 2 * hw : 3 * hw])
    norm_back(
        mid_t, gain[1], acc_b, acc_a, acc_a, e_low, (sum_a, sum_b, sum_c), 0, tokens_here
    )
    vec[:, 1:2] = lane_sum(sum_a[...])
    vec[:, 4:5] = lane_sum(sum_b[...])
    vec[:, 6:7] = lane_sum(sum_c[...])

    heads_back(os_, slice(0, tokens_here))
    attend_back(q1, k1, v1, eh, prob1, grads, (0, hw, 2 * hw), hd, per, sents, range(sents))
    held_now, out_now = held[0], out_s
    for g in (1, 0):
        bvec[g, :hw, 0:1] = lane_sum(grads[g, :hw])
        bvec[g, :hw, 1:2] = lane_sum(grads[g, 2 * hw : 3 * hw])
        weight_grads(g, [(x1, pad)], attn1)
        if g == 1:
            came_s = push(out_s, came[0], partner)
    for g in range(groups):
        for j in range(3):
            part = tn(ws[g, j], grads[g, j * hw : (j + 1) * hw])
            if g == 0 and j == 0:
                acc_b[...] = part
            else:
                acc_b[...] += part
    ring_u = second_ring("u", ring_u)
    ring_d = second_ring("d", ring_d)
    pass_memory(sents - 1)
    take(1, [came_x.wait])
    ring_x = [first_ring("x_a"), first_ring("x_b")]
    take(0, [came_s.wait])
    ring_s = [first_ring("s_a"), first_ring("s_b")]
    norm_back(
        tok_t, gain[0], acc_b, acc_a, acc_a, e_low, (sum_a, sum_b, sum_c), 0, tokens_here
    )
    vec[:, 0:1] = lane_sum(sum_a[...])
    vec[:, 3:4] = lane_sum(sum_b[...])
    for copy in block_copies:
        copy.wait()
    tout[...] = acc_a[...].T
    late += [fetch(tout, ref.gtok), push(tout, ref.gtok_in, partner)]

    small[...] = jnp.zeros_like(small)
    small[0:16, :] = vec[...].T[0:16]
    for g in range(groups):
        at = pl.multiple_of(16 + 8 * group_at[g], 8)
        small[pl.ds(at, 8), :hw] = bvec[g].T[0:8, :hw]
        small[pl.ds(at + 16, 8), :ublk] = ubias[g].T[0:8]
    if spread:
        small_mp, small_dp, small_row = (ref.small_mp, ref.small_dp, ref.small_row)
        push(small, small_mp, partner).wait()
        small_dp[d] = small[...] + small_mp[...]
        small_copies = [push(small_dp.at[d], small_dp.at[d], peer) for peer in rings]
        line_u = to_lines("u", ring_u)
        line_d = to_lines("d", ring_d)
        ring_x = [second_ring("x_a", ring_x[0]), second_ring("x_b", ring_x[1])]
        line_sum("u")
        line_sum("d")
        ring_s = [second_ring("s_a", ring_s[0]), second_ring("s_b", ring_s[1])]
        for copy in small_copies:
            copy.wait()
        total = small_dp[0]
        for j in range(1, n_dp):
            total += small_dp[j]
        small_row[r] = total
        small_copies = [push(small_row.at[r], small_row.at[r], peer) for peer in lines]
        line_x = to_lines("x_a", ring_x[0]) + to_lines("x_b", ring_x[1])
    for i in range(sents):
        wait_memory(i)
    if spread:
        line_s = to_lines("s_a", ring_s[0]) + to_lines("s_b", ring_s[1])
        for name in line_x + line_s:
            line_sum(name)
        sum_lines(2, line_u)
        sum_lines(3, line_d)
        sum_lines(1, line_x)
        for copy in small_copies:
            copy.wait()
        total = small_row[0]
        for j in range(1, n_row):
            total += small_row[j]
        small[...] = total
        sum_lines(0, line_s)
    for copy in late:
        copy.wait()


def layer(n_row, n_dp, scalars, vectors, arrays):
    shape = jax.ShapeDtypeStruct
    encoder, w_self, w_up = arrays["encoder"], arrays["w_self"], arrays["w_up"]
    width, tokens = encoder.shape[1], arrays["tokens"].shape[0] // 2
    hw, units = w_self.shape[1], w_up.shape[1]
    blocks, ublk = vectors["b_up"].shape
    sents = scalars["tgt_len"].shape[0] // 2
    slots, heads = tokens // sents, 2 * hw // HD
    pad, first = -(-3 * hw // 128) * 128, 3 * hw % 128
    rows = width // n_row
    spread = n_dp == 4
    wide, _ = window(rows // 2, rows // 4)
    sizes = {"s": 4 * hw, "x": 4 * hw, "u": units, "d": units}
    outs = {
        "block": ((tokens, width), F32, ANY),
        "block_in": ((tokens, width), F32, ANY),
        "gtok": ((tokens, width), F32, ANY),
        "gtok_in": ((tokens, width), F32, ANY),
        "glad": ((n_row, 2, tokens, width), BF16, ANY),
        "small": ((48, width), F32, VMEM),
        "up_in": (w_up.shape, BF16, ANY),
        "down_in": (arrays["w_down"].shape, BF16, ANY),
    }
    scratch = {}
    for name, size in sizes.items():
        outs["came_" + name] = ((n_row, rows, size), BF16, ANY)
        if spread:
            for piece in (name,) if name in "ud" else (name + "_a", name + "_b"):
                tall_first = piece == "u" or piece[-1] == "a"
                cols_of = size if name in "ud" else size // 2
                landing = rows // 2 if tall_first else 2 * wide
                outs["ring_" + piece] = ((n_row, landing, cols_of), BF16, ANY)
                outs["turn_" + piece] = ((n_row, wide, cols_of), BF16, ANY)
            outs["shard_" + name] = ((wide, size), F32, VMEM)
            scratch["held_" + name] = pltpu.VMEM((n_row, rows, size), BF16)
            scratch["line_" + name] = pltpu.VMEM((n_row - 1, wide, size), BF16)
            scratch["far_" + name] = pltpu.VMEM((wide, size), BF16)
        else:
            outs["held_" + name] = ((n_row, rows, size), BF16, VMEM)
    tall, low = pltpu.VMEM((width, tokens), F32), pltpu.VMEM((width, tokens), BF16)
    flat = pltpu.VMEM((tokens, width), BF16)
    scratch["ws"] = scratch["wc"] = pltpu.VMEM((2,) + w_self.shape, BF16)
    scratch["os"] = scratch["oc"] = pltpu.VMEM((2, hw, width), BF16)
    scratch["wu_buf"] = pltpu.VMEM((3, width, ublk), BF16)
    scratch["wd_buf"] = pltpu.VMEM((3, ublk, width), BF16)
    scratch["act_buf"] = scratch["dh_buf"] = pltpu.VMEM((2, ublk, slots), BF16)
    scratch["out_u"] = scratch["out_d"] = pltpu.VMEM((n_row, rows, units), BF16)
    scratch["out_s"] = scratch["out_x"] = pltpu.VMEM((n_row, rows, 4 * hw), BF16)
    scratch["abuf"] = pltpu.VMEM((2, rows, max(sizes.values())), BF16)
    scratch["tok_in"] = scratch["cot_in"] = flat
    scratch["enc"] = pltpu.VMEM((n_row, tokens, width), BF16)
    scratch["tout"] = pltpu.VMEM((tokens, width), F32)
    for name in ("mid_t", "late_t", "acc_a", "acc_b"):
        scratch[name] = tall
    for name in ("tok_t", "x1", "x2", "x3", "ct", "mem_t", "e_low"):
        scratch[name] = low
    for name in ("q1", "k1", "v1", "q2", "k2", "v2", "eh"):
        scratch[name] = pltpu.VMEM((2 * hw, tokens), BF16)
    for name in ("attn1", "attn2"):
        scratch[name] = pltpu.VMEM((2, first + hw, tokens), BF16)
    for name in ("prob1", "prob2"):
        scratch[name] = pltpu.VMEM((heads * sents, slots, slots), BF16)
    scratch["grads"] = pltpu.VMEM((2, pad, tokens), BF16)
    for name in ("sum_a", "sum_b", "sum_c", "vec", "cols"):
        scratch[name] = pltpu.VMEM((width, 128), F32)
    scratch["colm"] = pltpu.VMEM((128, width), F32)
    scratch["bm"] = pltpu.VMEM((2, 16, width), F32)
    scratch["bvec"] = pltpu.VMEM((2, -(-hw // 128) * 128, 128), F32)
    scratch["bcols"] = pltpu.VMEM((2, -(-hw // 128) * 128, 8), F32)
    scratch["ubias"] = pltpu.VMEM((2, ublk, 128), F32)
    scratch["bups"] = pltpu.VMEM((2, ublk, 8), F32)
    if spread:
        scratch["small_mp"] = pltpu.VMEM((48, width), F32)
        scratch["small_dp"] = pltpu.VMEM((n_dp, 48, width), F32)
        scratch["small_row"] = pltpu.VMEM((n_row, 48, width), F32)
    dma = pltpu.SemaphoreType.DMA
    scratch["via"] = pltpu.VMEM((sents, slots, width), BF16)
    scratch["near"] = pltpu.VMEM((slots, width), BF16)
    scratch["near_sem"] = dma
    scratch["enc_s"] = scratch["enc_r"] = dma((sents, n_row - 1))
    scratch["via_s"] = scratch["via_r"] = dma((sents,))
    scratch["mem_s"] = scratch["mem_r"] = dma((sents, n_row))
    scratch["link_s"] = scratch["link_r"] = dma((6, n_row))
    scratch["local_sem"] = dma((16,))
    scratch["send_sem"] = scratch["recv_sem"] = dma((80,))
    scratch["fetch_sem"] = dma((2, 3))
    scratch["push_sem"] = scratch["land_sem"] = dma((2, blocks))
    names = list(scalars) + list(vectors) + list(arrays) + list(outs) + list(scratch)
    smem = pl.BlockSpec(memory_space=pltpu.SMEM)
    results = pl.pallas_call(
        functools.partial(layer_kernel, n_row, n_dp, names),
        out_shape=tuple(shape(s, t) for s, t, _ in outs.values()),
        in_specs=[smem] * len(scalars) + [VMEM] * len(vectors) + [ANY] * len(arrays),
        out_specs=tuple(spec for _, _, spec in outs.values()),
        scratch_shapes=list(scratch.values()),
        compiler_params=pltpu.CompilerParams(
            collective_id=0, has_side_effects=True, vmem_limit_bytes=63 << 20
        ),
    )(*scalars.values(), *vectors.values(), *arrays.values())
    return dict(zip(outs, results))


def per_device(
    tokens, encoder, layer_pick, piece_heads, piece_ffn, tgt_len, src_len, norm_gain, norm_shift,
    out_bias, w_self, o_self, b_self, w_cross, o_cross, b_cross, w_up, b_up, w_down, cotangent,
):
    n_row, n_dp = lax.axis_size("row"), lax.axis_size("dp")
    r, d, c = place()
    width = tokens.shape[1]
    units, hw = w_up.shape[1], w_self.shape[2]
    ublk = 256
    out = layer(
        n_row, n_dp,
        dict(
            layer_pick=layer_pick, piece_heads=piece_heads, piece_ffn=piece_ffn,
            tgt_len=tgt_len, src_len=src_len,
        ),
        dict(
            norm_gain=norm_gain, norm_shift=norm_shift, out_bias=out_bias,
            b_self=b_self, b_cross=b_cross, b_up=b_up.reshape(-1, ublk),
        ),
        dict(
            tokens=tokens, cotangent=cotangent, encoder=encoder.reshape(-1, width),
            w_self=jnp.swapaxes(w_self, 1, 2), o_self=o_self,
            w_cross=jnp.swapaxes(w_cross, 1, 2), o_cross=o_cross, w_up=w_up, w_down=w_down,
        ),
    )
    share = width // n_row // n_dp
    small = out["small"]
    if n_dp == 4:
        _, start_of = window(2 * share, share)
        across = lax.rem(d, 2)
        shards = [
            lax.dynamic_slice_in_dim(
                out["shard_" + name], share * across - start_of(across), share
            )
            for name in "sxud"
        ]
    else:
        shards = [
            lax.psum_scatter(
                out["held_" + name].astype(F32).reshape(width, -1),
                ("row", "dp"), scatter_dimension=0, tiled=True,
            )
            for name in "sxud"
        ]
        small = lax.psum(small, ("row", "dp", "mp"))

    def both(mine, other):
        return jnp.where(
            c == 0, jnp.concatenate([mine, other]), jnp.concatenate([other, mine])
        )

    mine = lax.dynamic_index_in_dim(layer_pick, r, 1, keepdims=False).astype(F32)
    totals = jnp.sum(layer_pick.astype(F32), axis=1)
    grad_encoder = (mine / totals)[:, None, None, None] * out["glad"].astype(F32)
    at = (r * n_dp + d) * share
    norms = lax.dynamic_slice_in_dim(small[:9], at, share, axis=1)
    heads = lax.dynamic_slice_in_dim(small, 16 + 8 * c, 8)[:4, :hw]
    ups = lax.dynamic_slice_in_dim(small, 32 + 8 * c, 8)[: units // ublk, :ublk]
    cut = lambda v, i: v[:, i * hw : (i + 1) * hw]
    w_s, w_x, w_u, w_d = shards
    return (
        both(out["block"], out["block_in"]),
        both(out["gtok"], out["gtok_in"]),
        grad_encoder.reshape(1, -1, width),
        norms[0:3],
        norms[3:6],
        norms[6:9],
        jnp.stack([cut(w_s, 0), cut(w_s, 1), cut(w_s, 2)]),
        cut(w_s, 3).T,
        heads[0:2],
        jnp.stack([cut(w_x, 2), cut(w_x, 0), cut(w_x, 1)]),
        cut(w_x, 3).T,
        heads[2:4],
        w_u,
        ups.reshape(units),
        w_d.T,
    )


def solution(mesh):
    return jax.shard_map(
        per_device,
        mesh=mesh,
        in_specs=(
            P(("row", "dp"), None),
            P("row", "dp", None),
            P(),
            P(),
            P(),
            P(("row", "dp")),
            P(("row", "dp")),
            P(),
            P(),
            P(),
            P(None, None, "mp"),
            P("mp", None),
            P(None, "mp"),
            P(None, None, "mp"),
            P("mp", None),
            P(None, "mp"),
            P(None, "mp"),
            P("mp"),
            P("mp", None),
            P(("row", "dp"), None),
        ),
        out_specs=(
            P(("row", "dp"), None),
            P(("row", "dp"), None),
            P("row", "dp", None),
            P(None, ("row", "dp")),
            P(None, ("row", "dp")),
            P(None, ("row", "dp")),
            P(None, ("row", "dp"), "mp"),
            P("mp", ("row", "dp")),
            P(None, "mp"),
            P(None, ("row", "dp"), "mp"),
            P("mp", ("row", "dp")),
            P(None, "mp"),
            P(("row", "dp"), "mp"),
            P("mp"),
            P("mp", ("row", "dp")),
        ),
        check_vma=False,
    )
```

```python
import functools
import types
import jax
import jax.numpy as jnp
from jax import lax
from jax.experimental import pallas as pl
from jax.experimental.pallas import tpu as pltpu
from jax.sharding import PartitionSpec as P

HD = 80
EPSILON = 1e-05
MASKED = -1e30
F32, BF16 = jnp.float32, jnp.bfloat16
MESH = pl.DeviceIdType.MESH
ANY = pl.BlockSpec(memory_space=pl.ANY)
VMEM = pl.BlockSpec(memory_space=pltpu.VMEM)


def nn(a, b):
    return lax.dot_general(a, b, (((1,), (0,)), ((), ())), preferred_element_type=F32)


def nt(a, b):
    return lax.dot_general(a, b, (((1,), (1,)), ((), ())), preferred_element_type=F32)


def tn(a, b):
    return lax.dot_general(a, b, (((0,), (0,)), ((), ())), preferred_element_type=F32)


def lanes(i, n):
    return pl.ds(pl.multiple_of(i * n, n), n)


def layer_norm(v_ref, x_ref, gain, shift, begin, end):
    @pl.loop(begin // 128, end // 128)
    def _(i):
        v = v_ref[:, lanes(i, 128)].astype(F32)
        c = v - jnp.mean(v, axis=0, keepdims=True)
        r = lax.rsqrt(jnp.mean(c * c, axis=0, keepdims=True) + EPSILON)
        x_ref[:, lanes(i, 128)] = (c * r * gain + shift).astype(BF16)


def norm_back(v_ref, gain, up_ref, base_ref, out_ref, low_ref, sums, begin, end):
    gain_sum, shift_sum, bias_sum = sums
    if begin == 0:
        for ref in sums:
            ref[...] = jnp.zeros_like(ref)

    @pl.loop(begin // 128, end // 128)
    def _(i):
        at = lanes(i, 128)
        v = v_ref[:, at].astype(F32)
        c = v - jnp.mean(v, axis=0, keepdims=True)
        r = lax.rsqrt(jnp.mean(c * c, axis=0, keepdims=True) + EPSILON)
        xhat = c * r
        e = up_ref[:, at]
        gain_sum[...] += e * xhat
        shift_sum[...] += e
        eg = e * gain
        m1 = jnp.mean(eg, axis=0, keepdims=True)
        m2 = jnp.mean(eg * xhat, axis=0, keepdims=True)
        out = base_ref[:, at].astype(F32) + r * (eg - m1 - xhat * m2)
        out_ref[:, at] = out
        low = out.astype(BF16)
        low_ref[:, at] = low
        bias_sum[...] += low.astype(F32)


def attend(q_ref, k_ref, v_ref, out_ref, prob_ref, masks, head_on, hd, per, sents):
    groups, slots = out_ref.shape[0], q_ref.shape[1] // sents
    first = out_ref.shape[1] - per * hd
    for g in range(groups):

        @pl.loop(0, per, unroll=2)
        def _(h, g=g):
            rows = pl.ds(pl.multiple_of((g * per + h) * hd, 16), hd)
            to = pl.ds(pl.multiple_of(first + h * hd, 16), hd)
            for s, mask in masks.items():
                at = slice(s * slots, (s + 1) * slots)
                scores = tn(k_ref[rows, at], q_ref[rows, at]) * hd ** (-0.5)
                scores = jnp.where(mask, scores, MASKED)
                e = jnp.exp(scores - jnp.max(scores, axis=0, keepdims=True))
                total = jnp.sum(e, axis=0, keepdims=True)
                p = (e * (1.0 / total)).astype(BF16)
                prob_ref[(g * per + h) * sents + s] = p
                mixed = nn(v_ref[rows, at], p) * head_on(g, h)
                out_ref[g, to, at] = mixed.astype(BF16)


def attend_back(q_ref, k_ref, v_ref, e_ref, prob_ref, d_ref, at_rows, hd, per, sents, some):
    groups, slots = d_ref.shape[0], q_ref.shape[1] // sents
    for g in range(groups):

        @pl.loop(0, per, unroll=2)
        def _(h, g=g):
            rows = pl.ds(pl.multiple_of((g * per + h) * hd, 16), hd)
            dq_at, dk_at, dv_at = [
                pl.ds(pl.multiple_of(first + h * hd, 16), hd) for first in at_rows
            ]
            for s in some:
                at = slice(s * slots, (s + 1) * slots)
                e, p = e_ref[rows, at], prob_ref[(g * per + h) * sents + s]
                d_ref[g, dv_at, at] = nt(e, p).astype(BF16)
                dp = tn(v_ref[rows, at], e)
                pf = p.astype(F32)
                delta = jnp.sum(pf * dp, axis=0, keepdims=True)
                ds = (pf * (dp - delta) * hd ** (-0.5)).astype(BF16)
                d_ref[g, dq_at, at] = nn(k_ref[rows, at], ds).astype(BF16)
                d_ref[g, dk_at, at] = nt(q_ref[rows, at], ds).astype(BF16)


def lane_sum(values):
    return jnp.sum(values.astype(F32), axis=1, keepdims=True)


def place():
    return tuple(lax.axis_index(name) for name in ("row", "dp", "mp"))


def window(rows, share):
    wide = max(
        -(-(i + 1) * share // 16) * 16 - i * share // 16 * 16 for i in range(rows // share)
    )
    return wide, lambda i: pl.multiple_of(
        jnp.minimum(i * share // 16 * 16, rows - wide), 16
    )


def remote(src, dst, send_sem, recv_sem, peer):
    return pltpu.make_async_remote_copy(
        src_ref=src, dst_ref=dst, send_sem=send_sem, recv_sem=recv_sem,
        device_id=peer, device_id_type=MESH,
    )


def started(copy):
    copy.start()
    return copy


def layer_kernel(n_row, n_dp, names, *args):
    refs = dict(zip(names, args))
    ref = types.SimpleNamespace(**refs)
    layer_pick, piece_heads, piece_ffn, tgt_len, src_len = (ref.layer_pick, ref.piece_heads, ref.piece_ffn, ref.tgt_len, ref.src_len)
    tokens, cotangent, encoder = (ref.tokens, ref.cotangent, ref.encoder)
    ws, wc, os_, oc, wu_buf, wd_buf = (ref.ws, ref.wc, ref.os, ref.oc, ref.wu_buf, ref.wd_buf)
    act_buf, dh_buf, load_sem = ref.act_buf, ref.dh_buf, ref.load_sem
    via, near, near_sem = ref.via, ref.near, ref.near_sem
    enc_s, enc_r, via_s, via_r = ref.enc_s, ref.enc_r, ref.via_s, ref.via_r
    mem_s, mem_r, link_s, link_r = ref.mem_s, ref.mem_r, ref.link_s, ref.link_r
    tok_in, cot_in, enc, tout, tok_t, mid_t, late_t, acc_a, acc_b = (ref.tok_in, ref.cot_in, ref.enc, ref.tout, ref.tok_t, ref.mid_t, ref.late_t, ref.acc_a, ref.acc_b)
    x1, x2, x3, ct, mem_t, e_low, eh = (ref.x1, ref.x2, ref.x3, ref.ct, ref.mem_t, ref.e_low, ref.eh)
    q1, k1, v1, q2, k2, v2 = (ref.q1, ref.k1, ref.v1, ref.q2, ref.k2, ref.v2)
    attn1, attn2, prob1, prob2, grads = (ref.attn1, ref.attn2, ref.prob1, ref.prob2, ref.grads)
    sum_a, sum_b, sum_c, vec, bvec, ubias, colm, cols, bm, bcols, bups = (ref.sum_a, ref.sum_b, ref.sum_c, ref.vec, ref.bvec, ref.ubias, ref.colm, ref.cols, ref.bm, ref.bcols, ref.bups)
    out_s, out_x, out_u, out_d, abuf = (ref.out_s, ref.out_x, ref.out_u, ref.out_d, ref.abuf)
    local_sem, send_sem, recv_sem, fetch_sem, push_sem, land_sem = (ref.local_sem, ref.send_sem, ref.recv_sem, ref.fetch_sem, ref.push_sem, ref.land_sem)
    held, came = (ref.held_s, ref.held_x, ref.held_u, ref.held_d), (ref.came_s, ref.came_x, ref.came_u, ref.came_d)
    small, glad = (ref.small, ref.glad)
    spread = n_dp == 4

    width, tokens_here = tok_t.shape
    groups, _, hw, _ = ws.shape
    units, ublk, hd = ref.w_up.shape[1], bups.shape[1], HD
    blocks, per = units // ublk, hw // HD
    rows = width // n_row
    sents = tgt_len.shape[0] // 2
    slots = tokens_here // sents
    pad = -(-3 * hw // 128) * 128
    lead = 3 * hw // 128 * 128
    first = 3 * hw - lead
    r, d, c = place()
    partner = (r, d, 1 - c)
    rings = [(r, lax.rem(d + i, n_dp), c) for i in range(1, n_dp)] if spread else []
    lines = [(lax.rem(r + i, n_row), d, c) for i in range(1, n_row)]
    counts = {"local": 0, "link": 0}

    def fetch(src, dst):
        i = counts["local"]
        counts["local"] += 1
        return started(pltpu.make_async_copy(src, dst, local_sem.at[i]))

    def push(src, dst, peer):
        i = counts["link"]
        counts["link"] += 1
        return started(remote(src, dst, send_sem.at[i], recv_sem.at[i], peer))

    mine = pl.ds(pl.multiple_of(c * tokens_here, tokens_here), tokens_here)
    tok_copy = fetch(tokens.at[mine], tok_in)
    ws_copies = [fetch(ref.w_self, ws.at[0]), fetch(ref.o_self, os_.at[0])]
    bm[...] = jnp.zeros_like(bm)
    bm[0, 0:2, :hw] = ref.b_self[...]
    bm[0, 2:4, :hw] = ref.b_cross[...]
    bm[0, 8 : 8 + blocks, :ublk] = ref.b_up[...]
    colm[...] = jnp.zeros_like(colm)
    colm[0:3] = ref.norm_gain[...]
    colm[3:6] = ref.norm_shift[...]
    colm[6:9] = ref.out_bias[...]
    barrier = pltpu.get_barrier_semaphore()
    peers = [partner] + rings + lines
    for peer in peers:
        pl.semaphore_signal(barrier, inc=1, device_id=peer, device_id_type=MESH)
    pl.semaphore_wait(barrier, len(peers))
    ws_copies += [
        push(ref.w_self, ws.at[1], partner),
        push(bm.at[0], bm.at[1], partner),
        push(ref.o_self, os_.at[1], partner),
    ]
    def sentence(piece, i):
        start = (piece * 2 + c) * tokens_here + i * slots
        return encoder.at[pl.ds(pl.multiple_of(start, slots), slots)]

    columns = [slice(i * slots, (i + 1) * slots) for i in range(sents)]

    middle = (r == 1) | (r == 2)
    target, far = lax.rem(r + 2, 4), lax.rem(r + 1 + 2 * (2 - r), 4)
    merged = n_row == 4

    def block_to(i, k):
        peer = lines[k - 1]
        return remote(
            sentence(peer[0], i), enc.at[r, columns[i]], enc_s.at[i, k - 1], enc_r.at[i, k - 1], peer
        )

    def block_via(i):
        peer = (jnp.where(r == 0, 1, 2), d, c)
        return remote(sentence(3 - r, i), via.at[i], via_s.at[i], via_r.at[i], peer)

    def block_sum(i):
        return remote(
            via.at[i], enc.at[r, columns[i]], enc_s.at[i, 1], enc_r.at[i, 1], (target, d, c)
        )

    def block_near(i):
        return pltpu.make_async_copy(sentence(target, i), near, near_sem)

    own_blocks = []

    def send_far(i):
        own_blocks.append(fetch(sentence(r, i), enc.at[r, columns[i]]))
        if merged:

            @pl.when(middle)
            def _():
                block_near(i).start()

            @pl.when(jnp.logical_not(middle))
            def _():
                block_via(i).start()

    def send_blocks(i):
        if not merged:
            for k in range(1, n_row):
                block_to(i, k).start()
            return

        @pl.when(r != 3)
        def _():
            block_to(i, 1).start()

        @pl.when(r != 0)
        def _():
            block_to(i, 3).start()

        @pl.when(jnp.logical_not(middle))
        def _():
            block_to(i, 2).start()

    def send_sum(i):
        if merged:

            @pl.when(middle)
            def _():
                picks = [
                    jnp.full((1, width), layer_pick[target, j].astype(F32), F32)
                    for j in range(n_row)
                ]
                total = functools.reduce(jnp.add, picks)
                far_pick = jnp.full((1, width), layer_pick[target, far].astype(F32), F32)
                near_pick = jnp.full((1, width), layer_pick[target, r].astype(F32), F32)
                block_near(i).wait()
                block_via(i).wait_recv()
                via[i] = (
                    far_pick / total * via[i].astype(F32) + near_pick / total * near[...].astype(F32)
                ).astype(BF16)
                block_sum(i).start()

    def wait_blocks(i):
        own_blocks[i].wait()
        if not merged:
            for k in range(1, n_row):
                block_to(i, k).wait()
            return

        @pl.when(r != 3)
        def _():
            block_to(i, 1).wait_send()
            block_to(i, 3).wait_recv()

        @pl.when(r != 0)
        def _():
            block_to(i, 3).wait_send()
            block_to(i, 1).wait_recv()

        @pl.when(middle)
        def _():
            block_sum(i).wait_send()

        @pl.when(jnp.logical_not(middle))
        def _():
            block_to(i, 2).wait_send()
            block_via(i).wait_send()

        block_to(i, 2).wait_recv()

    send_far(0)
    if merged:

        @pl.when(r == 0)
        def _():
            enc[3] = jnp.zeros(enc.shape[1:], BF16)

        @pl.when(r == 3)
        def _():
            enc[0] = jnp.zeros(enc.shape[1:], BF16)

    wc_copies = [
        fetch(ref.w_cross, wc.at[0]),
        fetch(ref.o_cross, oc.at[0]),
        push(ref.w_cross, wc.at[1], partner),
        push(ref.o_cross, oc.at[1], partner),
    ]
    cot_copy = fetch(cotangent.at[mine], cot_in)
    ffn_copies = [
        push(ref.w_up, ref.up_in, partner),
        push(ref.w_down, ref.down_in, partner),
    ]

    cols[...] = colm[...].T
    gain, shift, obias = [[cols[:, j : j + 1] for j in range(3 * i, 3 * i + 3)] for i in range(3)]
    key_at = lax.broadcasted_iota(jnp.int32, (slots, slots), 0)
    query_at = lax.broadcasted_iota(jnp.int32, (slots, slots), 1)
    for zeroed in (attn1, attn2):
        zeroed[:, :first, :] = jnp.zeros((groups, first, tokens_here), BF16)
    grads[:, 3 * hw :, :] = jnp.zeros((groups, pad - 3 * hw, tokens_here), BF16)
    vec[...] = jnp.zeros_like(vec)
    bvec[...] = jnp.zeros_like(bvec)
    ubias[...] = jnp.zeros_like(ubias)
    heads_here, units_here = piece_heads[r], piece_ffn[r]
    group_at = [c, 1 - c]

    def head_on(g, h):
        return jnp.where(group_at[g] * per + h < heads_here, 1.0, 0.0)

    tok_copy.wait()
    tok_t[...] = tok_in[...].astype(F32).T.astype(BF16)
    layer_norm(tok_t, x1, gain[0], shift[0], 0, tokens_here)
    for copy in ws_copies:
        copy.wait()
    for g in range(groups):
        bcols[g] = bm[g, 0:8, : bcols.shape[1]].T
        bups[g] = bm[g, 8:16, :ublk].T
    for g in range(groups):
        at = slice(g * hw, (g + 1) * hw)
        q1[at] = (nn(ws[g, 0], x1[...]) + bcols[g, :hw, 0:1]).astype(BF16)
        k1[at] = nn(ws[g, 1], x1[...]).astype(BF16)
        v1[at] = (nn(ws[g, 2], x1[...]) + bcols[g, :hw, 1:2]).astype(BF16)
    send_blocks(0)
    masks = {
        i: (key_at <= query_at) & (key_at < tgt_len[c * sents + i]) for i in range(sents)
    }
    attend(q1, k1, v1, attn1, prob1, masks, head_on, hd, per, sents)
    send_sum(0)
    acc_a[...] = tn(os_[0], attn1[0, first:])
    for g in range(1, groups):
        acc_a[...] += tn(os_[g], attn1[g, first:])
    mid_t[...] = tok_t[...].astype(F32) + acc_a[...] + obias[0]
    layer_norm(mid_t, x2, gain[1], shift[1], 0, tokens_here)
    for copy in wc_copies:
        copy.wait()
    for g in range(groups):
        at = slice(g * hw, (g + 1) * hw)
        q2[at] = (nn(wc[g, 0], x2[...]) + bcols[g, :hw, 2:3]).astype(BF16)
    cot_copy.wait()
    ct[...] = cot_in[...].astype(F32).T.astype(BF16)

    picks = [
        jnp.full((1, width), layer_pick[r, i].astype(F32), F32) for i in range(layer_pick.shape[1])
    ]
    total = functools.reduce(jnp.add, picks)
    weights = [pick / total for pick in picks]
    if merged:
        summed = [False, r == 3, r == 0, False]
        absent = [r == 3, False, False, r == 0]
        weights = [
            jnp.where(one, 1.0, jnp.where(none, 0.0, weight))
            for one, none, weight in zip(summed, absent, weights)
        ]
    def cross(i):
        at = columns[i]
        wait_blocks(i)
        if i + 1 < sents:
            send_far(i + 1)
        if i > 0:
            send_memory(i - 1)
        memory = weights[0] * enc[0, at].astype(F32)
        for j in range(1, n_row):
            memory += weights[j] * enc[j, at].astype(F32)
        mem_t[:, at] = memory.T.astype(BF16)
        for g in range(groups):
            to = slice(g * hw, (g + 1) * hw)
            k2[to, at] = nn(wc[g, 1], mem_t[:, at]).astype(BF16)
            v2[to, at] = (nn(wc[g, 2], mem_t[:, at]) + bcols[g, :hw, 3:4]).astype(BF16)
        masks = {i: key_at < src_len[c * sents + i]}
        attend(q2, k2, v2, attn2, prob2, masks, head_on, hd, per, sents)
        branch = tn(oc[0], attn2[0, first:, at])
        for g in range(1, groups):
            branch += tn(oc[g], attn2[g, first:, at])
        late_t[:, at] = mid_t[:, at] + branch + obias[1]
        layer_norm(late_t, x3, gain[2], shift[2], at.start, at.stop)
        if i + 1 < sents:
            send_blocks(i + 1)

    def slot_of(phase, i):
        return lax.rem(phase * blocks + i, 3)

    def fetches(phase, i):
        slot, at = slot_of(phase, i), lanes(i, ublk)
        up, down = (ref.w_up, ref.w_down) if phase else (ref.up_in, ref.down_in)
        return [
            pltpu.make_async_copy(up.at[:, at], wu_buf.at[slot], fetch_sem.at[0, slot]),
            pltpu.make_async_copy(down.at[at, :], wd_buf.at[slot], fetch_sem.at[1, slot]),
        ]

    def pushes(i, k):
        at = lanes(i, ublk)
        return remote(
            (out_u, out_d)[k].at[:, :, at], came[2 + k].at[:, :, at],
            push_sem.at[k, i], land_sem.at[k, i], partner,
        )

    def feed_forward(n, ready):
        cols_at = columns[n]
        if n == 0:
            for copy in ready:
                copy.wait()
            for copy in fetches(0, 0):
                copy.start()
        acc_a[:, cols_at] = jnp.zeros((width, slots), F32)
        acc_b[:, cols_at] = jnp.zeros((width, slots), F32)

        def hidden(phase, i):
            g, slot, at = 1 - phase, slot_of(phase, i), lax.rem(i, 2)
            up, down = wu_buf.at[slot], wd_buf.at[slot]
            here = lax.broadcasted_iota(jnp.int32, bups.shape[1:], 1) == i
            h = nn(up[...].T, x3[:, cols_at]) + lane_sum(jnp.where(here, bups[g], 0.0))
            unit = group_at[g] * units + i * ublk
            unit = unit + lax.broadcasted_iota(jnp.int32, (ublk, 1), 0)
            on = jnp.where(unit < units_here, 1.0, 0.0)
            squared = h * h
            t = jnp.tanh(h * (0.7978845608028654 + 0.0356774081363001 * squared))
            cdf = 0.5 + 0.5 * t
            slope = cdf + h * (0.5 - 0.5 * t * t) * (
                0.7978845608028654 + 0.1070322244089003 * squared
            )
            act_buf[at] = (h * cdf * on).astype(BF16)
            dh = (nn(down[...], ct[:, cols_at]) * (slope * on)).astype(BF16)
            dh_buf[at] = dh
            in_sums = lax.broadcasted_iota(jnp.int32, ubias.shape[1:], 1) == i
            ubias[g] += jnp.where(in_sums, lane_sum(dh), 0.0)

        def spread_block(phase, i):
            slot, at = slot_of(phase, i), lax.rem(i, 2)
            sink_u, sink_d = (held[2], held[3]) if phase else (out_u, out_d)
            act, dh = act_buf[at], dh_buf[at]
            acc_a[:, cols_at] += tn(wd_buf[slot], act)
            acc_b[:, cols_at] += nn(wu_buf[slot], dh)
            shape, to = (n_row, rows, ublk), lanes(i, ublk)
            grad_u = nt(x3[:, cols_at], dh).reshape(shape)
            grad_d = nt(ct[:, cols_at], act).reshape(shape)
            if n > 0:
                grad_u += sink_u[:, :, to].astype(F32)
                grad_d += sink_d[:, :, to].astype(F32)
            sink_u[:, :, to] = grad_u.astype(BF16)
            sink_d[:, :, to] = grad_d.astype(BF16)

        def finished(i):
            if n + 1 == sents:
                for k in range(2):
                    pushes(i, k).start()

        for phase in range(2):
            more = phase == 0 or n + 1 < sents
            for copy in fetches(phase, 0):
                copy.wait()
            for copy in fetches(phase, 1):
                copy.start()
            hidden(phase, 0)
            if phase == 1:
                if n + 1 < sents:
                    send_sum(n + 1)
                spread_block(0, blocks - 1)
                finished(blocks - 1)

            @pl.loop(1, blocks)
            def _(i, phase=phase, more=more):
                for copy in fetches(phase, i):
                    copy.wait()

                @pl.when(i + 1 < blocks)
                def _():
                    for copy in fetches(phase, i + 1):
                        copy.start()

                if more:

                    @pl.when(i + 1 == blocks)
                    def _():
                        for copy in fetches(1 - phase, 0):
                            copy.start()

                hidden(phase, i)
                spread_block(phase, i - 1)
                if phase == 0:
                    finished(i - 1)

        spread_block(1, blocks - 1)
        tout[cols_at] = (late_t[:, cols_at] + acc_a[:, cols_at] + obias[2]).T
        norm_back(
            late_t, gain[2], acc_b, ct, acc_a, e_low, (sum_a, sum_b, sum_c),
            cols_at.start, cols_at.stop,
        )

    late = []
    half = rows // 2
    wide, start_of = window(half, half // 2)
    up, across = lax.div(d, 2), lax.rem(d, 2)
    ours = half * up + start_of(across)
    pieces = {
        "u": (2, 0, units, True),
        "d": (3, 0, units, False),
        "x_a": (1, 0, 2 * hw, True),
        "x_b": (1, 2 * hw, 4 * hw, False),
        "s_a": (0, 0, 2 * hw, True),
        "s_b": (0, 2 * hw, 4 * hw, False),
    }

    def add_in(part, begin, end, landing, places, shard=None):
        size = landing.shape[1]
        at = pl.ds(begin, end - begin)
        loads = [
            pltpu.make_async_copy(
                landing.at[z], abuf.at[z, pl.ds(0, size), pl.ds(0, end - begin)], load_sem.at[z]
            )
            for z in range(n_row)
        ]
        for load in loads:
            load.start()
        for z in range(n_row):
            loads[z].wait()
            for to, source, count in places:

                step = 80 if count % 80 == 0 else 48 if count % 48 == 0 else 16

                @pl.loop(0, count // step)
                def _(j, z=z, to=to, source=source, step=step):
                    held_at = pl.ds(pl.multiple_of(to + step * j, 16), step)
                    from_at = pl.ds(pl.multiple_of(source + step * j, 16), step)
                    total = held[part][z, held_at, at].astype(F32)
                    total += abuf[z, from_at, pl.ds(0, end - begin)].astype(F32)
                    held[part][z, held_at, at] = total.astype(BF16)
                    if shard is not None:

                        @pl.when(r == z)
                        def _():
                            shard[from_at, at] = total

    def take(part, arrived):
        for copy in arrived:
            copy()
        add_in(part, 0, held[part].shape[2], came[part], [(0, 0, rows)])

    def first_ring(name):
        if not spread:
            return []
        part, begin, end, tall_first = pieces[name]
        landing, at = refs["ring_" + name], pl.ds(begin, end - begin)
        if tall_first:
            peer = (r, lax.rem(d + 2, 4), c)
            return [push(held[part].at[:, pl.ds(half * (1 - up), half), at], landing, peer)]
        peer = (r, d + 1 - 2 * across, c)
        return [
            push(
                held[part].at[:, pl.ds(half * i + start_of(1 - across), wide), at],
                landing.at[:, pl.ds(wide * i, wide)], peer,
            )
            for i in range(2)
        ]

    def second_ring(name, copies):
        if not spread:
            return []
        part, begin, end, tall_first = pieces[name]
        landing, at = refs["ring_" + name], pl.ds(begin, end - begin)
        for copy in copies:
            copy.wait()
        if tall_first:
            add_in(part, begin, end, landing, [(half * up, 0, half)])
            peer, gone = (r, d + 1 - 2 * across, c), half * up + start_of(1 - across)
        else:
            places = [(half * i + start_of(across), wide * i, wide) for i in range(2)]
            add_in(part, begin, end, landing, places)
            peer, gone = (r, lax.rem(d + 2, 4), c), half * (1 - up) + start_of(across)
        gone = pl.multiple_of(gone, 16)
        return [push(held[part].at[:, pl.ds(gone, wide), at], refs["turn_" + name], peer)]

    def to_lines(name, copies):
        if not spread:
            return []
        part, begin, end, _ = pieces[name]
        for copy in copies:
            copy.wait()
        shard = refs["shard_" + "sxud"[part]]
        add_in(part, begin, end, refs["turn_" + name], [(pl.multiple_of(ours, 16), 0, wide)], shard)
        if not merged:
            for k in range(1, n_row):
                line_to(name, k).start()
            return [name]

        @pl.when(middle)
        def _():
            line_to(name, 1).start()
            line_to(name, 3).start()

        @pl.when(jnp.logical_not(middle))
        def _():
            line_via(name).start()

        return [name]

    def line_rest(name):
        if spread and merged:

            @pl.when(r == 0)
            def _():
                line_to(name, 1).start()

            @pl.when(r == 3)
            def _():
                line_to(name, 3).start()

            @pl.when(jnp.logical_not(middle))
            def _():
                line_to(name, 2).start()


    def line_part(name):
        part, begin, end, _ = pieces[name]
        return part, pl.ds(pl.multiple_of(ours, 16), wide), pl.ds(begin, end - begin)

    def line_to(name, k):
        part, here, at = line_part(name)
        p = list(pieces).index(name)
        peer = lines[k - 1]
        return remote(
            held[part].at[peer[0], here, at], refs["line_" + "sxud"[part]].at[k - 1, :, at],
            link_s.at[p, k - 1], link_r.at[p, k - 1], peer,
        )

    def line_via(name):
        part, here, at = line_part(name)
        p = list(pieces).index(name)
        peer = (jnp.where(r == 0, 1, 2), d, c)
        return remote(
            held[part].at[3 - r, here, at], refs["far_" + "sxud"[part]].at[:, at],
            link_s.at[p, n_row - 1], link_r.at[p, n_row - 1], peer,
        )

    def line_sum(name):
        if spread and merged:

            @pl.when(middle)
            def _():
                part, here, at = line_part(name)
                line_via(name).wait_recv()
                total = held[part][target, here, at].astype(F32)
                total += refs["far_" + "sxud"[part]][:, at].astype(F32)
                held[part][target, here, at] = total.astype(BF16)
                line_to(name, 2).start()

    def sum_lines(part, names):
        if not spread:
            return
        shard, line = refs["shard_" + "sxud"[part]], refs["line_" + "sxud"[part]]

        def arrived(k):
            for name in names:
                line_to(name, k).wait_recv()
            shard[...] += line[k - 1].astype(F32)

        if not merged:
            for k in range(1, n_row):
                for name in names:
                    line_to(name, k).wait_send()
                arrived(k)
            return

        @pl.when(r != 0)
        def _():
            for name in names:
                line_to(name, 3).wait_send()
            arrived(1)

        @pl.when(r != 3)
        def _():
            for name in names:
                line_to(name, 1).wait_send()
            arrived(3)

        @pl.when(jnp.logical_not(middle))
        def _():
            for name in names:
                line_via(name).wait_send()

        for name in names:
            line_to(name, 2).wait_send()
        arrived(2)

    def heads_back(weight, at):
        for g in range(groups):
            for h in range(per):
                to = slice(h * hd, (h + 1) * hd)
                eh[g * hw + h * hd : g * hw + (h + 1) * hd, at] = (
                    nn(weight[g, to], e_low[:, at]) * head_on(g, h)
                ).astype(BF16)

    def cross_back(i):
        at = columns[i]
        heads_back(oc, at)
        attend_back(q2, k2, v2, eh, prob2, grads, (2 * hw, 0, hw), hd, per, sents, [i])
        total = jnp.zeros((width, slots), F32)
        for g in range(groups):
            total += tn(wc[g, 1], grads[g, :hw, at]) + tn(wc[g, 2], grads[g, hw : 2 * hw, at])
        tok_in[at] = total.T.astype(BF16)
        late.append(fetch(tok_in.at[at], glad.at[r, c, at]))
        late.append(push(tok_in.at[at], glad.at[r, c, at], partner))

    def memory_to(i, k):
        at = columns[i]
        return remote(
            tok_in.at[at], glad.at[r, c, at], mem_s.at[i, k - 1], mem_r.at[i, k - 1], lines[k - 1]
        )

    def memory_on(i):
        came_at = glad.at[lax.rem(r + 2, 4), c, columns[i]]
        peer, k = (jnp.where(r == 2, 3, 0), d, c), jnp.where(r == 2, 2, 0)
        return remote(came_at, came_at, mem_s.at[i, n_row - 1], mem_r.at[i, k], peer)

    def share_memory(i, k):
        came_at = glad.at[lax.rem(r + n_row - k, n_row), c, columns[i]]
        late.append(push(came_at, came_at, partner))

    def send_memory(i):
        if merged:

            @pl.when(r != 3)
            def _():
                memory_to(i, 1).start()

            @pl.when(r != 0)
            def _():
                memory_to(i, 3).start()

            memory_to(i, 2).start()
        else:
            for k in range(1, n_row):
                memory_to(i, k).start()

    def pass_memory(i):
        if merged:
            memory_to(i, 2).wait()

            @pl.when(middle)
            def _():
                memory_on(i).start()

            share_memory(i, 2)

    def wait_memory(i):
        if not merged:
            for k in range(1, n_row):
                memory_to(i, k).wait()
                share_memory(i, k)
            return

        @pl.when(r != 3)
        def _():
            memory_to(i, 1).wait_send()

        @pl.when(r != 0)
        def _():
            memory_to(i, 3).wait_send()

        @pl.when(middle)
        def _():
            memory_on(i).wait_send()

        for k in (1, 3):
            memory_to(i, k).wait_recv()
            share_memory(i, k)

    for i in range(sents):
        cross(i)
        feed_forward(i, ffn_copies)
        if i + 1 == sents:
            block_copies = [fetch(tout, ref.block.at[c]), push(tout, ref.block.at[c], partner)]
            take(2, [pushes(j, 0).wait for j in range(blocks)])
            ring_u = first_ring("u")
            take(3, [pushes(j, 1).wait for j in range(blocks)])
            ring_d = first_ring("d")
        cross_back(i)
    for i in range(sents - 1):
        pass_memory(i)
    send_memory(sents - 1)
    vec[:, 8:9] = lane_sum(ct[...])
    vec[:, 2:3] = lane_sum(sum_a[...])
    vec[:, 5:6] = lane_sum(sum_b[...])
    vec[:, 7:8] = lane_sum(sum_c[...])

    def put(g, begin, value):
        sink = (held_now, out_now)[g]
        at = pl.ds(begin, value.shape[1])
        sink[:, :, at] = value.astype(BF16).reshape(n_row, rows, -1)

    def weight_grads(g, sources, attn):
        tail = nt(e_low[...], attn[g])
        begin = 0
        for source, end in sources:
            while begin < end:
                step = min(256, end - begin)
                value = nt(source[...], grads[g, begin : begin + step])
                if begin + step == pad:
                    keep = lead - begin
                    if keep:
                        put(g, begin, value[:, :keep])
                    put(g, lead, value[:, keep:] + tail[:, : pad - lead])
                else:
                    put(g, begin, value)
                begin += step
        put(g, pad, tail[:, pad - lead :])

    held_now, out_now = held[1], out_x
    for g in (1, 0):
        bvec[g, :hw, 2:3] = lane_sum(grads[g, 2 * hw : 3 * hw])
        bvec[g, :hw, 3:4] = lane_sum(grads[g, hw : 2 * hw])
        weight_grads(g, [(mem_t, 2 * hw), (x2, pad)], attn2)
        if g == 1:
            came_x = push(out_x, came[1], partner)
            acc_b[...] = tn(wc[g, 0], grads[g, 2 * hw : 3 * hw])
        else:
            acc_b[...] += tn(wc[g, 0], grads[g, 2 * hw : 3 * hw])
    norm_back(
        mid_t, gain[1], acc_b, acc_a, acc_a, e_low, (sum_a, sum_b, sum_c), 0, tokens_here
    )
    vec[:, 1:2] = lane_sum(sum_a[...])
    vec[:, 4:5] = lane_sum(sum_b[...])
    vec[:, 6:7] = lane_sum(sum_c[...])
    take(1, [came_x.wait])
    ring_x = [first_ring("x_a"), first_ring("x_b")]

    heads_back(os_, slice(0, tokens_here))
    attend_back(q1, k1, v1, eh, prob1, grads, (0, hw, 2 * hw), hd, per, sents, range(sents))
    held_now, out_now = held[0], out_s
    for g in (1, 0):
        bvec[g, :hw, 0:1] = lane_sum(grads[g, :hw])
        bvec[g, :hw, 1:2] = lane_sum(grads[g, 2 * hw : 3 * hw])
        weight_grads(g, [(x1, pad)], attn1)
        if g == 1:
            came_s = push(out_s, came[0], partner)
    for g in range(groups):
        for j in range(3):
            part = tn(ws[g, j], grads[g, j * hw : (j + 1) * hw])
            if g == 0 and j == 0:
                acc_b[...] = part
            else:
                acc_b[...] += part
    take(0, [came_s.wait])
    ring_u = second_ring("u", ring_u)
    ring_d = second_ring("d", ring_d)
    pass_memory(sents - 1)
    ring_s = [first_ring("s_a"), first_ring("s_b")]
    norm_back(
        tok_t, gain[0], acc_b, acc_a, acc_a, e_low, (sum_a, sum_b, sum_c), 0, tokens_here
    )
    vec[:, 0:1] = lane_sum(sum_a[...])
    vec[:, 3:4] = lane_sum(sum_b[...])
    for copy in block_copies:
        copy.wait()
    tout[...] = acc_a[...].T
    late += [fetch(tout, ref.gtok.at[c]), push(tout, ref.gtok.at[c], partner)]

    small_in, small_mp = ref.small_in, ref.small_mp
    aside = -(-hw // 128) * 128
    for g in range(groups):
        small_in[g] = vec[...].T[0:16]
        small_in[g, 10:14, :hw] = bvec[g].T[0:4, :hw]
        small_in[g, 10 : 10 + blocks, aside : aside + ublk] = ubias[g].T[0:blocks]
    push(small_in.at[1], small_mp, partner).wait()
    small[...] = small_in[0] + small_mp[...]
    if spread:
        small_dp, small_row = ref.small_dp, ref.small_row
        small_dp[d] = small[...]
        small_copies = [push(small_dp.at[d], small_dp.at[d], peer) for peer in rings]
        line_u = to_lines("u", ring_u)
        line_d = to_lines("d", ring_d)
        ring_x = [second_ring("x_a", ring_x[0]), second_ring("x_b", ring_x[1])]
        line_rest("u")
        line_rest("d")
        ring_s = [second_ring("s_a", ring_s[0]), second_ring("s_b", ring_s[1])]
        line_sum("u")
        line_sum("d")
        for copy in small_copies:
            copy.wait()
        total = small_dp[0]
        for j in range(1, n_dp):
            total += small_dp[j]
        small_row[r] = total
        small_copies = [push(small_row.at[r], small_row.at[r], peer) for peer in lines]
        line_x = to_lines("x_a", ring_x[0]) + to_lines("x_b", ring_x[1])
        line_s = to_lines("s_a", ring_s[0]) + to_lines("s_b", ring_s[1])
        for name in line_x + line_s:
            line_rest(name)
        for name in line_x + line_s:
            line_sum(name)
    for i in range(sents):
        wait_memory(i)
    if spread:
        sum_lines(2, line_u)
        sum_lines(3, line_d)
        sum_lines(1, line_x)
        for copy in small_copies:
            copy.wait()
        total = small_row[0]
        for j in range(1, n_row):
            total += small_row[j]
        small[...] = total
        sum_lines(0, line_s)
    for copy in late:
        copy.wait()


def layer(n_row, n_dp, scalars, vectors, arrays):
    shape = jax.ShapeDtypeStruct
    encoder, w_self, w_up = arrays["encoder"], arrays["w_self"], arrays["w_up"]
    width, tokens = encoder.shape[1], arrays["tokens"].shape[0] // 2
    hw, units = w_self.shape[1], w_up.shape[1]
    blocks, ublk = vectors["b_up"].shape
    sents = scalars["tgt_len"].shape[0] // 2
    slots, heads = tokens // sents, 2 * hw // HD
    pad, first = -(-3 * hw // 128) * 128, 3 * hw % 128
    rows = width // n_row
    spread = n_dp == 4
    wide, _ = window(rows // 2, rows // 4)
    sizes = {"s": 4 * hw, "x": 4 * hw, "u": units, "d": units}
    outs = {
        "block": ((2, tokens, width), F32, ANY),
        "gtok": ((2, tokens, width), F32, ANY),
        "glad": ((n_row, 2, tokens, width), BF16, ANY),
        "small": ((16, width), F32, VMEM),
        "up_in": (w_up.shape, BF16, ANY),
        "down_in": (arrays["w_down"].shape, BF16, ANY),
    }
    scratch = {}
    for name, size in sizes.items():
        outs["came_" + name] = ((n_row, rows, size), BF16, ANY)
        if spread:
            for piece in (name,) if name in "ud" else (name + "_a", name + "_b"):
                tall_first = piece == "u" or piece[-1] == "a"
                cols_of = size if name in "ud" else size // 2
                landing = rows // 2 if tall_first else 2 * wide
                outs["ring_" + piece] = ((n_row, landing, cols_of), BF16, ANY)
                outs["turn_" + piece] = ((n_row, wide, cols_of), BF16, ANY)
            outs["shard_" + name] = ((wide, size), F32, VMEM)
            scratch["held_" + name] = pltpu.VMEM((n_row, rows, size), BF16)
            scratch["line_" + name] = pltpu.VMEM((n_row - 1, wide, size), BF16)
            scratch["far_" + name] = pltpu.VMEM((wide, size), BF16)
        else:
            outs["held_" + name] = ((n_row, rows, size), BF16, VMEM)
    tall, low = pltpu.VMEM((width, tokens), F32), pltpu.VMEM((width, tokens), BF16)
    flat = pltpu.VMEM((tokens, width), BF16)
    scratch["ws"] = scratch["wc"] = pltpu.VMEM((2,) + w_self.shape, BF16)
    scratch["os"] = scratch["oc"] = pltpu.VMEM((2, hw, width), BF16)
    scratch["wu_buf"] = pltpu.VMEM((3, width, ublk), BF16)
    scratch["wd_buf"] = pltpu.VMEM((3, ublk, width), BF16)
    scratch["act_buf"] = scratch["dh_buf"] = pltpu.VMEM((2, ublk, slots), BF16)
    scratch["out_u"] = scratch["out_d"] = pltpu.VMEM((n_row, rows, units), BF16)
    scratch["out_s"] = scratch["out_x"] = pltpu.VMEM((n_row, rows, 4 * hw), BF16)
    scratch["abuf"] = pltpu.VMEM((n_row, rows, max(sizes.values())), BF16)
    scratch["load_sem"] = pltpu.SemaphoreType.DMA((n_row,))
    scratch["tok_in"] = scratch["cot_in"] = flat
    scratch["enc"] = pltpu.VMEM((n_row, tokens, width), BF16)
    scratch["tout"] = pltpu.VMEM((tokens, width), F32)
    for name in ("mid_t", "late_t", "acc_a", "acc_b"):
        scratch[name] = tall
    for name in ("tok_t", "x1", "x2", "x3", "ct", "mem_t", "e_low"):
        scratch[name] = low
    for name in ("q1", "k1", "v1", "q2", "k2", "v2", "eh"):
        scratch[name] = pltpu.VMEM((2 * hw, tokens), BF16)
    for name in ("attn1", "attn2"):
        scratch[name] = pltpu.VMEM((2, first + hw, tokens), BF16)
    for name in ("prob1", "prob2"):
        scratch[name] = pltpu.VMEM((heads * sents, slots, slots), BF16)
    scratch["grads"] = pltpu.VMEM((2, pad, tokens), BF16)
    for name in ("sum_a", "sum_b", "sum_c", "vec", "cols"):
        scratch[name] = pltpu.VMEM((width, 128), F32)
    scratch["colm"] = pltpu.VMEM((128, width), F32)
    scratch["bm"] = pltpu.VMEM((2, 16, width), F32)
    scratch["bvec"] = pltpu.VMEM((2, -(-hw // 128) * 128, 128), F32)
    scratch["bcols"] = pltpu.VMEM((2, -(-hw // 128) * 128, 8), F32)
    scratch["ubias"] = pltpu.VMEM((2, ublk, 128), F32)
    scratch["bups"] = pltpu.VMEM((2, ublk, 8), F32)
    if spread:
        scratch["small_dp"] = pltpu.VMEM((n_dp, 16, width), F32)
        scratch["small_row"] = pltpu.VMEM((n_row, 16, width), F32)
    dma = pltpu.SemaphoreType.DMA
    scratch["small_in"] = pltpu.VMEM((2, 16, width), F32)
    scratch["small_mp"] = pltpu.VMEM((16, width), F32)
    scratch["via"] = pltpu.VMEM((sents, slots, width), BF16)
    scratch["near"] = pltpu.VMEM((slots, width), BF16)
    scratch["near_sem"] = dma
    scratch["enc_s"] = scratch["enc_r"] = dma((sents, n_row - 1))
    scratch["via_s"] = scratch["via_r"] = dma((sents,))
    scratch["mem_s"] = scratch["mem_r"] = dma((sents, n_row))
    scratch["link_s"] = scratch["link_r"] = dma((6, n_row))
    scratch["local_sem"] = dma((16,))
    scratch["send_sem"] = scratch["recv_sem"] = dma((80,))
    scratch["fetch_sem"] = dma((2, 3))
    scratch["push_sem"] = scratch["land_sem"] = dma((2, blocks))
    names = list(scalars) + list(vectors) + list(arrays) + list(outs) + list(scratch)
    smem = pl.BlockSpec(memory_space=pltpu.SMEM)
    results = pl.pallas_call(
        functools.partial(layer_kernel, n_row, n_dp, names),
        out_shape=tuple(shape(s, t) for s, t, _ in outs.values()),
        in_specs=[smem] * len(scalars) + [VMEM] * len(vectors) + [ANY] * len(arrays),
        out_specs=tuple(spec for _, _, spec in outs.values()),
        scratch_shapes=list(scratch.values()),
        compiler_params=pltpu.CompilerParams(
            collective_id=0, has_side_effects=True, vmem_limit_bytes=63 << 20
        ),
    )(*scalars.values(), *vectors.values(), *arrays.values())
    return dict(zip(outs, results))


def per_device(
    tokens, encoder, layer_pick, piece_heads, piece_ffn, tgt_len, src_len, norm_gain, norm_shift,
    out_bias, w_self, o_self, b_self, w_cross, o_cross, b_cross, w_up, b_up, w_down, cotangent,
):
    n_row, n_dp = lax.axis_size("row"), lax.axis_size("dp")
    r, d, c = place()
    width = tokens.shape[1]
    units, hw = w_up.shape[1], w_self.shape[2]
    ublk = 256
    out = layer(
        n_row, n_dp,
        dict(
            layer_pick=layer_pick, piece_heads=piece_heads, piece_ffn=piece_ffn,
            tgt_len=tgt_len, src_len=src_len,
        ),
        dict(
            norm_gain=norm_gain, norm_shift=norm_shift, out_bias=out_bias,
            b_self=b_self, b_cross=b_cross, b_up=b_up.reshape(-1, ublk),
        ),
        dict(
            tokens=tokens, cotangent=cotangent, encoder=encoder.reshape(-1, width),
            w_self=jnp.swapaxes(w_self, 1, 2), o_self=o_self,
            w_cross=jnp.swapaxes(w_cross, 1, 2), o_cross=o_cross, w_up=w_up, w_down=w_down,
        ),
    )
    share = width // n_row // n_dp
    small = out["small"]
    if n_dp == 4:
        shards = [out["shard_" + name] for name in "sxud"]
    else:
        shards = [
            lax.psum_scatter(
                out["held_" + name].astype(F32).reshape(width, -1),
                ("row", "dp"), scatter_dimension=0, tiled=True,
            )
            for name in "sxud"
        ]
        small = lax.psum(small, ("row", "dp"))

    (
        block, gtok, grad_encoder, gain, shift, bias, w_s, o_s, b_s, w_x, o_x, b_x, w_u, b_u, w_d
    ) = outputs(
        layer_pick, out["block"].reshape(-1, width), out["gtok"].reshape(-1, width),
        out["glad"].reshape(-1, width), small, shards, share, hw, units, ublk,
    )
    return (
        block, gtok, grad_encoder.reshape(1, -1, width), gain, shift, bias,
        w_s, o_s.T, b_s, w_x, o_x.T, b_x, w_u, b_u.reshape(units), w_d.T,
    )


def outputs_kernel(
    share, hw, layer_pick, block_in, gtok_in, memory, small, shard_s, shard_x, shard_u, shard_d,
    block, gtok, encoder, gain, shift, bias, w_s, o_s, b_s, w_x, o_x, b_x, w_u, b_u, w_d,
):
    r, d, c = place()
    n_row, n_dp = layer_pick.shape[1], lax.axis_size("dp")
    width = memory.shape[1]
    step = pl.program_id(0)
    block[...] = block_in[...]
    gtok[...] = gtok_in[...]
    piece = lax.div(step * layer_pick.shape[0], pl.num_programs(0))
    pick = [jnp.full((1, width), layer_pick[piece, i].astype(F32), F32) for i in range(n_row)]
    mine = jnp.full((1, width), layer_pick[piece, r].astype(F32), F32)
    encoder[...] = mine / functools.reduce(jnp.add, pick) * memory[...].astype(F32)

    @pl.when(step == 0)
    def _():
        def own_rows(ref):
            if ref.shape[0] == share:
                return ref[...]
            across = lax.rem(d, 2)
            _, start_of = window(2 * share, share)
            return ref[pl.ds(pl.multiple_of(share * across - start_of(across), 8), share), :]

        def cut(values, i):
            if i:
                values = pltpu.roll(values, values.shape[1] - i * hw, 1)
            return values[:, :hw]

        values = own_rows(shard_s)
        for i in range(3):
            w_s[i] = cut(values, i)
        o_s[...] = cut(values, 3)
        values = own_rows(shard_x)
        for i in range(3):
            w_x[i] = cut(values, (2, 0, 1)[i])
        o_x[...] = cut(values, 3)
        w_u[...] = own_rows(shard_u)
        w_d[...] = own_rows(shard_d)
        at = (r * n_dp + d) * share
        norms = pltpu.roll(small[0:16, :], lax.rem(width - at, width), 1)
        gain[...] = norms[0:3, :share]
        shift[...] = norms[3:6, :share]
        bias[...] = norms[6:9, :share]
        b_s[...] = small[10:12, :hw]
        b_x[...] = small[12:14, :hw]
        aside = -(-hw // 128) * 128
        b_u[...] = small[10 : 10 + b_u.shape[0], aside : aside + b_u.shape[1]]


def outputs(layer_pick, block, gtok, memory, small, shards, share, hw, units, ublk):
    shape = jax.ShapeDtypeStruct
    steps, width = 8, memory.shape[1]
    cut = lambda v: pl.BlockSpec((v.shape[0] // steps, width), lambda i: (i, 0))
    sizes = [(3, share)] * 3 + [(3, share, hw), (share, hw), (2, hw)] * 2
    sizes += [(share, units), (units // ublk, ublk), (share, units)]
    tall = [block, gtok, memory]
    return pl.pallas_call(
        functools.partial(outputs_kernel, share, hw),
        grid=(steps,),
        out_shape=tuple(shape(v.shape, F32) for v in tall) + tuple(shape(v, F32) for v in sizes),
        in_specs=[pl.BlockSpec(memory_space=pltpu.SMEM)] + [cut(v) for v in tall] + [VMEM] * 5,
        out_specs=tuple(cut(v) for v in tall) + (VMEM,) * len(sizes),
        compiler_params=pltpu.CompilerParams(vmem_limit_bytes=62 << 20),
    )(layer_pick, block, gtok, memory, small, *shards)


def solution(mesh):
    return jax.shard_map(
        per_device,
        mesh=mesh,
        in_specs=(
            P(("row", "dp"), None),
            P("row", "dp", None),
            P(),
            P(),
            P(),
            P(("row", "dp")),
            P(("row", "dp")),
            P(),
            P(),
            P(),
            P(None, None, "mp"),
            P("mp", None),
            P(None, "mp"),
            P(None, None, "mp"),
            P("mp", None),
            P(None, "mp"),
            P(None, "mp"),
            P("mp"),
            P("mp", None),
            P(("row", "dp"), None),
        ),
        out_specs=(
            P(("row", "dp"), None),
            P(("row", "dp"), None),
            P("row", "dp", None),
            P(None, ("row", "dp")),
            P(None, ("row", "dp")),
            P(None, ("row", "dp")),
            P(None, ("row", "dp"), "mp"),
            P("mp", ("row", "dp")),
            P(None, "mp"),
            P(None, ("row", "dp"), "mp"),
            P("mp", ("row", "dp")),
            P(None, "mp"),
            P(("row", "dp"), "mp"),
            P("mp"),
            P("mp", ("row", "dp")),
        ),
        check_vma=False,
    )
```

```python
import functools
import types
import jax
import jax.numpy as jnp
from jax import lax
from jax.experimental import pallas as pl
from jax.experimental.pallas import tpu as pltpu
from jax.sharding import PartitionSpec as P

HD = 80
EPSILON = 1e-05
MASKED = -1e30
F32, BF16 = jnp.float32, jnp.bfloat16
MESH = pl.DeviceIdType.MESH
ANY = pl.BlockSpec(memory_space=pl.ANY)
VMEM = pl.BlockSpec(memory_space=pltpu.VMEM)


def nn(a, b):
    return lax.dot_general(a, b, (((1,), (0,)), ((), ())), preferred_element_type=F32)


def nt(a, b):
    return lax.dot_general(a, b, (((1,), (1,)), ((), ())), preferred_element_type=F32)


def tn(a, b):
    return lax.dot_general(a, b, (((0,), (0,)), ((), ())), preferred_element_type=F32)


def lanes(i, n):
    return pl.ds(pl.multiple_of(i * n, n), n)


def layer_norm(v_ref, x_ref, gain, shift, begin, end):
    @pl.loop(begin // 128, end // 128)
    def _(i):
        v = v_ref[:, lanes(i, 128)].astype(F32)
        c = v - jnp.mean(v, axis=0, keepdims=True)
        r = lax.rsqrt(jnp.mean(c * c, axis=0, keepdims=True) + EPSILON)
        x_ref[:, lanes(i, 128)] = (c * r * gain + shift).astype(BF16)


def norm_back(v_ref, gain, up_ref, base_ref, out_ref, low_ref, sums, begin, end):
    gain_sum, shift_sum, bias_sum = sums
    if begin == 0:
        for ref in sums:
            ref[...] = jnp.zeros_like(ref)

    @pl.loop(begin // 128, end // 128)
    def _(i):
        at = lanes(i, 128)
        v = v_ref[:, at].astype(F32)
        c = v - jnp.mean(v, axis=0, keepdims=True)
        r = lax.rsqrt(jnp.mean(c * c, axis=0, keepdims=True) + EPSILON)
        xhat = c * r
        e = up_ref[:, at]
        gain_sum[...] += e * xhat
        shift_sum[...] += e
        eg = e * gain
        m1 = jnp.mean(eg, axis=0, keepdims=True)
        m2 = jnp.mean(eg * xhat, axis=0, keepdims=True)
        out = base_ref[:, at].astype(F32) + r * (eg - m1 - xhat * m2)
        out_ref[:, at] = out
        low = out.astype(BF16)
        low_ref[:, at] = low
        bias_sum[...] += low.astype(F32)


def attend(q_ref, k_ref, v_ref, out_ref, prob_ref, masks, head_on, hd, per, sents):
    groups, slots = out_ref.shape[0], q_ref.shape[1] // sents
    first = out_ref.shape[1] - per * hd
    for g in range(groups):

        @pl.loop(0, per, unroll=2)
        def _(h, g=g):
            rows = pl.ds(pl.multiple_of((g * per + h) * hd, 16), hd)
            to = pl.ds(pl.multiple_of(first + h * hd, 16), hd)
            for s, mask in masks.items():
                at = slice(s * slots, (s + 1) * slots)
                scores = tn(k_ref[rows, at], q_ref[rows, at]) * hd ** (-0.5)
                scores = jnp.where(mask, scores, MASKED)
                e = jnp.exp(scores - jnp.max(scores, axis=0, keepdims=True))
                total = jnp.sum(e, axis=0, keepdims=True)
                p = (e * (1.0 / total)).astype(BF16)
                prob_ref[(g * per + h) * sents + s] = p
                mixed = nn(v_ref[rows, at], p) * head_on(g, h)
                out_ref[g, to, at] = mixed.astype(BF16)


def attend_back(q_ref, k_ref, v_ref, e_ref, prob_ref, d_ref, at_rows, hd, per, sents, some):
    groups, slots = d_ref.shape[0], q_ref.shape[1] // sents
    for g in range(groups):

        @pl.loop(0, per, unroll=2)
        def _(h, g=g):
            rows = pl.ds(pl.multiple_of((g * per + h) * hd, 16), hd)
            dq_at, dk_at, dv_at = [
                pl.ds(pl.multiple_of(first + h * hd, 16), hd) for first in at_rows
            ]
            for s in some:
                at = slice(s * slots, (s + 1) * slots)
                e, p = e_ref[rows, at], prob_ref[(g * per + h) * sents + s]
                d_ref[g, dv_at, at] = nt(e, p).astype(BF16)
                dp = tn(v_ref[rows, at], e)
                pf = p.astype(F32)
                delta = jnp.sum(pf * dp, axis=0, keepdims=True)
                ds = (pf * (dp - delta) * hd ** (-0.5)).astype(BF16)
                d_ref[g, dq_at, at] = nn(k_ref[rows, at], ds).astype(BF16)
                d_ref[g, dk_at, at] = nt(q_ref[rows, at], ds).astype(BF16)


def lane_sum(values):
    return jnp.sum(values.astype(F32), axis=1, keepdims=True)


def place():
    return tuple(lax.axis_index(name) for name in ("row", "dp", "mp"))


def window(rows, share):
    wide = max(
        -(-(i + 1) * share // 16) * 16 - i * share // 16 * 16 for i in range(rows // share)
    )
    return wide, lambda i: pl.multiple_of(
        jnp.minimum(i * share // 16 * 16, rows - wide), 16
    )


def remote(src, dst, send_sem, recv_sem, peer):
    return pltpu.make_async_remote_copy(
        src_ref=src, dst_ref=dst, send_sem=send_sem, recv_sem=recv_sem,
        device_id=peer, device_id_type=MESH,
    )


def started(copy):
    copy.start()
    return copy


def layer_kernel(n_row, n_dp, names, *args):
    refs = dict(zip(names, args))
    ref = types.SimpleNamespace(**refs)
    layer_pick, piece_heads, piece_ffn, tgt_len, src_len = (ref.layer_pick, ref.piece_heads, ref.piece_ffn, ref.tgt_len, ref.src_len)
    tokens, cotangent, encoder = (ref.tokens, ref.cotangent, ref.encoder)
    ws, wc, os_, oc, wu_buf, wd_buf = (ref.ws, ref.wc, ref.os, ref.oc, ref.wu_buf, ref.wd_buf)
    act_buf, dh_buf, load_sem = ref.act_buf, ref.dh_buf, ref.load_sem
    via, near, near_sem = ref.via, ref.near, ref.near_sem
    enc_s, enc_r, via_s, via_r = ref.enc_s, ref.enc_r, ref.via_s, ref.via_r
    mem_s, mem_r, link_s, link_r = ref.mem_s, ref.mem_r, ref.link_s, ref.link_r
    tok_in, cot_in, enc, tout, tok_t, mid_t, late_t, acc_a, acc_b = (ref.tok_in, ref.cot_in, ref.enc, ref.tout, ref.tok_t, ref.mid_t, ref.late_t, ref.acc_a, ref.acc_b)
    x1, x2, x3, ct, mem_t, e_low, eh = (ref.x1, ref.x2, ref.x3, ref.ct, ref.mem_t, ref.e_low, ref.eh)
    q1, k1, v1, q2, k2, v2 = (ref.q1, ref.k1, ref.v1, ref.q2, ref.k2, ref.v2)
    attn1, attn2, prob1, prob2, grads = (ref.attn1, ref.attn2, ref.prob1, ref.prob2, ref.grads)
    sum_a, sum_b, sum_c, vec, bvec, ubias, colm, cols, bm, bcols, bups = (ref.sum_a, ref.sum_b, ref.sum_c, ref.vec, ref.bvec, ref.ubias, ref.colm, ref.cols, ref.bm, ref.bcols, ref.bups)
    out_s, out_x, out_u, out_d, abuf = (ref.out_s, ref.out_x, ref.out_u, ref.out_d, ref.abuf)
    local_sem, send_sem, recv_sem, fetch_sem, push_sem, land_sem = (ref.local_sem, ref.send_sem, ref.recv_sem, ref.fetch_sem, ref.push_sem, ref.land_sem)
    held, came = (ref.held_s, ref.held_x, ref.held_u, ref.held_d), (ref.came_s, ref.came_x, ref.came_u, ref.came_d)
    small, glad = (ref.small, ref.glad)
    spread = n_dp == 4

    width, tokens_here = tok_t.shape
    groups, _, hw, _ = ws.shape
    units, ublk, hd = ref.w_up.shape[1], bups.shape[1], HD
    blocks, per = units // ublk, hw // HD
    rows = width // n_row
    sents = tgt_len.shape[0] // 2
    slots = tokens_here // sents
    pad = -(-3 * hw // 128) * 128
    lead = 3 * hw // 128 * 128
    first = 3 * hw - lead
    r, d, c = place()
    partner = (r, d, 1 - c)
    rings = [(r, lax.rem(d + i, n_dp), c) for i in range(1, n_dp)] if spread else []
    lines = [(lax.rem(r + i, n_row), d, c) for i in range(1, n_row)]
    counts = {"local": 0, "link": 0}

    def fetch(src, dst):
        i = counts["local"]
        counts["local"] += 1
        return started(pltpu.make_async_copy(src, dst, local_sem.at[i]))

    def push(src, dst, peer):
        i = counts["link"]
        counts["link"] += 1
        return started(remote(src, dst, send_sem.at[i], recv_sem.at[i], peer))

    mine = pl.ds(pl.multiple_of(c * tokens_here, tokens_here), tokens_here)
    tok_copy = fetch(tokens.at[mine], tok_in)
    ws_copies = [fetch(ref.w_self, ws.at[0]), fetch(ref.o_self, os_.at[0])]
    bm[...] = jnp.zeros_like(bm)
    bm[0, 0:2, :hw] = ref.b_self[...]
    bm[0, 2:4, :hw] = ref.b_cross[...]
    bm[0, 8 : 8 + blocks, :ublk] = ref.b_up[...]
    colm[...] = jnp.zeros_like(colm)
    colm[0:3] = ref.norm_gain[...]
    colm[3:6] = ref.norm_shift[...]
    colm[6:9] = ref.out_bias[...]
    barrier = pltpu.get_barrier_semaphore()
    peers = [partner] + rings + lines
    for peer in peers:
        pl.semaphore_signal(barrier, inc=1, device_id=peer, device_id_type=MESH)
    pl.semaphore_wait(barrier, len(peers))
    ws_copies += [
        push(ref.w_self, ws.at[1], partner),
        push(bm.at[0], bm.at[1], partner),
        push(ref.o_self, os_.at[1], partner),
    ]
    def sentence(piece, i):
        start = (piece * 2 + c) * tokens_here + i * slots
        return encoder.at[pl.ds(pl.multiple_of(start, slots), slots)]

    columns = [slice(i * slots, (i + 1) * slots) for i in range(sents)]

    middle = (r == 1) | (r == 2)
    target, far = lax.rem(r + 2, 4), lax.rem(r + 1 + 2 * (2 - r), 4)
    merged = n_row == 4

    def block_to(i, k):
        peer = lines[k - 1]
        return remote(
            sentence(peer[0], i), enc.at[r, columns[i]], enc_s.at[i, k - 1], enc_r.at[i, k - 1], peer
        )

    def block_via(i):
        peer = (jnp.where(r == 0, 1, 2), d, c)
        return remote(sentence(3 - r, i), via.at[i], via_s.at[i], via_r.at[i], peer)

    def block_sum(i):
        return remote(
            via.at[i], enc.at[r, columns[i]], enc_s.at[i, 1], enc_r.at[i, 1], (target, d, c)
        )

    def block_near(i):
        return pltpu.make_async_copy(sentence(target, i), near, near_sem)

    own_blocks = []

    def send_far(i):
        own_blocks.append(fetch(sentence(r, i), enc.at[r, columns[i]]))
        if merged:

            @pl.when(middle)
            def _():
                block_near(i).start()

            @pl.when(jnp.logical_not(middle))
            def _():
                block_via(i).start()

    def send_blocks(i):
        if not merged:
            for k in range(1, n_row):
                block_to(i, k).start()
            return

        @pl.when(r != 3)
        def _():
            block_to(i, 1).start()

        @pl.when(r != 0)
        def _():
            block_to(i, 3).start()

        @pl.when(jnp.logical_not(middle))
        def _():
            block_to(i, 2).start()

    def send_sum(i):
        if merged:

            @pl.when(middle)
            def _():
                picks = [
                    jnp.full((1, width), layer_pick[target, j].astype(F32), F32)
                    for j in range(n_row)
                ]
                total = functools.reduce(jnp.add, picks)
                far_pick = jnp.full((1, width), layer_pick[target, far].astype(F32), F32)
                near_pick = jnp.full((1, width), layer_pick[target, r].astype(F32), F32)
                block_near(i).wait()
                block_via(i).wait_recv()
                via[i] = (
                    far_pick / total * via[i].astype(F32) + near_pick / total * near[...].astype(F32)
                ).astype(BF16)
                block_sum(i).start()

    def wait_blocks(i):
        own_blocks[i].wait()
        if not merged:
            for k in range(1, n_row):
                block_to(i, k).wait()
            return

        @pl.when(r != 3)
        def _():
            block_to(i, 1).wait_send()
            block_to(i, 3).wait_recv()

        @pl.when(r != 0)
        def _():
            block_to(i, 3).wait_send()
            block_to(i, 1).wait_recv()

        @pl.when(middle)
        def _():
            block_sum(i).wait_send()

        @pl.when(jnp.logical_not(middle))
        def _():
            block_to(i, 2).wait_send()
            block_via(i).wait_send()

        block_to(i, 2).wait_recv()

    send_far(0)
    if merged:

        @pl.when(r == 0)
        def _():
            enc[3] = jnp.zeros(enc.shape[1:], BF16)

        @pl.when(r == 3)
        def _():
            enc[0] = jnp.zeros(enc.shape[1:], BF16)

    wc_copies = [
        fetch(ref.w_cross, wc.at[0]),
        fetch(ref.o_cross, oc.at[0]),
        push(ref.w_cross, wc.at[1], partner),
        push(ref.o_cross, oc.at[1], partner),
    ]
    cot_copy = fetch(cotangent.at[mine], cot_in)
    ffn_copies = [
        push(ref.w_up, ref.up_in, partner),
        push(ref.w_down, ref.down_in, partner),
    ]

    cols[...] = colm[...].T
    gain, shift, obias = [[cols[:, j : j + 1] for j in range(3 * i, 3 * i + 3)] for i in range(3)]
    key_at = lax.broadcasted_iota(jnp.int32, (slots, slots), 0)
    query_at = lax.broadcasted_iota(jnp.int32, (slots, slots), 1)
    for zeroed in (attn1, attn2):
        zeroed[:, :first, :] = jnp.zeros((groups, first, tokens_here), BF16)
    grads[:, 3 * hw :, :] = jnp.zeros((groups, pad - 3 * hw, tokens_here), BF16)
    vec[...] = jnp.zeros_like(vec)
    bvec[...] = jnp.zeros_like(bvec)
    ubias[...] = jnp.zeros_like(ubias)
    heads_here, units_here = piece_heads[r], piece_ffn[r]
    group_at = [c, 1 - c]

    def head_on(g, h):
        return jnp.where(group_at[g] * per + h < heads_here, 1.0, 0.0)

    tok_copy.wait()
    tok_t[...] = tok_in[...].astype(F32).T.astype(BF16)
    layer_norm(tok_t, x1, gain[0], shift[0], 0, tokens_here)
    for copy in ws_copies:
        copy.wait()
    for g in range(groups):
        bcols[g] = bm[g, 0:8, : bcols.shape[1]].T
        bups[g] = bm[g, 8:16, :ublk].T
    for g in range(groups):
        at = slice(g * hw, (g + 1) * hw)
        q1[at] = (nn(ws[g, 0], x1[...]) + bcols[g, :hw, 0:1]).astype(BF16)
        k1[at] = nn(ws[g, 1], x1[...]).astype(BF16)
        v1[at] = (nn(ws[g, 2], x1[...]) + bcols[g, :hw, 1:2]).astype(BF16)
    send_blocks(0)
    masks = {
        i: (key_at <= query_at) & (key_at < tgt_len[c * sents + i]) for i in range(sents)
    }
    attend(q1, k1, v1, attn1, prob1, masks, head_on, hd, per, sents)
    send_sum(0)
    acc_a[...] = tn(os_[0], attn1[0, first:])
    for g in range(1, groups):
        acc_a[...] += tn(os_[g], attn1[g, first:])
    mid_t[...] = tok_t[...].astype(F32) + acc_a[...] + obias[0]
    layer_norm(mid_t, x2, gain[1], shift[1], 0, tokens_here)
    for copy in wc_copies:
        copy.wait()
    for g in range(groups):
        at = slice(g * hw, (g + 1) * hw)
        q2[at] = (nn(wc[g, 0], x2[...]) + bcols[g, :hw, 2:3]).astype(BF16)
    cot_copy.wait()
    ct[...] = cot_in[...].astype(F32).T.astype(BF16)

    picks = [
        jnp.full((1, width), layer_pick[r, i].astype(F32), F32) for i in range(layer_pick.shape[1])
    ]
    total = functools.reduce(jnp.add, picks)
    weights = [pick / total for pick in picks]
    if merged:
        summed = [False, r == 3, r == 0, False]
        absent = [r == 3, False, False, r == 0]
        weights = [
            jnp.where(one, 1.0, jnp.where(none, 0.0, weight))
            for one, none, weight in zip(summed, absent, weights)
        ]
    def cross(i):
        at = columns[i]
        wait_blocks(i)
        if i + 1 < sents:
            send_far(i + 1)
        if i > 0:
            send_memory(i - 1)
        memory = weights[0] * enc[0, at].astype(F32)
        for j in range(1, n_row):
            memory += weights[j] * enc[j, at].astype(F32)
        mem_t[:, at] = memory.T.astype(BF16)
        for g in range(groups):
            to = slice(g * hw, (g + 1) * hw)
            k2[to, at] = nn(wc[g, 1], mem_t[:, at]).astype(BF16)
            v2[to, at] = (nn(wc[g, 2], mem_t[:, at]) + bcols[g, :hw, 3:4]).astype(BF16)
        masks = {i: key_at < src_len[c * sents + i]}
        attend(q2, k2, v2, attn2, prob2, masks, head_on, hd, per, sents)
        branch = tn(oc[0], attn2[0, first:, at])
        for g in range(1, groups):
            branch += tn(oc[g], attn2[g, first:, at])
        late_t[:, at] = mid_t[:, at] + branch + obias[1]
        layer_norm(late_t, x3, gain[2], shift[2], at.start, at.stop)
        if i + 1 < sents:
            send_blocks(i + 1)

    def slot_of(phase, i):
        return lax.rem(phase * blocks + i, 3)

    def fetches(phase, i):
        slot, at = slot_of(phase, i), lanes(i, ublk)
        up, down = (ref.w_up, ref.w_down) if phase else (ref.up_in, ref.down_in)
        return [
            pltpu.make_async_copy(up.at[:, at], wu_buf.at[slot], fetch_sem.at[0, slot]),
            pltpu.make_async_copy(down.at[at, :], wd_buf.at[slot], fetch_sem.at[1, slot]),
        ]

    def pushes(i, k):
        at = lanes(i, ublk)
        return remote(
            (out_u, out_d)[k].at[:, :, at], came[2 + k].at[:, :, at],
            push_sem.at[k, i], land_sem.at[k, i], partner,
        )

    def feed_forward(n, ready):
        cols_at = columns[n]
        if n == 0:
            for copy in ready:
                copy.wait()
            for copy in fetches(0, 0):
                copy.start()
        acc_a[:, cols_at] = jnp.zeros((width, slots), F32)
        acc_b[:, cols_at] = jnp.zeros((width, slots), F32)

        def hidden(phase, i):
            g, slot, at = 1 - phase, slot_of(phase, i), lax.rem(i, 2)
            up, down = wu_buf.at[slot], wd_buf.at[slot]
            here = lax.broadcasted_iota(jnp.int32, bups.shape[1:], 1) == i
            h = nn(up[...].T, x3[:, cols_at]) + lane_sum(jnp.where(here, bups[g], 0.0))
            unit = group_at[g] * units + i * ublk
            unit = unit + lax.broadcasted_iota(jnp.int32, (ublk, 1), 0)
            on = jnp.where(unit < units_here, 1.0, 0.0)
            squared = h * h
            t = jnp.tanh(h * (0.7978845608028654 + 0.0356774081363001 * squared))
            cdf = 0.5 + 0.5 * t
            slope = cdf + h * (0.5 - 0.5 * t * t) * (
                0.7978845608028654 + 0.1070322244089003 * squared
            )
            act_buf[at] = (h * cdf * on).astype(BF16)
            dh = (nn(down[...], ct[:, cols_at]) * (slope * on)).astype(BF16)
            dh_buf[at] = dh
            in_sums = lax.broadcasted_iota(jnp.int32, ubias.shape[1:], 1) == i
            ubias[g] += jnp.where(in_sums, lane_sum(dh), 0.0)

        def spread_block(phase, i):
            slot, at = slot_of(phase, i), lax.rem(i, 2)
            sink_u, sink_d = (held[2], held[3]) if phase else (out_u, out_d)
            act, dh = act_buf[at], dh_buf[at]
            acc_a[:, cols_at] += tn(wd_buf[slot], act)
            acc_b[:, cols_at] += nn(wu_buf[slot], dh)
            shape, to = (n_row, rows, ublk), lanes(i, ublk)
            grad_u = nt(x3[:, cols_at], dh).reshape(shape)
            grad_d = nt(ct[:, cols_at], act).reshape(shape)
            if n > 0:
                grad_u += sink_u[:, :, to].astype(F32)
                grad_d += sink_d[:, :, to].astype(F32)
            sink_u[:, :, to] = grad_u.astype(BF16)
            sink_d[:, :, to] = grad_d.astype(BF16)

        def finished(i):
            if n + 1 == sents:
                for k in range(2):
                    pushes(i, k).start()

        for phase in range(2):
            more = phase == 0 or n + 1 < sents
            for copy in fetches(phase, 0):
                copy.wait()
            for copy in fetches(phase, 1):
                copy.start()
            hidden(phase, 0)
            if phase == 1:
                if n + 1 < sents:
                    send_sum(n + 1)
                spread_block(0, blocks - 1)
                finished(blocks - 1)

            @pl.loop(1, blocks)
            def _(i, phase=phase, more=more):
                for copy in fetches(phase, i):
                    copy.wait()

                @pl.when(i + 1 < blocks)
                def _():
                    for copy in fetches(phase, i + 1):
                        copy.start()

                if more:

                    @pl.when(i + 1 == blocks)
                    def _():
                        for copy in fetches(1 - phase, 0):
                            copy.start()

                hidden(phase, i)
                spread_block(phase, i - 1)
                if phase == 0:
                    finished(i - 1)

        spread_block(1, blocks - 1)
        tout[cols_at] = (late_t[:, cols_at] + acc_a[:, cols_at] + obias[2]).T
        norm_back(
            late_t, gain[2], acc_b, ct, acc_a, e_low, (sum_a, sum_b, sum_c),
            cols_at.start, cols_at.stop,
        )

    late = []
    half = rows // 2
    wide, start_of = window(half, half // 2)
    up, across = lax.div(d, 2), lax.rem(d, 2)
    ours = half * up + start_of(across)
    pieces = {
        "u": (2, 0, units, True),
        "d": (3, 0, units, False),
        "x_a": (1, 0, 2 * hw, True),
        "x_b": (1, 2 * hw, 4 * hw, False),
        "s_a": (0, 0, 2 * hw, True),
        "s_b": (0, 2 * hw, 4 * hw, False),
    }

    def add_in(part, begin, end, landing, places, shard=None):
        size = landing.shape[1]
        at = pl.ds(begin, end - begin)
        loads = [
            pltpu.make_async_copy(
                landing.at[z], abuf.at[z, pl.ds(0, size), pl.ds(0, end - begin)], load_sem.at[z]
            )
            for z in range(n_row)
        ]
        for load in loads:
            load.start()
        for z in range(n_row):
            loads[z].wait()
            for to, source, count in places:

                step = 80 if count % 80 == 0 else 48 if count % 48 == 0 else 16

                @pl.loop(0, count // step)
                def _(j, z=z, to=to, source=source, step=step):
                    held_at = pl.ds(pl.multiple_of(to + step * j, 16), step)
                    from_at = pl.ds(pl.multiple_of(source + step * j, 16), step)
                    total = held[part][z, held_at, at].astype(F32)
                    total += abuf[z, from_at, pl.ds(0, end - begin)].astype(F32)
                    held[part][z, held_at, at] = total.astype(BF16)
                    if shard is not None:

                        @pl.when(r == z)
                        def _():
                            shard[from_at, at] = total

    def take(part, arrived):
        for copy in arrived:
            copy()
        add_in(part, 0, held[part].shape[2], came[part], [(0, 0, rows)])

    def first_ring(name):
        if not spread:
            return []
        part, begin, end, tall_first = pieces[name]
        landing, at = refs["ring_" + name], pl.ds(begin, end - begin)
        if tall_first:
            peer = (r, lax.rem(d + 2, 4), c)
            return [push(held[part].at[:, pl.ds(half * (1 - up), half), at], landing, peer)]
        peer = (r, d + 1 - 2 * across, c)
        return [
            push(
                held[part].at[:, pl.ds(half * i + start_of(1 - across), wide), at],
                landing.at[:, pl.ds(wide * i, wide)], peer,
            )
            for i in range(2)
        ]

    def second_ring(name, copies):
        if not spread:
            return []
        part, begin, end, tall_first = pieces[name]
        landing, at = refs["ring_" + name], pl.ds(begin, end - begin)
        for copy in copies:
            copy.wait()
        if tall_first:
            add_in(part, begin, end, landing, [(half * up, 0, half)])
            peer, gone = (r, d + 1 - 2 * across, c), half * up + start_of(1 - across)
        else:
            places = [(half * i + start_of(across), wide * i, wide) for i in range(2)]
            add_in(part, begin, end, landing, places)
            peer, gone = (r, lax.rem(d + 2, 4), c), half * (1 - up) + start_of(across)
        gone = pl.multiple_of(gone, 16)
        return [push(held[part].at[:, pl.ds(gone, wide), at], refs["turn_" + name], peer)]

    def to_lines(name, copies):
        if not spread:
            return []
        part, begin, end, _ = pieces[name]
        for copy in copies:
            copy.wait()
        shard = refs["shard_" + "sxud"[part]]
        add_in(part, begin, end, refs["turn_" + name], [(pl.multiple_of(ours, 16), 0, wide)], shard)
        if not merged:
            for k in range(1, n_row):
                line_to(name, k).start()
            return [name]

        @pl.when(middle)
        def _():
            line_to(name, 1).start()
            line_to(name, 3).start()

        @pl.when(jnp.logical_not(middle))
        def _():
            line_via(name).start()

        return [name]

    def line_rest(name):
        if spread and merged:

            @pl.when(r == 0)
            def _():
                line_to(name, 1).start()

            @pl.when(r == 3)
            def _():
                line_to(name, 3).start()

            @pl.when(jnp.logical_not(middle))
            def _():
                line_to(name, 2).start()


    def line_part(name):
        part, begin, end, _ = pieces[name]
        return part, pl.ds(pl.multiple_of(ours, 16), wide), pl.ds(begin, end - begin)

    def line_to(name, k):
        part, here, at = line_part(name)
        p = list(pieces).index(name)
        peer = lines[k - 1]
        return remote(
            held[part].at[peer[0], here, at], refs["line_" + "sxud"[part]].at[k - 1, :, at],
            link_s.at[p, k - 1], link_r.at[p, k - 1], peer,
        )

    def line_via(name):
        part, here, at = line_part(name)
        p = list(pieces).index(name)
        peer = (jnp.where(r == 0, 1, 2), d, c)
        return remote(
            held[part].at[3 - r, here, at], refs["far_" + "sxud"[part]].at[:, at],
            link_s.at[p, n_row - 1], link_r.at[p, n_row - 1], peer,
        )

    def line_sum(name):
        if spread and merged:

            @pl.when(middle)
            def _():
                part, here, at = line_part(name)
                line_via(name).wait_recv()
                total = held[part][target, here, at].astype(F32)
                total += refs["far_" + "sxud"[part]][:, at].astype(F32)
                held[part][target, here, at] = total.astype(BF16)
                line_to(name, 2).start()

    def sum_lines(part, names):
        if not spread:
            return
        shard, line = refs["shard_" + "sxud"[part]], refs["line_" + "sxud"[part]]

        def arrived(k):
            for name in names:
                line_to(name, k).wait_recv()
            shard[...] += line[k - 1].astype(F32)

        if not merged:
            for k in range(1, n_row):
                for name in names:
                    line_to(name, k).wait_send()
                arrived(k)
            return

        @pl.when(r != 0)
        def _():
            for name in names:
                line_to(name, 3).wait_send()
            arrived(1)

        @pl.when(r != 3)
        def _():
            for name in names:
                line_to(name, 1).wait_send()
            arrived(3)

        @pl.when(jnp.logical_not(middle))
        def _():
            for name in names:
                line_via(name).wait_send()

        for name in names:
            line_to(name, 2).wait_send()
        arrived(2)

    def heads_back(weight, at):
        for g in range(groups):
            for h in range(per):
                to = slice(h * hd, (h + 1) * hd)
                eh[g * hw + h * hd : g * hw + (h + 1) * hd, at] = (
                    nn(weight[g, to], e_low[:, at]) * head_on(g, h)
                ).astype(BF16)

    def cross_back(i):
        at = columns[i]
        heads_back(oc, at)
        attend_back(q2, k2, v2, eh, prob2, grads, (2 * hw, 0, hw), hd, per, sents, [i])
        total = jnp.zeros((width, slots), F32)
        for g in range(groups):
            total += tn(wc[g, 1], grads[g, :hw, at]) + tn(wc[g, 2], grads[g, hw : 2 * hw, at])
        tok_in[at] = total.T.astype(BF16)
        late.append(fetch(tok_in.at[at], glad.at[r, c, at]))
        late.append(push(tok_in.at[at], glad.at[r, c, at], partner))

    def memory_to(i, k):
        at = columns[i]
        return remote(
            tok_in.at[at], glad.at[r, c, at], mem_s.at[i, k - 1], mem_r.at[i, k - 1], lines[k - 1]
        )

    def memory_on(i):
        came_at = glad.at[lax.rem(r + 2, 4), c, columns[i]]
        peer, k = (jnp.where(r == 2, 3, 0), d, c), jnp.where(r == 2, 2, 0)
        return remote(came_at, came_at, mem_s.at[i, n_row - 1], mem_r.at[i, k], peer)

    def share_memory(i, k):
        came_at = glad.at[lax.rem(r + n_row - k, n_row), c, columns[i]]
        late.append(push(came_at, came_at, partner))

    def send_memory(i):
        if merged:

            @pl.when(r != 3)
            def _():
                memory_to(i, 1).start()

            @pl.when(r != 0)
            def _():
                memory_to(i, 3).start()

            memory_to(i, 2).start()
        else:
            for k in range(1, n_row):
                memory_to(i, k).start()

    def pass_memory(i):
        if merged:
            memory_to(i, 2).wait()

            @pl.when(middle)
            def _():
                memory_on(i).start()

            share_memory(i, 2)

    def wait_memory(i):
        if not merged:
            for k in range(1, n_row):
                memory_to(i, k).wait()
                share_memory(i, k)
            return

        @pl.when(r != 3)
        def _():
            memory_to(i, 1).wait_send()

        @pl.when(r != 0)
        def _():
            memory_to(i, 3).wait_send()

        @pl.when(middle)
        def _():
            memory_on(i).wait_send()

        for k in (1, 3):
            memory_to(i, k).wait_recv()
            share_memory(i, k)

    for i in range(sents):
        cross(i)
        feed_forward(i, ffn_copies)
        if i + 1 == sents:
            block_copies = [fetch(tout, ref.block.at[c]), push(tout, ref.block.at[c], partner)]
            take(2, [pushes(j, 0).wait for j in range(blocks)])
            ring_u = first_ring("u")
            take(3, [pushes(j, 1).wait for j in range(blocks)])
            ring_d = first_ring("d")
        cross_back(i)
    for i in range(sents - 1):
        pass_memory(i)
    send_memory(sents - 1)
    vec[:, 8:9] = lane_sum(ct[...])
    vec[:, 2:3] = lane_sum(sum_a[...])
    vec[:, 5:6] = lane_sum(sum_b[...])
    vec[:, 7:8] = lane_sum(sum_c[...])

    def put(g, begin, value):
        sink = (held_now, out_now)[g]
        at = pl.ds(begin, value.shape[1])
        sink[:, :, at] = value.astype(BF16).reshape(n_row, rows, -1)

    def weight_grads(g, sources, attn):
        tail = nt(e_low[...], attn[g])
        begin = 0
        for source, end in sources:
            while begin < end:
                step = min(256, end - begin)
                value = nt(source[...], grads[g, begin : begin + step])
                if begin + step == pad:
                    keep = lead - begin
                    if keep:
                        put(g, begin, value[:, :keep])
                    put(g, lead, value[:, keep:] + tail[:, : pad - lead])
                else:
                    put(g, begin, value)
                begin += step
        put(g, pad, tail[:, pad - lead :])

    held_now, out_now = held[1], out_x
    for g in (1, 0):
        bvec[g, :hw, 2:3] = lane_sum(grads[g, 2 * hw : 3 * hw])
        bvec[g, :hw, 3:4] = lane_sum(grads[g, hw : 2 * hw])
        weight_grads(g, [(mem_t, 2 * hw), (x2, pad)], attn2)
        if g == 1:
            came_x = push(out_x, came[1], partner)
            acc_b[...] = tn(wc[g, 0], grads[g, 2 * hw : 3 * hw])
        else:
            acc_b[...] += tn(wc[g, 0], grads[g, 2 * hw : 3 * hw])
    norm_back(
        mid_t, gain[1], acc_b, acc_a, acc_a, e_low, (sum_a, sum_b, sum_c), 0, tokens_here
    )
    vec[:, 1:2] = lane_sum(sum_a[...])
    vec[:, 4:5] = lane_sum(sum_b[...])
    vec[:, 6:7] = lane_sum(sum_c[...])
    take(1, [came_x.wait])
    ring_x = [first_ring("x_a"), first_ring("x_b")]

    heads_back(os_, slice(0, tokens_here))
    attend_back(q1, k1, v1, eh, prob1, grads, (0, hw, 2 * hw), hd, per, sents, range(sents))
    ring_u = second_ring("u", ring_u)
    ring_d = second_ring("d", ring_d)
    held_now, out_now = held[0], out_s
    for g in (1, 0):
        bvec[g, :hw, 0:1] = lane_sum(grads[g, :hw])
        bvec[g, :hw, 1:2] = lane_sum(grads[g, 2 * hw : 3 * hw])
        weight_grads(g, [(x1, pad)], attn1)
        if g == 1:
            came_s = push(out_s, came[0], partner)
    for g in range(groups):
        for j in range(3):
            part = tn(ws[g, j], grads[g, j * hw : (j + 1) * hw])
            if g == 0 and j == 0:
                acc_b[...] = part
            else:
                acc_b[...] += part
    take(0, [came_s.wait])
    ring_s = [first_ring("s_a"), first_ring("s_b")]
    norm_back(
        tok_t, gain[0], acc_b, acc_a, acc_a, e_low, (sum_a, sum_b, sum_c), 0, tokens_here
    )
    vec[:, 0:1] = lane_sum(sum_a[...])
    vec[:, 3:4] = lane_sum(sum_b[...])
    for copy in block_copies:
        copy.wait()
    tout[...] = acc_a[...].T
    late += [fetch(tout, ref.gtok.at[c]), push(tout, ref.gtok.at[c], partner)]

    pass_memory(sents - 1)

    small_in, small_mp = ref.small_in, ref.small_mp
    aside = -(-hw // 128) * 128
    for g in range(groups):
        small_in[g] = vec[...].T[0:16]
        small_in[g, 10:14, :hw] = bvec[g].T[0:4, :hw]
        small_in[g, 10 : 10 + blocks, aside : aside + ublk] = ubias[g].T[0:blocks]
    push(small_in.at[1], small_mp, partner).wait()
    small[...] = small_in[0] + small_mp[...]
    if spread:
        small_dp, small_row = ref.small_dp, ref.small_row
        small_dp[d] = small[...]
        small_copies = [push(small_dp.at[d], small_dp.at[d], peer) for peer in rings]
        line_u = to_lines("u", ring_u)
        line_d = to_lines("d", ring_d)
        ring_x = [second_ring("x_a", ring_x[0]), second_ring("x_b", ring_x[1])]
        line_rest("u")
        line_rest("d")
        ring_s = [second_ring("s_a", ring_s[0]), second_ring("s_b", ring_s[1])]
        line_sum("u")
        line_sum("d")
        for copy in small_copies:
            copy.wait()
        total = small_dp[0]
        for j in range(1, n_dp):
            total += small_dp[j]
        small_row[r] = total
        small_copies = [push(small_row.at[r], small_row.at[r], peer) for peer in lines]
        line_x = to_lines("x_a", ring_x[0]) + to_lines("x_b", ring_x[1])
        line_s = to_lines("s_a", ring_s[0]) + to_lines("s_b", ring_s[1])
        for name in line_x + line_s:
            line_rest(name)
        for name in line_x + line_s:
            line_sum(name)
    for i in range(sents):
        wait_memory(i)
    if spread:
        sum_lines(2, line_u)
        sum_lines(3, line_d)
        sum_lines(1, line_x)
        for copy in small_copies:
            copy.wait()
        total = small_row[0]
        for j in range(1, n_row):
            total += small_row[j]
        small[...] = total
        sum_lines(0, line_s)
    for copy in late:
        copy.wait()


def layer(n_row, n_dp, scalars, vectors, arrays):
    shape = jax.ShapeDtypeStruct
    encoder, w_self, w_up = arrays["encoder"], arrays["w_self"], arrays["w_up"]
    width, tokens = encoder.shape[1], arrays["tokens"].shape[0] // 2
    hw, units = w_self.shape[1], w_up.shape[1]
    blocks, ublk = vectors["b_up"].shape
    sents = scalars["tgt_len"].shape[0] // 2
    slots, heads = tokens // sents, 2 * hw // HD
    pad, first = -(-3 * hw // 128) * 128, 3 * hw % 128
    rows = width // n_row
    spread = n_dp == 4
    wide, _ = window(rows // 2, rows // 4)
    sizes = {"s": 4 * hw, "x": 4 * hw, "u": units, "d": units}
    outs = {
        "block": ((2, tokens, width), F32, ANY),
        "gtok": ((2, tokens, width), F32, ANY),
        "glad": ((n_row, 2, tokens, width), BF16, ANY),
        "small": ((16, width), F32, VMEM),
        "up_in": (w_up.shape, BF16, ANY),
        "down_in": (arrays["w_down"].shape, BF16, ANY),
    }
    scratch = {}
    for name, size in sizes.items():
        outs["came_" + name] = ((n_row, rows, size), BF16, ANY)
        if spread:
            for piece in (name,) if name in "ud" else (name + "_a", name + "_b"):
                tall_first = piece == "u" or piece[-1] == "a"
                cols_of = size if name in "ud" else size // 2
                landing = rows // 2 if tall_first else 2 * wide
                outs["ring_" + piece] = ((n_row, landing, cols_of), BF16, ANY)
                outs["turn_" + piece] = ((n_row, wide, cols_of), BF16, ANY)
            outs["shard_" + name] = ((wide, size), F32, VMEM)
            scratch["held_" + name] = pltpu.VMEM((n_row, rows, size), BF16)
            scratch["line_" + name] = pltpu.VMEM((n_row - 1, wide, size), BF16)
            scratch["far_" + name] = pltpu.VMEM((wide, size), BF16)
        else:
            outs["held_" + name] = ((n_row, rows, size), BF16, VMEM)
    tall, low = pltpu.VMEM((width, tokens), F32), pltpu.VMEM((width, tokens), BF16)
    flat = pltpu.VMEM((tokens, width), BF16)
    scratch["ws"] = scratch["wc"] = pltpu.VMEM((2,) + w_self.shape, BF16)
    scratch["os"] = scratch["oc"] = pltpu.VMEM((2, hw, width), BF16)
    scratch["wu_buf"] = pltpu.VMEM((3, width, ublk), BF16)
    scratch["wd_buf"] = pltpu.VMEM((3, ublk, width), BF16)
    scratch["act_buf"] = scratch["dh_buf"] = pltpu.VMEM((2, ublk, slots), BF16)
    scratch["out_u"] = scratch["out_d"] = pltpu.VMEM((n_row, rows, units), BF16)
    scratch["out_s"] = scratch["out_x"] = pltpu.VMEM((n_row, rows, 4 * hw), BF16)
    scratch["abuf"] = pltpu.VMEM((n_row, rows, max(sizes.values())), BF16)
    scratch["load_sem"] = pltpu.SemaphoreType.DMA((n_row,))
    scratch["tok_in"] = scratch["cot_in"] = flat
    scratch["enc"] = pltpu.VMEM((n_row, tokens, width), BF16)
    scratch["tout"] = pltpu.VMEM((tokens, width), F32)
    for name in ("mid_t", "late_t", "acc_a", "acc_b"):
        scratch[name] = tall
    for name in ("tok_t", "x1", "x2", "x3", "ct", "mem_t", "e_low"):
        scratch[name] = low
    for name in ("q1", "k1", "v1", "q2", "k2", "v2", "eh"):
        scratch[name] = pltpu.VMEM((2 * hw, tokens), BF16)
    for name in ("attn1", "attn2"):
        scratch[name] = pltpu.VMEM((2, first + hw, tokens), BF16)
    for name in ("prob1", "prob2"):
        scratch[name] = pltpu.VMEM((heads * sents, slots, slots), BF16)
    scratch["grads"] = pltpu.VMEM((2, pad, tokens), BF16)
    for name in ("sum_a", "sum_b", "sum_c", "vec", "cols"):
        scratch[name] = pltpu.VMEM((width, 128), F32)
    scratch["colm"] = pltpu.VMEM((128, width), F32)
    scratch["bm"] = pltpu.VMEM((2, 16, width), F32)
    scratch["bvec"] = pltpu.VMEM((2, -(-hw // 128) * 128, 128), F32)
    scratch["bcols"] = pltpu.VMEM((2, -(-hw // 128) * 128, 8), F32)
    scratch["ubias"] = pltpu.VMEM((2, ublk, 128), F32)
    scratch["bups"] = pltpu.VMEM((2, ublk, 8), F32)
    if spread:
        scratch["small_dp"] = pltpu.VMEM((n_dp, 16, width), F32)
        scratch["small_row"] = pltpu.VMEM((n_row, 16, width), F32)
    dma = pltpu.SemaphoreType.DMA
    scratch["small_in"] = pltpu.VMEM((2, 16, width), F32)
    scratch["small_mp"] = pltpu.VMEM((16, width), F32)
    scratch["via"] = pltpu.VMEM((sents, slots, width), BF16)
    scratch["near"] = pltpu.VMEM((slots, width), BF16)
    scratch["near_sem"] = dma
    scratch["enc_s"] = scratch["enc_r"] = dma((sents, n_row - 1))
    scratch["via_s"] = scratch["via_r"] = dma((sents,))
    scratch["mem_s"] = scratch["mem_r"] = dma((sents, n_row))
    scratch["link_s"] = scratch["link_r"] = dma((6, n_row))
    scratch["local_sem"] = dma((16,))
    scratch["send_sem"] = scratch["recv_sem"] = dma((80,))
    scratch["fetch_sem"] = dma((2, 3))
    scratch["push_sem"] = scratch["land_sem"] = dma((2, blocks))
    names = list(scalars) + list(vectors) + list(arrays) + list(outs) + list(scratch)
    smem = pl.BlockSpec(memory_space=pltpu.SMEM)
    results = pl.pallas_call(
        functools.partial(layer_kernel, n_row, n_dp, names),
        out_shape=tuple(shape(s, t) for s, t, _ in outs.values()),
        in_specs=[smem] * len(scalars) + [VMEM] * len(vectors) + [ANY] * len(arrays),
        out_specs=tuple(spec for _, _, spec in outs.values()),
        scratch_shapes=list(scratch.values()),
        compiler_params=pltpu.CompilerParams(
            collective_id=0, has_side_effects=True, vmem_limit_bytes=63 << 20
        ),
    )(*scalars.values(), *vectors.values(), *arrays.values())
    return dict(zip(outs, results))


def per_device(
    tokens, encoder, layer_pick, piece_heads, piece_ffn, tgt_len, src_len, norm_gain, norm_shift,
    out_bias, w_self, o_self, b_self, w_cross, o_cross, b_cross, w_up, b_up, w_down, cotangent,
):
    n_row, n_dp = lax.axis_size("row"), lax.axis_size("dp")
    r, d, c = place()
    width = tokens.shape[1]
    units, hw = w_up.shape[1], w_self.shape[2]
    ublk = 256
    out = layer(
        n_row, n_dp,
        dict(
            layer_pick=layer_pick, piece_heads=piece_heads, piece_ffn=piece_ffn,
            tgt_len=tgt_len, src_len=src_len,
        ),
        dict(
            norm_gain=norm_gain, norm_shift=norm_shift, out_bias=out_bias,
            b_self=b_self, b_cross=b_cross, b_up=b_up.reshape(-1, ublk),
        ),
        dict(
            tokens=tokens, cotangent=cotangent, encoder=encoder.reshape(-1, width),
            w_self=jnp.swapaxes(w_self, 1, 2), o_self=o_self,
            w_cross=jnp.swapaxes(w_cross, 1, 2), o_cross=o_cross, w_up=w_up, w_down=w_down,
        ),
    )
    share = width // n_row // n_dp
    small = out["small"]
    if n_dp == 4:
        shards = [out["shard_" + name] for name in "sxud"]
    else:
        shards = [
            lax.psum_scatter(
                out["held_" + name].astype(F32).reshape(width, -1),
                ("row", "dp"), scatter_dimension=0, tiled=True,
            )
            for name in "sxud"
        ]
        small = lax.psum(small, ("row", "dp"))

    (
        block, gtok, grad_encoder, gain, shift, bias, w_s, o_s, b_s, w_x, o_x, b_x, w_u, b_u, w_d
    ) = outputs(
        layer_pick, out["block"].reshape(-1, width), out["gtok"].reshape(-1, width),
        out["glad"].reshape(-1, width), small, shards, share, hw, units, ublk,
    )
    return (
        block, gtok, grad_encoder.reshape(1, -1, width), gain, shift, bias,
        w_s, o_s.T, b_s, w_x, o_x.T, b_x, w_u, b_u.reshape(units), w_d.T,
    )


def outputs_kernel(
    share, hw, layer_pick, block_in, gtok_in, memory, small, shard_s, shard_x, shard_u, shard_d,
    block, gtok, encoder, gain, shift, bias, w_s, o_s, b_s, w_x, o_x, b_x, w_u, b_u, w_d,
):
    r, d, c = place()
    n_row, n_dp = layer_pick.shape[1], lax.axis_size("dp")
    width = memory.shape[1]
    step = pl.program_id(0)
    block[...] = block_in[...]
    gtok[...] = gtok_in[...]
    piece = lax.div(step * layer_pick.shape[0], pl.num_programs(0))
    pick = [jnp.full((1, width), layer_pick[piece, i].astype(F32), F32) for i in range(n_row)]
    mine = jnp.full((1, width), layer_pick[piece, r].astype(F32), F32)
    encoder[...] = mine / functools.reduce(jnp.add, pick) * memory[...].astype(F32)

    @pl.when(step == 0)
    def _():
        def own_rows(ref):
            if ref.shape[0] == share:
                return ref[...]
            across = lax.rem(d, 2)
            _, start_of = window(2 * share, share)
            return ref[pl.ds(pl.multiple_of(share * across - start_of(across), 8), share), :]

        def cut(values, i):
            if i:
                values = pltpu.roll(values, values.shape[1] - i * hw, 1)
            return values[:, :hw]

        values = own_rows(shard_s)
        for i in range(3):
            w_s[i] = cut(values, i)
        o_s[...] = cut(values, 3)
        values = own_rows(shard_x)
        for i in range(3):
            w_x[i] = cut(values, (2, 0, 1)[i])
        o_x[...] = cut(values, 3)
        w_u[...] = own_rows(shard_u)
        w_d[...] = own_rows(shard_d)
        at = (r * n_dp + d) * share
        norms = pltpu.roll(small[0:16, :], lax.rem(width - at, width), 1)
        gain[...] = norms[0:3, :share]
        shift[...] = norms[3:6, :share]
        bias[...] = norms[6:9, :share]
        b_s[...] = small[10:12, :hw]
        b_x[...] = small[12:14, :hw]
        aside = -(-hw // 128) * 128
        b_u[...] = small[10 : 10 + b_u.shape[0], aside : aside + b_u.shape[1]]


def outputs(layer_pick, block, gtok, memory, small, shards, share, hw, units, ublk):
    shape = jax.ShapeDtypeStruct
    steps, width = 4, memory.shape[1]
    cut = lambda v: pl.BlockSpec((v.shape[0] // steps, width), lambda i: (i, 0))
    sizes = [(3, share)] * 3 + [(3, share, hw), (share, hw), (2, hw)] * 2
    sizes += [(share, units), (units // ublk, ublk), (share, units)]
    tall = [block, gtok, memory]
    return pl.pallas_call(
        functools.partial(outputs_kernel, share, hw),
        grid=(steps,),
        out_shape=tuple(shape(v.shape, F32) for v in tall) + tuple(shape(v, F32) for v in sizes),
        in_specs=[pl.BlockSpec(memory_space=pltpu.SMEM)] + [cut(v) for v in tall] + [VMEM] * 5,
        out_specs=tuple(cut(v) for v in tall) + (VMEM,) * len(sizes),
        compiler_params=pltpu.CompilerParams(vmem_limit_bytes=62 << 20),
    )(layer_pick, block, gtok, memory, small, *shards)


def solution(mesh):
    return jax.shard_map(
        per_device,
        mesh=mesh,
        in_specs=(
            P(("row", "dp"), None),
            P("row", "dp", None),
            P(),
            P(),
            P(),
            P(("row", "dp")),
            P(("row", "dp")),
            P(),
            P(),
            P(),
            P(None, None, "mp"),
            P("mp", None),
            P(None, "mp"),
            P(None, None, "mp"),
            P("mp", None),
            P(None, "mp"),
            P(None, "mp"),
            P("mp"),
            P("mp", None),
            P(("row", "dp"), None),
        ),
        out_specs=(
            P(("row", "dp"), None),
            P(("row", "dp"), None),
            P("row", "dp", None),
            P(None, ("row", "dp")),
            P(None, ("row", "dp")),
            P(None, ("row", "dp")),
            P(None, ("row", "dp"), "mp"),
            P("mp", ("row", "dp")),
            P(None, "mp"),
            P(None, ("row", "dp"), "mp"),
            P("mp", ("row", "dp")),
            P(None, "mp"),
            P(("row", "dp"), "mp"),
            P("mp"),
            P("mp", ("row", "dp")),
        ),
        check_vma=False,
    )
```

```python
import functools
import types
import jax
import jax.numpy as jnp
from jax import lax
from jax.experimental import pallas as pl
from jax.experimental.pallas import tpu as pltpu
from jax.sharding import PartitionSpec as P

HD = 80
EPSILON = 1e-05
MASKED = -1e30
F32, BF16 = jnp.float32, jnp.bfloat16
MESH = pl.DeviceIdType.MESH
ANY = pl.BlockSpec(memory_space=pl.ANY)
VMEM = pl.BlockSpec(memory_space=pltpu.VMEM)


def nn(a, b):
    return lax.dot_general(a, b, (((1,), (0,)), ((), ())), preferred_element_type=F32)


def nt(a, b):
    return lax.dot_general(a, b, (((1,), (1,)), ((), ())), preferred_element_type=F32)


def tn(a, b):
    return lax.dot_general(a, b, (((0,), (0,)), ((), ())), preferred_element_type=F32)


def lanes(i, n):
    return pl.ds(pl.multiple_of(i * n, n), n)


def layer_norm(v_ref, x_ref, gain, shift, begin, end):
    @pl.loop(begin // 128, end // 128)
    def _(i):
        v = v_ref[:, lanes(i, 128)].astype(F32)
        c = v - jnp.mean(v, axis=0, keepdims=True)
        r = lax.rsqrt(jnp.mean(c * c, axis=0, keepdims=True) + EPSILON)
        x_ref[:, lanes(i, 128)] = (c * r * gain + shift).astype(BF16)


def norm_back(v_ref, gain, up_ref, base_ref, out_ref, low_ref, sums, begin, end):
    gain_sum, shift_sum, bias_sum = sums
    if begin == 0:
        for ref in sums:
            ref[...] = jnp.zeros_like(ref)

    @pl.loop(begin // 128, end // 128)
    def _(i):
        at = lanes(i, 128)
        v = v_ref[:, at].astype(F32)
        c = v - jnp.mean(v, axis=0, keepdims=True)
        r = lax.rsqrt(jnp.mean(c * c, axis=0, keepdims=True) + EPSILON)
        xhat = c * r
        e = up_ref[:, at]
        gain_sum[...] += e * xhat
        shift_sum[...] += e
        eg = e * gain
        m1 = jnp.mean(eg, axis=0, keepdims=True)
        m2 = jnp.mean(eg * xhat, axis=0, keepdims=True)
        out = base_ref[:, at].astype(F32) + r * (eg - m1 - xhat * m2)
        out_ref[:, at] = out
        low = out.astype(BF16)
        low_ref[:, at] = low
        bias_sum[...] += low.astype(F32)


def attend(q_ref, k_ref, v_ref, out_ref, prob_ref, masks, head_on, hd, per, sents):
    groups, slots = out_ref.shape[0], q_ref.shape[1] // sents
    first = out_ref.shape[1] - per * hd
    for g in range(groups):

        @pl.loop(0, per, unroll=2 * sents // len(masks))
        def _(h, g=g):
            rows = pl.ds(pl.multiple_of((g * per + h) * hd, 16), hd)
            to = pl.ds(pl.multiple_of(first + h * hd, 16), hd)
            for s, mask in masks.items():
                at = slice(s * slots, (s + 1) * slots)
                scores = tn(k_ref[rows, at], q_ref[rows, at]) * hd ** (-0.5)
                scores = jnp.where(mask, scores, MASKED)
                e = jnp.exp(scores - jnp.max(scores, axis=0, keepdims=True))
                total = jnp.sum(e, axis=0, keepdims=True)
                p = (e * (1.0 / total)).astype(BF16)
                prob_ref[(g * per + h) * sents + s] = p
                mixed = nn(v_ref[rows, at], p) * head_on(g, h)
                out_ref[g, to, at] = mixed.astype(BF16)


def attend_back(q_ref, k_ref, v_ref, e_ref, prob_ref, d_ref, at_rows, hd, per, sents, some):
    groups, slots = d_ref.shape[0], q_ref.shape[1] // sents
    for g in range(groups):

        @pl.loop(0, per, unroll=2 * sents // len(some))
        def _(h, g=g):
            rows = pl.ds(pl.multiple_of((g * per + h) * hd, 16), hd)
            dq_at, dk_at, dv_at = [
                pl.ds(pl.multiple_of(first + h * hd, 16), hd) for first in at_rows
            ]
            for s in some:
                at = slice(s * slots, (s + 1) * slots)
                e, p = e_ref[rows, at], prob_ref[(g * per + h) * sents + s]
                d_ref[g, dv_at, at] = nt(e, p).astype(BF16)
                dp = tn(v_ref[rows, at], e)
                pf = p.astype(F32)
                delta = jnp.sum(pf * dp, axis=0, keepdims=True)
                ds = (pf * (dp - delta) * hd ** (-0.5)).astype(BF16)
                d_ref[g, dq_at, at] = nn(k_ref[rows, at], ds).astype(BF16)
                d_ref[g, dk_at, at] = nt(q_ref[rows, at], ds).astype(BF16)


def lane_sum(values):
    return jnp.sum(values.astype(F32), axis=1, keepdims=True)


def place():
    return tuple(lax.axis_index(name) for name in ("row", "dp", "mp"))


def window(rows, share):
    wide = max(
        -(-(i + 1) * share // 16) * 16 - i * share // 16 * 16 for i in range(rows // share)
    )
    return wide, lambda i: pl.multiple_of(
        jnp.minimum(i * share // 16 * 16, rows - wide), 16
    )


def remote(src, dst, send_sem, recv_sem, peer):
    return pltpu.make_async_remote_copy(
        src_ref=src, dst_ref=dst, send_sem=send_sem, recv_sem=recv_sem,
        device_id=peer, device_id_type=MESH,
    )


def started(copy):
    copy.start()
    return copy


def layer_kernel(n_row, n_dp, names, *args):
    refs = dict(zip(names, args))
    ref = types.SimpleNamespace(**refs)
    layer_pick, piece_heads, piece_ffn, tgt_len, src_len = (ref.layer_pick, ref.piece_heads, ref.piece_ffn, ref.tgt_len, ref.src_len)
    tokens, cotangent, encoder = (ref.tokens, ref.cotangent, ref.encoder)
    ws, wc, os_, oc, wu_buf, wd_buf = (ref.ws, ref.wc, ref.os, ref.oc, ref.wu_buf, ref.wd_buf)
    act_buf, dh_buf, load_sem = ref.act_buf, ref.dh_buf, ref.load_sem
    via, near, near_sem = ref.via, ref.near, ref.near_sem
    enc_s, enc_r, via_s, via_r = ref.enc_s, ref.enc_r, ref.via_s, ref.via_r
    mem_s, mem_r, link_s, link_r = ref.mem_s, ref.mem_r, ref.link_s, ref.link_r
    tok_in, cot_in, enc, tout, tok_t, mid_t, late_t, acc_a, acc_b = (ref.tok_in, ref.cot_in, ref.enc, ref.tout, ref.tok_t, ref.mid_t, ref.late_t, ref.acc_a, ref.acc_b)
    x1, x2, x3, ct, mem_t, e_low, eh = (ref.x1, ref.x2, ref.x3, ref.ct, ref.mem_t, ref.e_low, ref.eh)
    q1, k1, v1, q2, k2, v2 = (ref.q1, ref.k1, ref.v1, ref.q2, ref.k2, ref.v2)
    attn1, attn2, prob1, prob2, grads = (ref.attn1, ref.attn2, ref.prob1, ref.prob2, ref.grads)
    sum_a, sum_b, sum_c, vec, bvec, ubias, colm, cols, bm, bcols, bups = (ref.sum_a, ref.sum_b, ref.sum_c, ref.vec, ref.bvec, ref.ubias, ref.colm, ref.cols, ref.bm, ref.bcols, ref.bups)
    out_s, out_x, out_u, out_d, abuf = (ref.out_s, ref.out_x, ref.out_u, ref.out_d, ref.abuf)
    local_sem, send_sem, recv_sem, fetch_sem, push_sem, land_sem = (ref.local_sem, ref.send_sem, ref.recv_sem, ref.fetch_sem, ref.push_sem, ref.land_sem)
    held, came = (ref.held_s, ref.held_x, ref.held_u, ref.held_d), (ref.came_s, ref.came_x, ref.came_u, ref.came_d)
    small, glad = (ref.small, ref.glad)
    spread = n_dp == 4

    width, tokens_here = tok_t.shape
    groups, _, hw, _ = ws.shape
    units, ublk, hd = ref.w_up.shape[1], bups.shape[1], HD
    blocks, per = units // ublk, hw // HD
    rows = width // n_row
    sents = tgt_len.shape[0] // 2
    slots = tokens_here // sents
    pad = -(-3 * hw // 128) * 128
    lead = 3 * hw // 128 * 128
    first = 3 * hw - lead
    r, d, c = place()
    partner = (r, d, 1 - c)
    rings = [(r, lax.rem(d + i, n_dp), c) for i in range(1, n_dp)] if spread else []
    lines = [(lax.rem(r + i, n_row), d, c) for i in range(1, n_row)]
    counts = {"local": 0, "link": 0}

    def fetch(src, dst):
        i = counts["local"]
        counts["local"] += 1
        return started(pltpu.make_async_copy(src, dst, local_sem.at[i]))

    def push(src, dst, peer):
        i = counts["link"]
        counts["link"] += 1
        return started(remote(src, dst, send_sem.at[i], recv_sem.at[i], peer))

    mine = pl.ds(pl.multiple_of(c * tokens_here, tokens_here), tokens_here)
    tok_copy = fetch(tokens.at[mine], tok_in)
    ws_copies = [fetch(ref.w_self, ws.at[0]), fetch(ref.o_self, os_.at[0])]
    bm[...] = jnp.zeros_like(bm)
    bm[0, 0:2, :hw] = ref.b_self[...]
    bm[0, 2:4, :hw] = ref.b_cross[...]
    bm[0, 8 : 8 + blocks, :ublk] = ref.b_up[...]
    colm[...] = jnp.zeros_like(colm)
    colm[0:3] = ref.norm_gain[...]
    colm[3:6] = ref.norm_shift[...]
    colm[6:9] = ref.out_bias[...]
    barrier = pltpu.get_barrier_semaphore()
    peers = [partner] + rings + lines
    for peer in peers:
        pl.semaphore_signal(barrier, inc=1, device_id=peer, device_id_type=MESH)
    pl.semaphore_wait(barrier, len(peers))
    ws_copies += [
        push(ref.w_self, ws.at[1], partner),
        push(bm.at[0], bm.at[1], partner),
        push(ref.o_self, os_.at[1], partner),
    ]
    def sentence(piece, i):
        start = (piece * 2 + c) * tokens_here + i * slots
        return encoder.at[pl.ds(pl.multiple_of(start, slots), slots)]

    columns = [slice(i * slots, (i + 1) * slots) for i in range(sents)]

    middle = (r == 1) | (r == 2)
    target, far = lax.rem(r + 2, 4), lax.rem(r + 1 + 2 * (2 - r), 4)
    merged = n_row == 4

    def block_to(i, k):
        peer = lines[k - 1]
        return remote(
            sentence(peer[0], i), enc.at[r, columns[i]], enc_s.at[i, k - 1], enc_r.at[i, k - 1], peer
        )

    def block_via(i):
        peer = (jnp.where(r == 0, 1, 2), d, c)
        return remote(sentence(3 - r, i), via.at[i], via_s.at[i], via_r.at[i], peer)

    def block_sum(i):
        return remote(
            via.at[i], enc.at[r, columns[i]], enc_s.at[i, 1], enc_r.at[i, 1], (target, d, c)
        )

    def block_near(i):
        return pltpu.make_async_copy(sentence(target, i), near, near_sem)

    own_blocks = []

    def send_far(i):
        own_blocks.append(fetch(sentence(r, i), enc.at[r, columns[i]]))
        if merged:

            @pl.when(middle)
            def _():
                block_near(i).start()

            @pl.when(jnp.logical_not(middle))
            def _():
                block_via(i).start()

    def send_blocks(i):
        if not merged:
            for k in range(1, n_row):
                block_to(i, k).start()
            return

        @pl.when(r != 3)
        def _():
            block_to(i, 1).start()

        @pl.when(r != 0)
        def _():
            block_to(i, 3).start()

        @pl.when(jnp.logical_not(middle))
        def _():
            block_to(i, 2).start()

    def send_sum(i):
        if merged:

            @pl.when(middle)
            def _():
                picks = [
                    jnp.full((1, width), layer_pick[target, j].astype(F32), F32)
                    for j in range(n_row)
                ]
                total = functools.reduce(jnp.add, picks)
                far_pick = jnp.full((1, width), layer_pick[target, far].astype(F32), F32)
                near_pick = jnp.full((1, width), layer_pick[target, r].astype(F32), F32)
                block_near(i).wait()
                block_via(i).wait_recv()
                via[i] = (
                    far_pick / total * via[i].astype(F32) + near_pick / total * near[...].astype(F32)
                ).astype(BF16)
                block_sum(i).start()

    def wait_blocks(i):
        own_blocks[i].wait()
        if not merged:
            for k in range(1, n_row):
                block_to(i, k).wait()
            return

        @pl.when(r != 3)
        def _():
            block_to(i, 1).wait_send()
            block_to(i, 3).wait_recv()

        @pl.when(r != 0)
        def _():
            block_to(i, 3).wait_send()
            block_to(i, 1).wait_recv()

        @pl.when(middle)
        def _():
            block_sum(i).wait_send()

        @pl.when(jnp.logical_not(middle))
        def _():
            block_to(i, 2).wait_send()
            block_via(i).wait_send()

        block_to(i, 2).wait_recv()

    send_far(0)
    if merged:

        @pl.when(r == 0)
        def _():
            enc[3] = jnp.zeros(enc.shape[1:], BF16)

        @pl.when(r == 3)
        def _():
            enc[0] = jnp.zeros(enc.shape[1:], BF16)

    wc_copies = [
        fetch(ref.w_cross, wc.at[0]),
        fetch(ref.o_cross, oc.at[0]),
        push(ref.w_cross, wc.at[1], partner),
        push(ref.o_cross, oc.at[1], partner),
    ]
    cot_copy = fetch(cotangent.at[mine], cot_in)
    ffn_copies = [
        push(ref.w_up, ref.up_in, partner),
        push(ref.w_down, ref.down_in, partner),
    ]

    cols[...] = colm[...].T
    gain, shift, obias = [[cols[:, j : j + 1] for j in range(3 * i, 3 * i + 3)] for i in range(3)]
    key_at = lax.broadcasted_iota(jnp.int32, (slots, slots), 0)
    query_at = lax.broadcasted_iota(jnp.int32, (slots, slots), 1)
    for zeroed in (attn1, attn2):
        zeroed[:, :first, :] = jnp.zeros((groups, first, tokens_here), BF16)
    grads[:, 3 * hw :, :] = jnp.zeros((groups, pad - 3 * hw, tokens_here), BF16)
    vec[...] = jnp.zeros_like(vec)
    bvec[...] = jnp.zeros_like(bvec)
    ubias[...] = jnp.zeros_like(ubias)
    heads_here, units_here = piece_heads[r], piece_ffn[r]
    group_at = [c, 1 - c]

    def head_on(g, h):
        return jnp.where(group_at[g] * per + h < heads_here, 1.0, 0.0)

    tok_copy.wait()
    tok_t[...] = tok_in[...].astype(F32).T.astype(BF16)
    layer_norm(tok_t, x1, gain[0], shift[0], 0, tokens_here)
    for copy in ws_copies:
        copy.wait()
    for g in range(groups):
        bcols[g] = bm[g, 0:8, : bcols.shape[1]].T
        bups[g] = bm[g, 8:16, :ublk].T
    for g in range(groups):
        at = slice(g * hw, (g + 1) * hw)
        q1[at] = (nn(ws[g, 0], x1[...]) + bcols[g, :hw, 0:1]).astype(BF16)
        k1[at] = nn(ws[g, 1], x1[...]).astype(BF16)
        v1[at] = (nn(ws[g, 2], x1[...]) + bcols[g, :hw, 1:2]).astype(BF16)
    send_blocks(0)
    masks = {
        i: (key_at <= query_at) & (key_at < tgt_len[c * sents + i]) for i in range(sents)
    }
    attend(q1, k1, v1, attn1, prob1, masks, head_on, hd, per, sents)
    send_sum(0)
    acc_a[...] = tn(os_[0], attn1[0, first:])
    for g in range(1, groups):
        acc_a[...] += tn(os_[g], attn1[g, first:])
    mid_t[...] = tok_t[...].astype(F32) + acc_a[...] + obias[0]
    layer_norm(mid_t, x2, gain[1], shift[1], 0, tokens_here)
    for copy in wc_copies:
        copy.wait()
    for g in range(groups):
        at = slice(g * hw, (g + 1) * hw)
        q2[at] = (nn(wc[g, 0], x2[...]) + bcols[g, :hw, 2:3]).astype(BF16)
    cot_copy.wait()
    ct[...] = cot_in[...].astype(F32).T.astype(BF16)

    picks = [
        jnp.full((1, width), layer_pick[r, i].astype(F32), F32) for i in range(layer_pick.shape[1])
    ]
    total = functools.reduce(jnp.add, picks)
    weights = [pick / total for pick in picks]
    if merged:
        summed = [False, r == 3, r == 0, False]
        absent = [r == 3, False, False, r == 0]
        weights = [
            jnp.where(one, 1.0, jnp.where(none, 0.0, weight))
            for one, none, weight in zip(summed, absent, weights)
        ]
    def cross(i):
        at = columns[i]
        wait_blocks(i)
        if i + 1 < sents:
            send_far(i + 1)
        if i > 0:
            send_memory(i - 1)
        memory = weights[0] * enc[0, at].astype(F32)
        for j in range(1, n_row):
            memory += weights[j] * enc[j, at].astype(F32)
        mem_t[:, at] = memory.T.astype(BF16)
        for g in range(groups):
            to = slice(g * hw, (g + 1) * hw)
            k2[to, at] = nn(wc[g, 1], mem_t[:, at]).astype(BF16)
            v2[to, at] = (nn(wc[g, 2], mem_t[:, at]) + bcols[g, :hw, 3:4]).astype(BF16)
        masks = {i: key_at < src_len[c * sents + i]}
        attend(q2, k2, v2, attn2, prob2, masks, head_on, hd, per, sents)
        branch = tn(oc[0], attn2[0, first:, at])
        for g in range(1, groups):
            branch += tn(oc[g], attn2[g, first:, at])
        late_t[:, at] = mid_t[:, at] + branch + obias[1]
        layer_norm(late_t, x3, gain[2], shift[2], at.start, at.stop)
        if i + 1 < sents:
            send_blocks(i + 1)

    def slot_of(phase, i):
        return lax.rem(phase * blocks + i, 3)

    def fetches(phase, i):
        slot, at = slot_of(phase, i), lanes(i, ublk)
        up, down = (ref.w_up, ref.w_down) if phase else (ref.up_in, ref.down_in)
        return [
            pltpu.make_async_copy(up.at[:, at], wu_buf.at[slot], fetch_sem.at[0, slot]),
            pltpu.make_async_copy(down.at[at, :], wd_buf.at[slot], fetch_sem.at[1, slot]),
        ]

    def pushes(i, k):
        at = lanes(i, ublk)
        return remote(
            (out_u, out_d)[k].at[:, :, at], came[2 + k].at[:, :, at],
            push_sem.at[k, i], land_sem.at[k, i], partner,
        )

    def feed_forward(n, ready):
        cols_at = columns[n]
        if n == 0:
            for copy in ready:
                copy.wait()
            for copy in fetches(0, 0):
                copy.start()
        acc_a[:, cols_at] = jnp.zeros((width, slots), F32)
        acc_b[:, cols_at] = jnp.zeros((width, slots), F32)

        def hidden(phase, i):
            g, slot, at = 1 - phase, slot_of(phase, i), lax.rem(i, 2)
            up, down = wu_buf.at[slot], wd_buf.at[slot]
            here = lax.broadcasted_iota(jnp.int32, bups.shape[1:], 1) == i
            h = nn(up[...].T, x3[:, cols_at]) + lane_sum(jnp.where(here, bups[g], 0.0))
            unit = group_at[g] * units + i * ublk
            unit = unit + lax.broadcasted_iota(jnp.int32, (ublk, 1), 0)
            on = jnp.where(unit < units_here, 1.0, 0.0)
            squared = h * h
            t = jnp.tanh(h * (0.7978845608028654 + 0.0356774081363001 * squared))
            cdf = 0.5 + 0.5 * t
            slope = cdf + h * (0.5 - 0.5 * t * t) * (
                0.7978845608028654 + 0.1070322244089003 * squared
            )
            act_buf[at] = (h * cdf * on).astype(BF16)
            dh = (nn(down[...], ct[:, cols_at]) * (slope * on)).astype(BF16)
            dh_buf[at] = dh
            in_sums = lax.broadcasted_iota(jnp.int32, ubias.shape[1:], 1) == i
            ubias[g] += jnp.where(in_sums, lane_sum(dh), 0.0)

        def spread_block(phase, i):
            slot, at = slot_of(phase, i), lax.rem(i, 2)
            sink_u, sink_d = (held[2], held[3]) if phase else (out_u, out_d)
            act, dh = act_buf[at], dh_buf[at]
            acc_a[:, cols_at] += tn(wd_buf[slot], act)
            acc_b[:, cols_at] += nn(wu_buf[slot], dh)
            shape, to = (n_row, rows, ublk), lanes(i, ublk)
            grad_u = nt(x3[:, cols_at], dh).reshape(shape)
            grad_d = nt(ct[:, cols_at], act).reshape(shape)
            if n > 0:
                grad_u += sink_u[:, :, to].astype(F32)
                grad_d += sink_d[:, :, to].astype(F32)
            sink_u[:, :, to] = grad_u.astype(BF16)
            sink_d[:, :, to] = grad_d.astype(BF16)

        def finished(i):
            if n + 1 == sents:
                for k in range(2):
                    pushes(i, k).start()

        for phase in range(2):
            more = phase == 0 or n + 1 < sents
            for copy in fetches(phase, 0):
                copy.wait()
            for copy in fetches(phase, 1):
                copy.start()
            hidden(phase, 0)
            if phase == 1:
                if n + 1 < sents:
                    send_sum(n + 1)
                spread_block(0, blocks - 1)
                finished(blocks - 1)

            @pl.loop(1, blocks)
            def _(i, phase=phase, more=more):
                for copy in fetches(phase, i):
                    copy.wait()

                @pl.when(i + 1 < blocks)
                def _():
                    for copy in fetches(phase, i + 1):
                        copy.start()

                if more:

                    @pl.when(i + 1 == blocks)
                    def _():
                        for copy in fetches(1 - phase, 0):
                            copy.start()

                hidden(phase, i)
                spread_block(phase, i - 1)
                if phase == 0:
                    finished(i - 1)

        spread_block(1, blocks - 1)
        tout[cols_at] = (late_t[:, cols_at] + acc_a[:, cols_at] + obias[2]).T
        norm_back(
            late_t, gain[2], acc_b, ct, acc_a, e_low, (sum_a, sum_b, sum_c),
            cols_at.start, cols_at.stop,
        )

    late = []
    half = rows // 2
    wide, start_of = window(half, half // 2)
    up, across = lax.div(d, 2), lax.rem(d, 2)
    ours = half * up + start_of(across)
    pieces = {
        "u": (2, 0, units, True),
        "d": (3, 0, units, False),
        "x_a": (1, 0, 2 * hw, True),
        "x_b": (1, 2 * hw, 4 * hw, False),
        "s_a": (0, 0, 2 * hw, True),
        "s_b": (0, 2 * hw, 4 * hw, False),
    }

    def add_in(part, begin, end, landing, places, shard=None):
        size = landing.shape[1]
        at = pl.ds(begin, end - begin)
        loads = [
            pltpu.make_async_copy(
                landing.at[z], abuf.at[z, pl.ds(0, size), pl.ds(0, end - begin)], load_sem.at[z]
            )
            for z in range(n_row)
        ]
        for load in loads:
            load.start()
        for z in range(n_row):
            loads[z].wait()
            for to, source, count in places:

                step = 80 if count % 80 == 0 else 48 if count % 48 == 0 else 16

                @pl.loop(0, count // step)
                def _(j, z=z, to=to, source=source, step=step):
                    held_at = pl.ds(pl.multiple_of(to + step * j, 16), step)
                    from_at = pl.ds(pl.multiple_of(source + step * j, 16), step)
                    total = held[part][z, held_at, at].astype(F32)
                    total += abuf[z, from_at, pl.ds(0, end - begin)].astype(F32)
                    held[part][z, held_at, at] = total.astype(BF16)
                    if shard is not None:

                        @pl.when(r == z)
                        def _():
                            shard[from_at, at] = total

    def take(part, arrived):
        for copy in arrived:
            copy()
        add_in(part, 0, held[part].shape[2], came[part], [(0, 0, rows)])

    def first_ring(name):
        if not spread:
            return []
        part, begin, end, tall_first = pieces[name]
        landing, at = refs["ring_" + name], pl.ds(begin, end - begin)
        if tall_first:
            peer = (r, lax.rem(d + 2, 4), c)
            return [push(held[part].at[:, pl.ds(half * (1 - up), half), at], landing, peer)]
        peer = (r, d + 1 - 2 * across, c)
        return [
            push(
                held[part].at[:, pl.ds(half * i + start_of(1 - across), wide), at],
                landing.at[:, pl.ds(wide * i, wide)], peer,
            )
            for i in range(2)
        ]

    def second_ring(name, copies):
        if not spread:
            return []
        part, begin, end, tall_first = pieces[name]
        landing, at = refs["ring_" + name], pl.ds(begin, end - begin)
        for copy in copies:
            copy.wait()
        if tall_first:
            add_in(part, begin, end, landing, [(half * up, 0, half)])
            peer, gone = (r, d + 1 - 2 * across, c), half * up + start_of(1 - across)
        else:
            places = [(half * i + start_of(across), wide * i, wide) for i in range(2)]
            add_in(part, begin, end, landing, places)
            peer, gone = (r, lax.rem(d + 2, 4), c), half * (1 - up) + start_of(across)
        gone = pl.multiple_of(gone, 16)
        return [push(held[part].at[:, pl.ds(gone, wide), at], refs["turn_" + name], peer)]

    def to_lines(name, copies):
        if not spread:
            return []
        part, begin, end, _ = pieces[name]
        for copy in copies:
            copy.wait()
        shard = refs["shard_" + "sxud"[part]]
        add_in(part, begin, end, refs["turn_" + name], [(pl.multiple_of(ours, 16), 0, wide)], shard)
        if not merged:
            for k in range(1, n_row):
                line_to(name, k).start()
            return [name]

        @pl.when(middle)
        def _():
            line_to(name, 1).start()
            line_to(name, 3).start()

        @pl.when(jnp.logical_not(middle))
        def _():
            line_via(name).start()

        return [name]

    def line_rest(name):
        if spread and merged:

            @pl.when(r == 0)
            def _():
                line_to(name, 1).start()

            @pl.when(r == 3)
            def _():
                line_to(name, 3).start()

            @pl.when(jnp.logical_not(middle))
            def _():
                line_to(name, 2).start()


    def line_part(name):
        part, begin, end, _ = pieces[name]
        return part, pl.ds(pl.multiple_of(ours, 16), wide), pl.ds(begin, end - begin)

    def line_to(name, k):
        part, here, at = line_part(name)
        p = list(pieces).index(name)
        peer = lines[k - 1]
        return remote(
            held[part].at[peer[0], here, at], refs["line_" + "sxud"[part]].at[k - 1, :, at],
            link_s.at[p, k - 1], link_r.at[p, k - 1], peer,
        )

    def line_via(name):
        part, here, at = line_part(name)
        p = list(pieces).index(name)
        peer = (jnp.where(r == 0, 1, 2), d, c)
        return remote(
            held[part].at[3 - r, here, at], refs["far_" + "sxud"[part]].at[:, at],
            link_s.at[p, n_row - 1], link_r.at[p, n_row - 1], peer,
        )

    def line_sum(name):
        if spread and merged:

            @pl.when(middle)
            def _():
                part, here, at = line_part(name)
                line_via(name).wait_recv()
                total = held[part][target, here, at].astype(F32)
                total += refs["far_" + "sxud"[part]][:, at].astype(F32)
                held[part][target, here, at] = total.astype(BF16)
                line_to(name, 2).start()

    def sum_lines(part, names):
        if not spread:
            return
        shard, line = refs["shard_" + "sxud"[part]], refs["line_" + "sxud"[part]]

        def arrived(k):
            for name in names:
                line_to(name, k).wait_recv()
            shard[...] += line[k - 1].astype(F32)

        if not merged:
            for k in range(1, n_row):
                for name in names:
                    line_to(name, k).wait_send()
                arrived(k)
            return

        @pl.when(r != 0)
        def _():
            for name in names:
                line_to(name, 3).wait_send()
            arrived(1)

        @pl.when(r != 3)
        def _():
            for name in names:
                line_to(name, 1).wait_send()
            arrived(3)

        @pl.when(jnp.logical_not(middle))
        def _():
            for name in names:
                line_via(name).wait_send()

        for name in names:
            line_to(name, 2).wait_send()
        arrived(2)

    def heads_back(weight, at):
        for g in range(groups):
            for h in range(per):
                to = slice(h * hd, (h + 1) * hd)
                eh[g * hw + h * hd : g * hw + (h + 1) * hd, at] = (
                    nn(weight[g, to], e_low[:, at]) * head_on(g, h)
                ).astype(BF16)

    def cross_back(i):
        at = columns[i]
        heads_back(oc, at)
        attend_back(q2, k2, v2, eh, prob2, grads, (2 * hw, 0, hw), hd, per, sents, [i])
        total = jnp.zeros((width, slots), F32)
        for g in range(groups):
            total += tn(wc[g, 1], grads[g, :hw, at]) + tn(wc[g, 2], grads[g, hw : 2 * hw, at])
        tok_in[at] = total.T.astype(BF16)
        late.append(fetch(tok_in.at[at], glad.at[r, c, at]))
        late.append(push(tok_in.at[at], glad.at[r, c, at], partner))

    def memory_to(i, k):
        at = columns[i]
        return remote(
            tok_in.at[at], glad.at[r, c, at], mem_s.at[i, k - 1], mem_r.at[i, k - 1], lines[k - 1]
        )

    def memory_on(i):
        came_at = glad.at[lax.rem(r + 2, 4), c, columns[i]]
        peer, k = (jnp.where(r == 2, 3, 0), d, c), jnp.where(r == 2, 2, 0)
        return remote(came_at, came_at, mem_s.at[i, n_row - 1], mem_r.at[i, k], peer)

    def share_memory(i, k):
        came_at = glad.at[lax.rem(r + n_row - k, n_row), c, columns[i]]
        late.append(push(came_at, came_at, partner))

    def send_memory(i):
        if merged:

            @pl.when(r != 3)
            def _():
                memory_to(i, 1).start()

            @pl.when(r != 0)
            def _():
                memory_to(i, 3).start()

            memory_to(i, 2).start()
        else:
            for k in range(1, n_row):
                memory_to(i, k).start()

    def pass_memory(i):
        if merged:
            memory_to(i, 2).wait()

            @pl.when(middle)
            def _():
                memory_on(i).start()

            share_memory(i, 2)

    def wait_memory(i):
        if not merged:
            for k in range(1, n_row):
                memory_to(i, k).wait()
                share_memory(i, k)
            return

        @pl.when(r != 3)
        def _():
            memory_to(i, 1).wait_send()

        @pl.when(r != 0)
        def _():
            memory_to(i, 3).wait_send()

        @pl.when(middle)
        def _():
            memory_on(i).wait_send()

        for k in (1, 3):
            memory_to(i, k).wait_recv()
            share_memory(i, k)

    for i in range(sents):
        cross(i)
        feed_forward(i, ffn_copies)
        if i + 1 == sents:
            block_copies = [fetch(tout, ref.block.at[c]), push(tout, ref.block.at[c], partner)]
            take(2, [pushes(j, 0).wait for j in range(blocks)])
            ring_u = first_ring("u")
            take(3, [pushes(j, 1).wait for j in range(blocks)])
            ring_d = first_ring("d")
        cross_back(i)
    for i in range(sents - 1):
        pass_memory(i)
    send_memory(sents - 1)
    vec[:, 8:9] = lane_sum(ct[...])
    vec[:, 2:3] = lane_sum(sum_a[...])
    vec[:, 5:6] = lane_sum(sum_b[...])
    vec[:, 7:8] = lane_sum(sum_c[...])

    def put(g, begin, value):
        sink = (held_now, out_now)[g]
        at = pl.ds(begin, value.shape[1])
        sink[:, :, at] = value.astype(BF16).reshape(n_row, rows, -1)

    def weight_grads(g, sources, attn):
        tail = nt(e_low[...], attn[g])
        begin = 0
        for source, end in sources:
            while begin < end:
                step = min(256, end - begin)
                value = nt(source[...], grads[g, begin : begin + step])
                if begin + step == pad:
                    keep = lead - begin
                    if keep:
                        put(g, begin, value[:, :keep])
                    put(g, lead, value[:, keep:] + tail[:, : pad - lead])
                else:
                    put(g, begin, value)
                begin += step
        put(g, pad, tail[:, pad - lead :])

    held_now, out_now = held[1], out_x
    for g in (1, 0):
        bvec[g, :hw, 2:3] = lane_sum(grads[g, 2 * hw : 3 * hw])
        bvec[g, :hw, 3:4] = lane_sum(grads[g, hw : 2 * hw])
        weight_grads(g, [(mem_t, 2 * hw), (x2, pad)], attn2)
        if g == 1:
            came_x = push(out_x, came[1], partner)
            acc_b[...] = tn(wc[g, 0], grads[g, 2 * hw : 3 * hw])
        else:
            acc_b[...] += tn(wc[g, 0], grads[g, 2 * hw : 3 * hw])
    norm_back(
        mid_t, gain[1], acc_b, acc_a, acc_a, e_low, (sum_a, sum_b, sum_c), 0, tokens_here
    )
    vec[:, 1:2] = lane_sum(sum_a[...])
    vec[:, 4:5] = lane_sum(sum_b[...])
    vec[:, 6:7] = lane_sum(sum_c[...])
    take(1, [came_x.wait])
    ring_x = [first_ring("x_a"), first_ring("x_b")]

    heads_back(os_, slice(0, tokens_here))
    attend_back(q1, k1, v1, eh, prob1, grads, (0, hw, 2 * hw), hd, per, sents, range(sents))
    ring_u = second_ring("u", ring_u)
    ring_d = second_ring("d", ring_d)
    held_now, out_now = held[0], out_s
    for g in (1, 0):
        bvec[g, :hw, 0:1] = lane_sum(grads[g, :hw])
        bvec[g, :hw, 1:2] = lane_sum(grads[g, 2 * hw : 3 * hw])
        weight_grads(g, [(x1, pad)], attn1)
        if g == 1:
            came_s = push(out_s, came[0], partner)
    for g in range(groups):
        for j in range(3):
            part = tn(ws[g, j], grads[g, j * hw : (j + 1) * hw])
            if g == 0 and j == 0:
                acc_b[...] = part
            else:
                acc_b[...] += part
    take(0, [came_s.wait])
    ring_s = [first_ring("s_a"), first_ring("s_b")]
    norm_back(
        tok_t, gain[0], acc_b, acc_a, acc_a, e_low, (sum_a, sum_b, sum_c), 0, tokens_here
    )
    vec[:, 0:1] = lane_sum(sum_a[...])
    vec[:, 3:4] = lane_sum(sum_b[...])
    for copy in block_copies:
        copy.wait()
    tout[...] = acc_a[...].T
    late += [fetch(tout, ref.gtok.at[c]), push(tout, ref.gtok.at[c], partner)]

    pass_memory(sents - 1)

    small_in, small_mp = ref.small_in, ref.small_mp
    aside = -(-hw // 128) * 128
    for g in range(groups):
        small_in[g] = vec[...].T[0:16]
        small_in[g, 10:14, :hw] = bvec[g].T[0:4, :hw]
        small_in[g, 10 : 10 + blocks, aside : aside + ublk] = ubias[g].T[0:blocks]
    push(small_in.at[1], small_mp, partner).wait()
    small[...] = small_in[0] + small_mp[...]
    if spread:
        small_dp, small_row = ref.small_dp, ref.small_row
        small_dp[d] = small[...]
        small_copies = [push(small_dp.at[d], small_dp.at[d], peer) for peer in rings]
        line_u = to_lines("u", ring_u)
        line_d = to_lines("d", ring_d)
        line_rest("u")
        line_rest("d")
        ring_x = [second_ring("x_a", ring_x[0]), second_ring("x_b", ring_x[1])]
        ring_s = [second_ring("s_a", ring_s[0]), second_ring("s_b", ring_s[1])]
        line_sum("u")
        line_sum("d")
        for copy in small_copies:
            copy.wait()
        total = small_dp[0]
        for j in range(1, n_dp):
            total += small_dp[j]
        small_row[r] = total
        small_copies = [push(small_row.at[r], small_row.at[r], peer) for peer in lines]
        line_x = to_lines("x_a", ring_x[0]) + to_lines("x_b", ring_x[1])
        line_s = to_lines("s_a", ring_s[0]) + to_lines("s_b", ring_s[1])
        for name in line_x + line_s:
            line_rest(name)
        for name in line_x + line_s:
            line_sum(name)
    for i in range(sents):
        wait_memory(i)
    if spread:
        sum_lines(2, line_u)
        sum_lines(3, line_d)
        sum_lines(1, line_x)
        for copy in small_copies:
            copy.wait()
        total = small_row[0]
        for j in range(1, n_row):
            total += small_row[j]
        small[...] = total
        sum_lines(0, line_s)
    for copy in late:
        copy.wait()


def layer(n_row, n_dp, scalars, vectors, arrays):
    shape = jax.ShapeDtypeStruct
    encoder, w_self, w_up = arrays["encoder"], arrays["w_self"], arrays["w_up"]
    width, tokens = encoder.shape[1], arrays["tokens"].shape[0] // 2
    hw, units = w_self.shape[1], w_up.shape[1]
    blocks, ublk = vectors["b_up"].shape
    sents = scalars["tgt_len"].shape[0] // 2
    slots, heads = tokens // sents, 2 * hw // HD
    pad, first = -(-3 * hw // 128) * 128, 3 * hw % 128
    rows = width // n_row
    spread = n_dp == 4
    wide, _ = window(rows // 2, rows // 4)
    sizes = {"s": 4 * hw, "x": 4 * hw, "u": units, "d": units}
    outs = {
        "block": ((2, tokens, width), F32, ANY),
        "gtok": ((2, tokens, width), F32, ANY),
        "glad": ((n_row, 2, tokens, width), BF16, ANY),
        "small": ((16, width), F32, VMEM),
        "up_in": (w_up.shape, BF16, ANY),
        "down_in": (arrays["w_down"].shape, BF16, ANY),
    }
    scratch = {}
    for name, size in sizes.items():
        outs["came_" + name] = ((n_row, rows, size), BF16, ANY)
        if spread:
            for piece in (name,) if name in "ud" else (name + "_a", name + "_b"):
                tall_first = piece == "u" or piece[-1] == "a"
                cols_of = size if name in "ud" else size // 2
                landing = rows // 2 if tall_first else 2 * wide
                outs["ring_" + piece] = ((n_row, landing, cols_of), BF16, ANY)
                outs["turn_" + piece] = ((n_row, wide, cols_of), BF16, ANY)
            outs["shard_" + name] = ((wide, size), F32, VMEM)
            scratch["held_" + name] = pltpu.VMEM((n_row, rows, size), BF16)
            scratch["line_" + name] = pltpu.VMEM((n_row - 1, wide, size), BF16)
            scratch["far_" + name] = pltpu.VMEM((wide, size), BF16)
        else:
            outs["held_" + name] = ((n_row, rows, size), BF16, VMEM)
    tall, low = pltpu.VMEM((width, tokens), F32), pltpu.VMEM((width, tokens), BF16)
    flat = pltpu.VMEM((tokens, width), BF16)
    scratch["ws"] = scratch["wc"] = pltpu.VMEM((2,) + w_self.shape, BF16)
    scratch["os"] = scratch["oc"] = pltpu.VMEM((2, hw, width), BF16)
    scratch["wu_buf"] = pltpu.VMEM((3, width, ublk), BF16)
    scratch["wd_buf"] = pltpu.VMEM((3, ublk, width), BF16)
    scratch["act_buf"] = scratch["dh_buf"] = pltpu.VMEM((2, ublk, slots), BF16)
    scratch["out_u"] = scratch["out_d"] = pltpu.VMEM((n_row, rows, units), BF16)
    scratch["out_s"] = scratch["out_x"] = pltpu.VMEM((n_row, rows, 4 * hw), BF16)
    scratch["abuf"] = pltpu.VMEM((n_row, rows, max(sizes.values())), BF16)
    scratch["load_sem"] = pltpu.SemaphoreType.DMA((n_row,))
    scratch["tok_in"] = scratch["cot_in"] = flat
    scratch["enc"] = pltpu.VMEM((n_row, tokens, width), BF16)
    scratch["tout"] = pltpu.VMEM((tokens, width), F32)
    for name in ("mid_t", "late_t", "acc_a", "acc_b"):
        scratch[name] = tall
    for name in ("tok_t", "x1", "x2", "x3", "ct", "mem_t", "e_low"):
        scratch[name] = low
    for name in ("q1", "k1", "v1", "q2", "k2", "v2", "eh"):
        scratch[name] = pltpu.VMEM((2 * hw, tokens), BF16)
    for name in ("attn1", "attn2"):
        scratch[name] = pltpu.VMEM((2, first + hw, tokens), BF16)
    for name in ("prob1", "prob2"):
        scratch[name] = pltpu.VMEM((heads * sents, slots, slots), BF16)
    scratch["grads"] = pltpu.VMEM((2, pad, tokens), BF16)
    for name in ("sum_a", "sum_b", "sum_c", "vec", "cols"):
        scratch[name] = pltpu.VMEM((width, 128), F32)
    scratch["colm"] = pltpu.VMEM((128, width), F32)
    scratch["bm"] = pltpu.VMEM((2, 16, width), F32)
    scratch["bvec"] = pltpu.VMEM((2, -(-hw // 128) * 128, 128), F32)
    scratch["bcols"] = pltpu.VMEM((2, -(-hw // 128) * 128, 8), F32)
    scratch["ubias"] = pltpu.VMEM((2, ublk, 128), F32)
    scratch["bups"] = pltpu.VMEM((2, ublk, 8), F32)
    if spread:
        scratch["small_dp"] = pltpu.VMEM((n_dp, 16, width), F32)
        scratch["small_row"] = pltpu.VMEM((n_row, 16, width), F32)
    dma = pltpu.SemaphoreType.DMA
    scratch["small_in"] = pltpu.VMEM((2, 16, width), F32)
    scratch["small_mp"] = pltpu.VMEM((16, width), F32)
    scratch["via"] = pltpu.VMEM((sents, slots, width), BF16)
    scratch["near"] = pltpu.VMEM((slots, width), BF16)
    scratch["near_sem"] = dma
    scratch["enc_s"] = scratch["enc_r"] = dma((sents, n_row - 1))
    scratch["via_s"] = scratch["via_r"] = dma((sents,))
    scratch["mem_s"] = scratch["mem_r"] = dma((sents, n_row))
    scratch["link_s"] = scratch["link_r"] = dma((6, n_row))
    scratch["local_sem"] = dma((16,))
    scratch["send_sem"] = scratch["recv_sem"] = dma((80,))
    scratch["fetch_sem"] = dma((2, 3))
    scratch["push_sem"] = scratch["land_sem"] = dma((2, blocks))
    names = list(scalars) + list(vectors) + list(arrays) + list(outs) + list(scratch)
    smem = pl.BlockSpec(memory_space=pltpu.SMEM)
    results = pl.pallas_call(
        functools.partial(layer_kernel, n_row, n_dp, names),
        out_shape=tuple(shape(s, t) for s, t, _ in outs.values()),
        in_specs=[smem] * len(scalars) + [VMEM] * len(vectors) + [ANY] * len(arrays),
        out_specs=tuple(spec for _, _, spec in outs.values()),
        scratch_shapes=list(scratch.values()),
        compiler_params=pltpu.CompilerParams(
            collective_id=0, has_side_effects=True, vmem_limit_bytes=63 << 20
        ),
    )(*scalars.values(), *vectors.values(), *arrays.values())
    return dict(zip(outs, results))


def per_device(
    tokens, encoder, layer_pick, piece_heads, piece_ffn, tgt_len, src_len, norm_gain, norm_shift,
    out_bias, w_self, o_self, b_self, w_cross, o_cross, b_cross, w_up, b_up, w_down, cotangent,
):
    n_row, n_dp = lax.axis_size("row"), lax.axis_size("dp")
    r, d, c = place()
    width = tokens.shape[1]
    units, hw = w_up.shape[1], w_self.shape[2]
    ublk = 256
    out = layer(
        n_row, n_dp,
        dict(
            layer_pick=layer_pick, piece_heads=piece_heads, piece_ffn=piece_ffn,
            tgt_len=tgt_len, src_len=src_len,
        ),
        dict(
            norm_gain=norm_gain, norm_shift=norm_shift, out_bias=out_bias,
            b_self=b_self, b_cross=b_cross, b_up=b_up.reshape(-1, ublk),
        ),
        dict(
            tokens=tokens, cotangent=cotangent, encoder=encoder.reshape(-1, width),
            w_self=jnp.swapaxes(w_self, 1, 2), o_self=o_self,
            w_cross=jnp.swapaxes(w_cross, 1, 2), o_cross=o_cross, w_up=w_up, w_down=w_down,
        ),
    )
    share = width // n_row // n_dp
    small = out["small"]
    if n_dp == 4:
        shards = [out["shard_" + name] for name in "sxud"]
    else:
        shards = [
            lax.psum_scatter(
                out["held_" + name].astype(F32).reshape(width, -1),
                ("row", "dp"), scatter_dimension=0, tiled=True,
            )
            for name in "sxud"
        ]
        small = lax.psum(small, ("row", "dp"))

    (
        block, gtok, grad_encoder, gain, shift, bias, w_s, o_s, b_s, w_x, o_x, b_x, w_u, b_u, w_d
    ) = outputs(
        layer_pick, out["block"].reshape(-1, width), out["gtok"].reshape(-1, width),
        out["glad"].reshape(-1, width), small, shards, share, hw, units, ublk,
    )
    return (
        block, gtok, grad_encoder.reshape(1, -1, width), gain, shift, bias,
        w_s, o_s.T, b_s, w_x, o_x.T, b_x, w_u, b_u.reshape(units), w_d.T,
    )


def outputs_kernel(
    share, hw, layer_pick, block_in, gtok_in, memory, small, shard_s, shard_x, shard_u, shard_d,
    block, gtok, encoder, gain, shift, bias, w_s, o_s, b_s, w_x, o_x, b_x, w_u, b_u, w_d,
):
    r, d, c = place()
    n_row, n_dp = layer_pick.shape[1], lax.axis_size("dp")
    width = memory.shape[1]
    step = pl.program_id(0)
    block[...] = block_in[...]
    gtok[...] = gtok_in[...]
    piece = lax.div(step * layer_pick.shape[0], pl.num_programs(0))
    pick = [jnp.full((1, width), layer_pick[piece, i].astype(F32), F32) for i in range(n_row)]
    mine = jnp.full((1, width), layer_pick[piece, r].astype(F32), F32)
    encoder[...] = mine / functools.reduce(jnp.add, pick) * memory[...].astype(F32)

    @pl.when(step == 0)
    def _():
        def own_rows(ref):
            if ref.shape[0] == share:
                return ref[...]
            across = lax.rem(d, 2)
            _, start_of = window(2 * share, share)
            return ref[pl.ds(pl.multiple_of(share * across - start_of(across), 8), share), :]

        def cut(values, i):
            if i:
                values = pltpu.roll(values, values.shape[1] - i * hw, 1)
            return values[:, :hw]

        values = own_rows(shard_s)
        for i in range(3):
            w_s[i] = cut(values, i)
        o_s[...] = cut(values, 3)
        values = own_rows(shard_x)
        for i in range(3):
            w_x[i] = cut(values, (2, 0, 1)[i])
        o_x[...] = cut(values, 3)
        w_u[...] = own_rows(shard_u)
        w_d[...] = own_rows(shard_d)
        at = (r * n_dp + d) * share
        norms = pltpu.roll(small[0:16, :], lax.rem(width - at, width), 1)
        gain[...] = norms[0:3, :share]
        shift[...] = norms[3:6, :share]
        bias[...] = norms[6:9, :share]
        b_s[...] = small[10:12, :hw]
        b_x[...] = small[12:14, :hw]
        aside = -(-hw // 128) * 128
        b_u[...] = small[10 : 10 + b_u.shape[0], aside : aside + b_u.shape[1]]


def outputs(layer_pick, block, gtok, memory, small, shards, share, hw, units, ublk):
    shape = jax.ShapeDtypeStruct
    steps, width = 4, memory.shape[1]
    cut = lambda v: pl.BlockSpec((v.shape[0] // steps, width), lambda i: (i, 0))
    sizes = [(3, share)] * 3 + [(3, share, hw), (share, hw), (2, hw)] * 2
    sizes += [(share, units), (units // ublk, ublk), (share, units)]
    tall = [block, gtok, memory]
    return pl.pallas_call(
        functools.partial(outputs_kernel, share, hw),
        grid=(steps,),
        out_shape=tuple(shape(v.shape, F32) for v in tall) + tuple(shape(v, F32) for v in sizes),
        in_specs=[pl.BlockSpec(memory_space=pltpu.SMEM)] + [cut(v) for v in tall] + [VMEM] * 5,
        out_specs=tuple(cut(v) for v in tall) + (VMEM,) * len(sizes),
        compiler_params=pltpu.CompilerParams(vmem_limit_bytes=62 << 20),
    )(layer_pick, block, gtok, memory, small, *shards)


def solution(mesh):
    return jax.shard_map(
        per_device,
        mesh=mesh,
        in_specs=(
            P(("row", "dp"), None),
            P("row", "dp", None),
            P(),
            P(),
            P(),
            P(("row", "dp")),
            P(("row", "dp")),
            P(),
            P(),
            P(),
            P(None, None, "mp"),
            P("mp", None),
            P(None, "mp"),
            P(None, None, "mp"),
            P("mp", None),
            P(None, "mp"),
            P(None, "mp"),
            P("mp"),
            P("mp", None),
            P(("row", "dp"), None),
        ),
        out_specs=(
            P(("row", "dp"), None),
            P(("row", "dp"), None),
            P("row", "dp", None),
            P(None, ("row", "dp")),
            P(None, ("row", "dp")),
            P(None, ("row", "dp")),
            P(None, ("row", "dp"), "mp"),
            P("mp", ("row", "dp")),
            P(None, "mp"),
            P(None, ("row", "dp"), "mp"),
            P("mp", ("row", "dp")),
            P(None, "mp"),
            P(("row", "dp"), "mp"),
            P("mp"),
            P("mp", ("row", "dp")),
        ),
        check_vma=False,
    )
```
